128 devices in a mesh: rep: 4 (over z_lo, core), fsdp: 32 (over x, z_hi, y).
Axes of the slice: x: 4, y: 4, z: 4 (z_hi: 2, z_lo: 2; z = z_hi * 2 + z_lo), core: 2. Of those that a mesh axis runs over, the one named last changes fastest.
Arguments:
- tokens: bfloat16 [65536, 768], P(('rep', 'fsdp')), may hold values from -6 to 6
- image_lengths: int32 [128, 6], P(('rep', 'fsdp')), may hold values from 1 to 256, 512 in all within a row
- pad_counts: int32 [128], P(('rep', 'fsdp')), may hold values from 0 to 127
- out_grad: bfloat16 [65536, 768], P(('rep', 'fsdp')), may hold values from -6 to 6
- first_gain: bfloat16 [768], P('fsdp'), may hold values from 0.25 to 1.75
- first_shift: bfloat16 [768], P('fsdp'), may hold values from -2 to 2
- input_weight: bfloat16 [768, 2304], P('fsdp'), may hold values from -0.21875 to 0.21875
- query_bias: bfloat16 [768], P('fsdp'), may hold values from -2 to 2
- value_bias: bfloat16 [768], P('fsdp'), may hold values from -2 to 2
- output_weight: bfloat16 [768, 768], P('fsdp'), may hold values from -2 to 2
- output_bias: bfloat16 [768], P('fsdp'), may hold values from -2 to 2
- second_gain: bfloat16 [768], P('fsdp'), may hold values from 0.25 to 1.75
- second_shift: bfloat16 [768], P('fsdp'), may hold values from -2 to 2
- up_weight: bfloat16 [768, 3072], P('fsdp'), may hold values from -0.21875 to 0.21875
- up_bias: bfloat16 [3072], P('fsdp'), may hold values from -2 to 2
- down_weight: bfloat16 [3072, 768], P('fsdp'), may hold values from -0.109375 to 0.109375
- down_bias: bfloat16 [768], P('fsdp'), may hold values from -2 to 2
Outputs:
- layer_out: bfloat16 [65536, 768], P(('rep', 'fsdp'))
- input_grad: float32 [65536, 768], P(('rep', 'fsdp'))
- first_gain_gradient: float32 [768], P('fsdp')
- first_shift_gradient: float32 [768], P('fsdp')
- input_weight_gradient: float32 [768, 2304], P('fsdp')
- query_bias_gradient: float32 [768], P('fsdp')
- value_bias_gradient: float32 [768], P('fsdp')
- output_weight_gradient: float32 [768, 768], P('fsdp')
- output_bias_gradient: float32 [768], P('fsdp')
- second_gain_gradient: float32 [768], P('fsdp')
- second_shift_gradient: float32 [768], P('fsdp')
- up_weight_gradient: float32 [768, 3072], P('fsdp')
- up_bias_gradient: float32 [3072], P('fsdp')
- down_weight_gradient: float32 [3072, 768], P('fsdp')
- down_bias_gradient: float32 [768], P('fsdp')
The draws below stay inside these ranges and needn't reach their ends.
Inputs may be any that keep to these rules, and one draw needn't show every extreme that they name: `image_lengths`: each row sums to 512, and the largest image of each row has 256 patches.
All inputs are finite; a program needn't handle non-finite values.
Results may differ from the reference program's by a relative error of at most 0.025.
Values may be sent and summed in bfloat16 or wider, within the bound.
A program may use at most 128 MiB of HBM per device.

```python
import math
import jax
import jax.numpy as jnp
import numpy as np
from jax import lax

D = 768
HEADS = 12
HEAD = 64
FF = 3072
TOK_DEV = 512
IMGS = 6
SEQS = 128
TOKENS = 65536


def set_ends(values, rng, low, largest):
    index_at = [jax.random.randint(jax.random.fold_in(rng, axis), (), 0, length) for axis, length in enumerate(values.shape)]
    main_axis = values.shape.index(max(values.shape))
    beside = index_at[:main_axis] + [(index_at[main_axis] + 1) % values.shape[main_axis]] + index_at[main_axis + 1:]
    return values.at[tuple(index_at)].set(low).at[tuple(beside)].set(largest)


def steps_of(stream_key, shape, cuts, least, largest):
    def one(axis_at, parts):
        heights = jax.random.uniform(jax.random.fold_in(jax.random.fold_in(stream_key, 6), axis_at), (parts,), jnp.float32, least / len(cuts), largest / len(cuts))
        return jnp.repeat(jnp.exp(heights), shape[axis_at] // parts).reshape((-1,) + (1,) * (len(shape) - axis_at - 1))

    loudness = one(*cuts[0])
    for cut in cuts[1:]:
        loudness = loudness * one(*cut)
    return loudness


def split_up(count, total, most, lean):
    portions = [(1 << 20) // math.isqrt(grade ** lean) + 1 for grade in range(2, count + 1)]
    surplus, holding = total - most - (count - 1), [1] * (count - 1)
    while surplus > 0:
        free = [i for i in range(count - 1) if holding[i] < most]
        mass, remaining = sum([portions[i] for i in free]), surplus
        for i in free:
            addition = min(most - holding[i], max(1, remaining * portions[i] // mass), surplus)
            holding[i] = holding[i] + addition
            surplus = surplus - addition
    return np.array([most] + holding)


def uneven(key, amount, total, most, skew):
    if amount == 2:
        one = jax.random.randint(key, (), max(1, total - most), min(most, total - 1) + 1)
        return jnp.stack([one, total - one])
    tallies = jnp.asarray(split_up(amount, total, most, skew), jnp.int32)
    pairs = (amount - 1) // 2
    giver, receiver = tallies[1:1 + 2 * pairs:2], tallies[2:2 + 2 * pairs:2]
    slack = jnp.minimum(giver - 1, most - receiver)
    moved = jax.random.randint(jax.random.fold_in(key, 1), (pairs,), 0, 1 << 20) % (slack + 1)
    tallies = tallies.at[1:1 + 2 * pairs:2].set(giver - moved).at[2:2 + 2 * pairs:2].set(receiver + moved)
    return tallies[jax.random.permutation(jax.random.fold_in(key, 2), amount)]


def noise(key, dims, scale, most, split=(), kind=jnp.bfloat16):
    level = steps_of(key, dims, split, -0.22, 0.18) if split else 1.0
    result = jax.random.normal(key, dims, jnp.float32) * scale * level
    return jnp.minimum(jnp.maximum(result, -most), most).astype(kind)


def setup_inputs(seed: int = 0) -> dict:
    seeds = jax.random.split(jax.random.key(seed), 18)
    tokens = noise(seeds[0], (TOKENS, D), 1.0, 6.0, ((0, 128),))
    image_lengths = jax.vmap(lambda own: uneven(own, IMGS, TOK_DEV, TOK_DEV // 2, 0))(jax.random.split(seeds[1], SEQS)).reshape((SEQS, IMGS)).astype(jnp.int32)
    pad_counts = set_ends(jax.random.randint(seeds[2], (SEQS,), 0, TOK_DEV // 4), jax.random.fold_in(seeds[2], 1), 0, (TOK_DEV // 4) - 1).astype(jnp.int32)
    out_grad = noise(seeds[3], (TOKENS, D), 1.0, 6.0, ((0, 128),))
    first_gain = jnp.clip(1.0 + 0.15 * jax.random.normal(seeds[4], (D,), jnp.float32), 0.25, 1.75).astype(jnp.bfloat16)
    first_shift = noise(seeds[5], (D,), 0.3, 2.0, ((0, 32),))
    input_weight = noise(seeds[6], (D, 3 * D), D ** -0.5, 0.21875, ((0, 32),))
    query_bias = noise(seeds[7], (D,), 0.3, 2.0, ((0, 32),))
    value_bias = noise(seeds[8], (D,), 0.3, 2.0, ((0, 32),))
    output_weight = noise(seeds[9], (D, D), (D * 6 // TOK_DEV) ** -0.5, 2.0, ((0, 32),))
    output_bias = noise(seeds[10], (D,), 0.3, 2.0, ((0, 32),))
    second_gain = jnp.clip(1.0 + 0.15 * jax.random.normal(seeds[11], (D,), jnp.float32), 0.25, 1.75).astype(jnp.bfloat16)
    second_shift = noise(seeds[12], (D,), 0.3, 2.0, ((0, 32),))
    up_weight = noise(seeds[13], (D, FF), D ** -0.5, 0.21875, ((0, 32),))
    up_bias = noise(seeds[14], (FF,), 0.3, 2.0, ((0, 32),))
    down_weight = noise(seeds[15], (FF, D), FF ** -0.5, 0.109375, ((0, 32),))
    down_bias = noise(seeds[16], (D,), 0.3, 2.0, ((0, 32),))
    return {"tokens": tokens, "image_lengths": image_lengths, "pad_counts": pad_counts, "out_grad": out_grad, "first_gain": first_gain, "first_shift": first_shift, "input_weight": input_weight, "query_bias": query_bias, "value_bias": value_bias, "output_weight": output_weight, "output_bias": output_bias, "second_gain": second_gain, "second_shift": second_shift, "up_weight": up_weight, "up_bias": up_bias, "down_weight": down_weight, "down_bias": down_bias}


@jax.custom_vjp
def low(v):
    return lax.optimization_barrier(v.astype(jnp.bfloat16)).astype(jnp.float32)

@jax.custom_vjp
def low_back(v):
    return v

def low_keep(v):
    return (low(v), None)

def low_pass(kept, grad):
    return (grad,)

def back_keep(v):
    return (v, None)

def back_low(kept, grad):
    return (low(grad),)
low.defvjp(low_keep, low_pass)
low_back.defvjp(back_keep, back_low)
EPSILON = 1e-06
HIGHEST = lax.Precision.HIGHEST

def product(left, right):
    return jnp.dot(left, right, precision=HIGHEST)

def layer_norm(values, gain, shift):
    average = lax.optimization_barrier(jnp.mean(values, axis=1, keepdims=True))
    centred = values - average
    spread = lax.optimization_barrier(jnp.mean(centred * centred, axis=1, keepdims=True))
    return centred * lax.rsqrt(spread + EPSILON) * gain + shift

def sequence_mask(lengths_row, padding, length):
    positions = jnp.arange(length, dtype=jnp.int32)
    starts = (jnp.cumsum(lengths_row) - lengths_row).astype(jnp.int32)
    segment = lax.optimization_barrier(jnp.sum((positions[:, None] >= starts[None, :]).astype(jnp.int32), axis=1))
    valid = positions < (length - padding).astype(jnp.int32)
    same = (segment[:, None] == segment[None, :]) & valid[:, None] & valid[None, :]
    return same | (positions[:, None] == positions[None, :])

def attend_sequence(packed):
    joint_rows, lengths_row, padding = packed
    length = joint_rows.shape[0]
    allowed = sequence_mask(lengths_row, padding, length)
    queries = joint_rows[:, :D].reshape(length, HEADS, HEAD)
    keys = joint_rows[:, D:2 * D].reshape(length, HEADS, HEAD)
    values = joint_rows[:, 2 * D:].reshape(length, HEADS, HEAD)
    scores = jnp.einsum('qhd,khd->hqk', queries, keys, precision=HIGHEST) * HEAD ** (-0.5)
    scores = jnp.where(allowed[None], low_back(scores), -1e+30)
    weights = jax.nn.softmax(scores, axis=-1)
    mixed = jnp.einsum('hqk,khd->qhd', low(weights), values, precision=HIGHEST)
    return mixed.reshape(length, D)

def reference(tokens, image_lengths, pad_counts, out_grad, first_gain, first_shift, input_weight, query_bias, value_bias, output_weight, output_bias, second_gain, second_shift, up_weight, up_bias, down_weight, down_bias):

    def forward(inputs, gain_one, shift_one, joint_weight, bias_query, bias_value, proj_weight, proj_bias, gain_two, shift_two, weight_up, bias_up, weight_down, bias_down):
        hidden_one = low(layer_norm(inputs, gain_one, shift_one))
        joint_bias = jnp.concatenate([bias_query, jnp.zeros_like(bias_query), bias_value])
        joint = low(low_back(product(hidden_one, joint_weight) + joint_bias))
        mixed = lax.map(jax.checkpoint(attend_sequence), (joint.reshape(SEQS, TOK_DEV, 3 * D), image_lengths, pad_counts))
        attended = low(low_back(mixed.reshape(SEQS * TOK_DEV, D)))
        residual = inputs + low_back(product(attended, proj_weight) + proj_bias)
        hidden_two = low(layer_norm(residual, gain_two, shift_two))
        pre_act = low_back(product(hidden_two, weight_up) + bias_up)
        activated = low(jax.nn.gelu(pre_act))
        return residual + low_back(product(activated, weight_down) + bias_down)
    floats = jnp.float32
    layer_value, backward = jax.vjp(forward, tokens.astype(floats), first_gain.astype(floats), first_shift.astype(floats), input_weight.astype(floats), query_bias.astype(floats), value_bias.astype(floats), output_weight.astype(floats), output_bias.astype(floats), second_gain.astype(floats), second_shift.astype(floats), up_weight.astype(floats), up_bias.astype(floats), down_weight.astype(floats), down_bias.astype(floats))
    grad_in, grad_gain_one, grad_shift_one, grad_joint, grad_query, grad_value, grad_proj, grad_proj_bias, grad_gain_two, grad_shift_two, grad_up, grad_up_bias, grad_down, grad_down_bias = backward(out_grad.astype(floats))
    return (layer_value.astype(jnp.bfloat16), grad_in, grad_gain_one, grad_shift_one, grad_joint, grad_query, grad_value, grad_proj, grad_proj_bias, grad_gain_two, grad_shift_two, grad_up, grad_up_bias, grad_down, grad_down_bias)
```

```python
import functools

import jax
import jax.numpy as jnp
from jax import lax
from jax.experimental import pallas as pl
from jax.experimental.pallas import tpu as pltpu
from jax.sharding import PartitionSpec as P

MESH = pl.DeviceIdType.MESH
BF = jnp.bfloat16
F32 = jnp.float32
EPSILON = 1e-06
ROWS, D, FF, HEADS, HEAD = 512, 768, 3072, 12, 64
TILE = 384
SMALL = 128
LOW = -1e30


def nn(left, right):
    return jnp.dot(left, right, preferred_element_type=F32)


def nt(left, right):
    return lax.dot_general(left, right, (((1,), (1,)), ((), ())), preferred_element_type=F32)


def tn(left, right):
    return lax.dot_general(left, right, (((0,), (0,)), ((), ())), preferred_element_type=F32)


class Where:
    def __init__(self):
        self.r = lax.axis_index("rep")
        self.f = lax.axis_index("fsdp")
        self.zl, self.core = self.r // 2, self.r % 2
        self.x, self.zh, self.y = self.f // 8, (self.f // 4) % 2, self.f % 4
        self.zo = 1 - self.zh
        c = self.core
        self.a = self.y + c * (self.x - self.y)
        self.b = self.x + c * (self.y - self.x)
        self.ap, self.a2, self.am = (self.a + 1) % 4, (self.a + 2) % 4, (self.a + 3) % 4
        self.bp, self.b2, self.bm = (self.b + 1) % 4, (self.b + 2) % 4, (self.b + 3) % 4
        self.a_up, self.a_down = self.at(1, 0), self.at(3, 0)
        self.b_up, self.b_down = self.at(0, 1), self.at(0, 3)
        self.twin = {"rep": self.r + 1 - 2 * c, "fsdp": self.f}
        other = (1 - self.zl) * 2 + c
        self.cross = {"rep": other, "fsdp": (self.x * 2 + self.zo) * 4 + self.y}
        self.pair = {"rep": other, "fsdp": self.f}

    def at(self, da, db):
        c = self.core
        y = (self.y + (1 - c) * da + c * db) % 4
        x = (self.x + c * da + (1 - c) * db) % 4
        return {"rep": self.r, "fsdp": (x * 2 + self.zh) * 4 + y}

    def greet(self):
        sem = pltpu.get_barrier_semaphore()
        for device in (self.a_up, self.a_down, self.b_up, self.b_down, self.twin, self.cross, self.pair):
            pl.semaphore_signal(sem, inc=1, device_id=device, device_id_type=MESH)

    def meet(self):
        pl.semaphore_wait(pltpu.get_barrier_semaphore(), 7)


class Copies:
    def remote(self, k, src, dst, device):
        return pltpu.make_async_remote_copy(
            src_ref=src,
            dst_ref=dst,
            send_sem=self.ss.at[k],
            recv_sem=self.rs.at[k],
            device_id=device,
            device_id_type=MESH,
        )

    def send(self, *which):
        for k in which:
            self.remote(k, *self.route(k)).start()

    def take(self, *which):
        for k in which:
            here = self.lands(k)
            self.remote(k, here, here, self.w.twin).wait_recv()

    def end(self):
        for k in range(self.count):
            self.remote(k, *self.route(k)).wait_send()


class Gather(Copies):
    count = 16

    def __init__(self, w, src, raw, ss, rs):
        self.w, self.src, self.raw, self.ss, self.rs = w, src, raw, ss, rs
        self.half = src.shape[1] // 2

    def own(self):
        return self.src.at[:, pl.ds(pl.multiple_of(self.w.core * self.half, 128), self.half)]

    def slot(self, *i):
        return self.raw.at[(self.w.core, *i)]

    def route(self, k):
        w = self.w
        if k < 3:
            return self.own(), self.slot(w.b, w.zh, w.a), (w.cross, w.a_up, w.a_down)[k]
        place, device = {
            3: ((w.b, w.zo, w.a), w.a_up),
            4: ((w.b, w.zo, w.a), w.a_down),
            5: ((w.b, 0, w.am), w.a_up),
            6: ((w.b, 1, w.ap), w.a_down),
            7: ((w.b,), w.b_up),
            8: ((w.b,), w.b_down),
            9: ((w.bm, 0), w.b_up),
            10: ((w.bp, 1), w.b_down),
            11: ((w.b,), w.twin),
            12: ((w.bm,), w.twin),
            13: ((w.bp,), w.twin),
            14: ((w.b2, 0), w.twin),
            15: ((w.b2, 1), w.twin),
        }[k]
        here = self.slot(*place)
        return here, here, device

    def lands(self, k):
        w = self.w
        if k >= 11:
            o = 1 - w.core
            return self.raw.at[
                {
                    11: (o, w.a),
                    12: (o, w.am),
                    13: (o, w.ap),
                    14: (o, w.a2, 0),
                    15: (o, w.a2, 1),
                }[k]
            ]
        return self.slot(
            *{
                0: (w.b, w.zo, w.a),
                1: (w.b, w.zh, w.am),
                2: (w.b, w.zh, w.ap),
                3: (w.b, w.zo, w.am),
                4: (w.b, w.zo, w.ap),
                5: (w.b, 0, w.a2),
                6: (w.b, 1, w.a2),
                7: (w.bm,),
                8: (w.bp,),
                9: (w.b2, 0),
                10: (w.b2, 1),
            }[k]
        )

    def g0(self):
        w = self.w
        self.send(0, 1, 2)
        self.raw[w.core, w.b, w.zh, w.a] = self.own()[...]

    def g1(self):
        self.take(0)
        self.send(3, 4)

    def g2(self):
        self.take(1, 2, 3, 4)
        self.send(5, 6)

    def g3(self):
        self.take(5, 6)
        self.send(7, 8, 11)

    def g4(self):
        self.take(7, 8)
        self.send(9, 10, 12, 13)

    def g5(self):
        self.take(9, 10)
        self.send(14, 15)

    def g6(self):
        self.take(11, 12, 13, 14, 15)


class Reduce(Copies):
    count = 19

    def __init__(self, w, part, columns, bufs, ss, rs):
        self.w, self.part, self.ss, self.rs = w, part, ss, rs
        self.tw, self.r1, self.fx, self.ar, self.af, self.zr, self.pr, self.done = bufs
        self.rows, self.columns = self.tw.shape[-2], pl.ds(columns, self.tw.shape[-1])

    def s(self, h, *i):
        left = (slice(None),) * (4 - 1 - len(i))
        return self.part.at[(h, *i, *left, slice(0, self.rows), self.columns)]

    def route(self, k):
        w, c = self.w, self.w.core
        if k < 4:
            j = (w.a2, w.ap, w.am, w.a)[k]
            return self.s(1 - c, j), self.tw.at[j], w.twin
        if k == 18:
            return self.done.at[c], self.done.at[c], w.twin
        place, device = {
            4: ((w.b2, 0), w.b_up),
            5: ((w.b2, 1), w.b_down),
            6: ((w.bp, 1), w.b_up),
            7: ((w.bm, 0), w.b_down),
            8: ((w.bp, 0), w.b_up),
            9: ((w.bm, 1), w.b_down),
            10: ((w.b, 0, w.a2), w.a_up),
            11: ((w.b, 1, w.a2), w.a_down),
            12: ((w.b, 1, w.ap), w.a_up),
            13: ((w.b, 0, w.am), w.a_down),
            14: ((w.b, 0, w.ap), w.a_up),
            15: ((w.b, 1, w.am), w.a_down),
            16: ((w.b, w.zo, w.a), w.cross),
            17: ((w.b, w.zh, w.a), w.pair),
        }[k]
        return self.s(c, *place), self.lands(k), device

    def lands(self, k):
        w = self.w
        if k < 4:
            return self.tw.at[(w.b2, w.bp, w.bm, w.b)[k]]
        if k == 18:
            return self.done.at[1 - w.core]
        return {
            4: self.r1.at[0],
            5: self.r1.at[1],
            6: self.fx.at[0, 1],
            7: self.fx.at[1, 0],
            8: self.fx.at[0, 0],
            9: self.fx.at[1, 1],
            10: self.ar.at[0],
            11: self.ar.at[1],
            12: self.af.at[0, 1],
            13: self.af.at[1, 0],
            14: self.af.at[0, 0],
            15: self.af.at[1, 1],
            16: self.zr,
            17: self.pr,
        }[k]

    def add(self, place, *terms):
        here = self.s(self.w.core, *place)
        total = here[...].astype(F32)
        for term in terms:
            total = total + term[...].astype(F32)
        here[...] = total.astype(BF)

    def add8(self, b, *terms):
        def one(i, _):
            z, a = i // 4, i % 4
            self.add((b, z, a), *[t.at[z, a] for t in terms])
            return 0

        lax.fori_loop(0, 8, one, 0)

    def add4(self, b, z, term):
        def one(a, _):
            self.add((b, z, a), term.at[a])
            return 0

        lax.fori_loop(0, 4, one, 0)

    def r0(self):
        self.send(0, 1, 2, 3)

    def r1_(self):
        w = self.w
        self.take(0)
        self.add8(w.b2, self.tw.at[w.b2])
        self.send(4, 5)
        self.take(1)
        self.add8(w.bp, self.tw.at[w.bp])
        self.send(6)
        self.take(2)
        self.add8(w.bm, self.tw.at[w.bm])
        self.send(7)

    def r2(self):
        w = self.w
        self.take(3)
        self.add8(w.b, self.tw.at[w.b])
        self.take(4)
        self.add4(w.bp, 0, self.r1.at[0])
        self.send(8)
        self.take(5)
        self.add4(w.bm, 1, self.r1.at[1])
        self.send(9)

    def r3(self):
        self.take(6, 7, 8, 9)
        self.add8(self.w.b, self.fx.at[0], self.fx.at[1])
        self.send(10, 11, 12, 13)

    def r4(self):
        w = self.w
        self.take(10, 11)
        self.add((w.b, 0, w.ap), self.ar.at[0])
        self.send(14)
        self.add((w.b, 1, w.am), self.ar.at[1])
        self.send(15)

    def r5(self):
        w = self.w
        self.take(12, 13, 14, 15)
        for z in range(2):
            self.add((w.b, z, w.a), self.af.at[0, z], self.af.at[1, z])
        self.send(16)

    def r6(self):
        w = self.w
        self.take(16)
        self.add((w.b, w.zh, w.a), self.zr)
        self.send(17)

    def r7(self):
        w = self.w
        self.take(17)
        self.done[w.core] = self.s(w.core, w.b, w.zh, w.a)[...].astype(F32) + self.pr[...].astype(F32)
        self.send(18)

    def r8(self):
        self.take(18)


STAGES = ("r0", "r1_", "r2", "r3", "r4", "r5", "r6", "r7", "r8")


def reduce_scratch(rows, half):
    return [
        pltpu.VMEM((4, 2, 4, rows, half), BF),
        pltpu.VMEM((2, 4, rows, half), BF),
        pltpu.VMEM((2, 2, 4, rows, half), BF),
        pltpu.VMEM((2, rows, half), BF),
        pltpu.VMEM((2, 2, rows, half), BF),
        pltpu.VMEM((rows, half), BF),
        pltpu.VMEM((rows, half), BF),
        pltpu.VMEM((2, rows, half), F32),
    ]


def assemble(raw, out, width):
    rows = raw.shape[4]

    def one(g, _):
        x, z = g // 2, g % 2
        place = pl.ds(pl.multiple_of(g * 4 * rows, 4 * rows), 4 * rows)
        for h in range(2):
            parts = [
                raw[0, x, z, y, :, :width] if h == 0 else raw[1, y, z, x, :, :width] for y in range(4)
            ]
            out[place, h * width : (h + 1) * width] = jnp.concatenate(parts, axis=0)
        return 0

    lax.fori_loop(0, 8, one, 0)


def scatter_rows(value, part, h, first):
    n = value.shape[1]
    for f in range(32):
        x, z, y = f // 8, (f // 4) % 2, f % 4
        part[h, x + h * (y - x), z, y + h * (x - y), :, pl.ds(first, n)] = value[
            24 * f : 24 * f + 24
        ].astype(BF)


def stats(x):
    centred = x - jnp.mean(x, axis=1, keepdims=True)
    inv = lax.rsqrt(jnp.mean(centred * centred, axis=1, keepdims=True) + EPSILON)
    return centred * inv, inv


def norm_backward(grad, normed, inv, gain):
    e = grad * gain
    return inv * (
        e - jnp.mean(e, axis=1, keepdims=True) - normed * jnp.mean(e * normed, axis=1, keepdims=True)
    )


def column_sum(v):
    return jnp.sum(v, axis=0, keepdims=True)


def iota(shape, d):
    return lax.broadcasted_iota(jnp.int32, shape, d)


def by24(n):
    return lax.shift_right_logical(n * 2731, 16)


def select24():
    n = iota((SMALL, D), 1)
    return (n - 24 * by24(n) == iota((SMALL, D), 0)).astype(F32).astype(BF)


def select96():
    n = iota((SMALL, FF), 1)
    return (n - 96 * lax.shift_right_logical(by24(n), 2) == iota((SMALL, FF), 0)).astype(F32).astype(BF)


def row_blocks(count, body):
    step = ROWS // count

    def one(i, c):
        return body(pl.ds(pl.multiple_of(i * step, step), step), c)

    return one


def kernel(
    tokens, lengths, pads, og, in_shard, out_shard, up_shard, down_shard,
    layer_out, input_grad, d_in, d_out, d_up, d_down, d_small,
    raw_in, raw_out, raw_up, raw_down, small, w_in, w_out, w_up, w_down,
    h1, joint, lse, attended, residual, h2, h2t, dh2, vec, ub, gvec, dub,
    gs, gr, rs, rr, *bufs,
):
    w = Where()
    w.greet()
    gq, go, gu, gd = [
        Gather(w, s, r, gs.at[i], gr.at[i])
        for i, (s, r) in enumerate(
            ((in_shard, raw_in), (out_shard, raw_out), (up_shard, raw_up), (down_shard, raw_down))
        )
    ]
    every = (gq, go, gu, gd)
    places = [(raw_up, 0), (raw_up, 768), (raw_down, 0), (raw_out, 0)]
    places += [(raw_in, 0), (raw_in, 384), (raw_in, 768), (small, 0)]
    ru0, ru1, rd, ro, rq0, rq1, rq2, rv = [
        Reduce(w, part, first, bufs[8 * i : 8 * i + 8], rs.at[i], rr.at[i])
        for i, (part, first) in enumerate(places)
    ]

    gvec[...] = jnp.zeros_like(gvec)

    def codes(dim):
        pos = iota((ROWS, 1) if dim == 0 else (1, ROWS), dim)
        seg = jnp.zeros_like(pos)
        start = jnp.int32(0)
        for j in range(lengths.shape[1]):
            seg = seg + (pos >= start).astype(jnp.int32)
            start = start + lengths[0, j]
        return jnp.where(pos < ROWS - pads[0, 0], seg, -1 - pos)

    w.meet()
    for g in every:
        g.g0()
    for g in every:
        g.g1()
    for g in every:
        g.g2()
    for g in every:
        g.g3()
    gq.g4()
    gq.g5()
    go.g4()
    gu.g4()
    gd.g4()
    gq.g6()
    assemble(raw_in, w_in, 1152)

    packed = raw_in[0, :, :, :, 0:16, 1152:1280].reshape(32 * 16, SMALL)
    spread = nn(packed, select24())
    n, row = iota((ROWS, D), 1), iota((ROWS, D), 0)
    spread = jnp.where(by24(n) == lax.shift_right_logical(row, 4), spread, 0.0)
    vec[...] = jnp.sum(spread.reshape(32, 16, D), axis=0)
    packed = raw_in[0, :, :, :, 0:16, 1152:1280].reshape(32, 16, SMALL)[:, 8:9].reshape(32, SMALL)
    spread = nn(packed, select96())
    n, row = iota((32, FF), 1), iota((32, FF), 0)
    ub[...] = column_sum(jnp.where(lax.shift_right_logical(by24(n), 2) == row, spread, 0.0))

    def norm_one(rows, c):
        normed, _ = stats(tokens[rows, :].astype(F32))
        h1[rows, :] = (normed * vec[0:1, :] + vec[1:2, :]).astype(BF)
        return c

    lax.fori_loop(0, 4, row_blocks(4, norm_one), 0)

    for t in range(3):
        bias = (vec[2:3, :], jnp.zeros((1, D), F32), vec[3:4, :])[t]
        for u in range(2):
            columns = slice(t * D + u * TILE, t * D + (u + 1) * TILE)
            joint[:, columns] = (nn(h1[...], w_in[:, columns]) + bias[:, u * TILE : (u + 1) * TILE]).astype(BF)

    same = codes(0)
    lane = iota((1, 128), 1)

    def scores(queries, keys, first):
        mine = (lane >= 64 * first) & (lane < 64 * first + 64)
        picked = jnp.where(mine, queries.astype(F32) * HEAD**-0.5, 0.0).astype(BF)
        return jnp.where(same == codes(1), nt(keys, picked), LOW)

    def pair_columns(p):
        return [pl.ds(pl.multiple_of(t * D + p * 128, 128), 128) for t in range(3)]

    def attend(p, c):
        cq, ck, cv = pair_columns(p)
        queries, keys, values = joint[:, cq], joint[:, ck], joint[:, cv]
        mixed = None
        for first in range(2):
            s = scores(queries, keys, first)
            top = jnp.max(s, axis=0, keepdims=True)
            e = jnp.exp(s - top)
            total = jnp.sum(e, axis=0, keepdims=True)
            weights = (e * (1.0 / total)).astype(BF)
            lse[2 * p + first] = top + jnp.log(total)
            o = tn(weights, values)
            mixed = o if first == 0 else jnp.where(lane < 64, mixed, o)
        attended[:, cq] = mixed.astype(BF)

        @pl.when(p == 0)
        def _():
            go.g5()

        @pl.when(p == 1)
        def _():
            gu.g5()

        @pl.when(p == 3)
        def _():
            gd.g5()

        return c

    lax.fori_loop(0, 6, attend, 0)

    go.g6()
    assemble(raw_out, w_out, TILE)
    for u in range(2):
        columns = slice(u * TILE, (u + 1) * TILE)
        residual[:, columns] = (
            tokens[:, columns].astype(F32) + nn(attended[...], w_out[:, columns]) + vec[4:5, columns]
        )

    def norm_two(rows, c):
        normed, _ = stats(residual[rows, :])
        h2[rows, :] = (normed * vec[5:6, :] + vec[6:7, :]).astype(BF)
        return c

    lax.fori_loop(0, 4, row_blocks(4, norm_two), 0)
    h2t[...] = h2[...].T
    gu.g6()
    assemble(raw_up, w_up, 1536)
    gd.g6()
    assemble(raw_down, w_down, TILE)
    for g in every:
        g.end()

    input_grad[...] = residual[...] + vec[7:8, :]
    dh2[...] = jnp.zeros_like(dh2)

    def tile(i, c):
        t = i // 2 + 4 * (i % 2)
        columns = pl.ds(pl.multiple_of(t * TILE, TILE), TILE)
        u = nn(h2[...], w_up[:, columns]) + ub[:, columns]
        k = 0.7978845608028654
        th = jnp.tanh(k * (u + 0.044715 * (u * u * u)))
        low = 0.5 * (1.0 + th)
        act = (u * low).astype(BF)
        slope = low + (0.5 * k) * u * (1.0 - th * th) * (1.0 + (3 * 0.044715) * (u * u))
        down = w_down[columns, :]
        input_grad[...] += nn(act, down)
        grad_pre = (nt(og[...], down) * slope).astype(BF)
        dub[:, columns] = column_sum(grad_pre.astype(F32))
        scatter_rows(nn(h2t[...], grad_pre), raw_up, t // 4, pl.multiple_of((t % 4) * TILE, 128))
        dh2[...] += nt(grad_pre, w_up[:, columns])
        grad_down = tn(act, og[...]).astype(BF)
        x, z = t // 2, t % 2
        for y in range(4):
            raw_down[0, x, z, y] = grad_down[96 * y : 96 * y + 96, :TILE]
            raw_down[1, y, z, x] = grad_down[96 * y : 96 * y + 96, TILE:]

        @pl.when(i == 3)
        def _():
            ru0.r0()

        @pl.when(i == 4)
        def _():
            ru0.r1_()

        @pl.when(i == 5)
        def _():
            ru0.r2()

        return c

    lax.fori_loop(0, 8, tile, 0)
    rd.r0()
    ru1.r0()
    ru0.r3()
    layer_out[...] = input_grad[...].astype(BF)

    def back_two(rows, c):
        normed, inv = stats(residual[rows, :])
        grad = dh2[rows, :]
        up = og[rows, :].astype(F32)
        total = up + norm_backward(grad, normed, inv, vec[5:6, :])
        residual[rows, :] = total
        rounded = total.astype(BF)
        w_up[rows, 0:D] = rounded
        return (
            c[0] + column_sum(rounded.astype(F32)),
            c[1] + column_sum(grad * normed),
            c[2] + column_sum(grad),
            c[3] + column_sum(up),
        )

    zero = jnp.zeros((1, D), F32)
    sums = lax.fori_loop(0, 4, row_blocks(4, back_two), (zero, zero, zero, zero))
    for j, v in zip((4, 5, 6, 7), sums):
        gvec[j : j + 1, :] = v
    rd.r1_()
    grad_branch = w_up.at[0:ROWS, 0:D]
    grad_attended = w_up.at[0:ROWS, D : 2 * D]
    for u in range(2):
        columns = slice(u * TILE, (u + 1) * TILE)
        scatter_rows(tn(attended[...], grad_branch[:, columns]), raw_out, u, 0)
        grad_attended[:, columns] = nt(grad_branch[...], w_out[columns, :]).astype(BF)
    ro.r0()
    ru1.r1_()
    rd.r2()
    ru0.r4()
    h1t = h2t
    h1t[...] = h1[...].T

    def attend_back(p, c):
        cq, ck, cv = pair_columns(p)
        queries, keys, values = joint[:, cq], joint[:, ck], joint[:, cv]
        gradient = grad_attended[:, cq]
        dq = dk = dv = None
        for first in range(2):
            mine = (lane >= 64 * first) & (lane < 64 * first + 64)
            weights = jnp.exp(scores(queries, keys, first) - lse[2 * p + first])
            picked = jnp.where(mine, gradient, jnp.zeros_like(gradient))
            grad_weights = nt(values, picked)
            along = jnp.sum(grad_weights * weights, axis=0, keepdims=True)
            grad_scores = (weights * (grad_weights - along)).astype(BF)
            v = nn(weights.astype(BF), gradient)
            k = nn(grad_scores, queries) * HEAD**-0.5
            q = tn(grad_scores, keys) * HEAD**-0.5
            if first == 0:
                dq, dk, dv = q, k, v
            else:
                dq, dk, dv = [jnp.where(lane < 64, l, r) for l, r in ((dq, q), (dk, k), (dv, v))]
        dq, dk, dv = dq.astype(BF), dk.astype(BF), dv.astype(BF)
        joint[:, cq], joint[:, ck], joint[:, cv] = dq, dk, dv
        gvec[2:3, cq] = column_sum(dq.astype(F32))
        gvec[3:4, cq] = column_sum(dv.astype(F32))
        both = jnp.concatenate([dq, dk, dv], axis=1)
        scatter_rows(nn(h1t[...], both), raw_in, p % 2, pl.multiple_of((p // 2) * TILE, 128))
        plan = (
            (ro.r1_, ru1.r2, rd.r3, ru0.r5),
            (rq0.r0, ro.r2, ru1.r3, rd.r4, ru0.r6),
            (rq0.r1_, ro.r3, ru1.r4, rd.r5, ru0.r7),
            (rq1.r0, rq0.r2, ro.r4, ru1.r5, rd.r6, ru0.r8),
            (rq1.r1_, rq0.r3, ro.r5, ru1.r6, rd.r7),
            (rq2.r0, rq1.r2, rq0.r4, ro.r6, ru1.r7, rd.r8),
        )
        for i, stages in enumerate(plan):

            @pl.when(p == i)
            def _(stages=stages):
                for stage in stages:
                    stage()

        return c

    lax.fori_loop(0, 6, attend_back, 0)

    rq2.r1_()
    for u in range(2):
        columns = slice(u * TILE, (u + 1) * TILE)
        dh2[:, columns] = nt(joint[...], w_in[columns, :])
    rq2.r2()
    rq1.r3()
    rq0.r5()
    ro.r7()
    ru1.r8()

    def back_one(rows, c):
        normed, inv = stats(tokens[rows, :].astype(F32))
        grad = dh2[rows, :]
        input_grad[rows, :] = residual[rows, :] + norm_backward(grad, normed, inv, vec[0:1, :])
        return c[0] + column_sum(grad * normed), c[1] + column_sum(grad)

    sums = lax.fori_loop(0, 4, row_blocks(4, back_one), (zero, zero))
    for j, v in zip((0, 1), sums):
        gvec[j : j + 1, :] = v

    n, row = iota((32, 16, D), 2), iota((32, 16, D), 0)
    spread = jnp.where(by24(n) == row, jnp.broadcast_to(gvec[...][None], (32, 16, D)), 0.0)
    own = nt(spread.reshape(512, D).astype(BF), select24()).astype(BF).reshape(32, 16, SMALL)
    n, row = iota((32, FF), 1), iota((32, FF), 0)
    spread = jnp.where(lax.shift_right_logical(by24(n), 2) == row, jnp.broadcast_to(dub[...], (32, FF)), 0.0)
    hidden = nt(spread.astype(BF), select96())
    for f in range(32):
        x, z, y = f // 8, (f // 4) % 2, f % 4
        small[0, x, z, y] = own[f]
        small[1, y, z, x] = jnp.broadcast_to(hidden[f : f + 1], (16, SMALL)).astype(BF)
    rv.r0()
    rq2.r3()
    rq1.r4()
    rv.r1_()
    rq0.r6()
    ro.r8()
    rv.r2()
    rq2.r4()
    rq1.r5()
    rv.r3()
    rq0.r7()
    rq2.r5()
    rv.r4()
    rq1.r6()
    rq0.r8()
    rq2.r6()
    rv.r5()
    rq1.r7()
    rv.r6()
    rq2.r7()
    rq1.r8()
    rv.r7()
    rq2.r8()
    rv.r8()

    for h in range(2):
        d_up[:, h * 1536 : h * 1536 + 768] = ru0.done[h]
        d_up[:, h * 1536 + 768 : h * 1536 + 1536] = ru1.done[h]
        d_down[:, h * TILE : (h + 1) * TILE] = rd.done[h]
        d_out[:, h * TILE : (h + 1) * TILE] = ro.done[h]
        d_small[h] = rv.done[h]
        for k, r in enumerate((rq0, rq1, rq2)):
            for j in range(3):
                to = j * D + (2 * k + h) * 128
                d_in[:, to : to + 128] = r.done[h, :, 128 * j : 128 * j + 128]
    for r in (ru0, ru1, rd, ro, rq0, rq1, rq2, rv):
        r.end()


def shards(
    tokens, image_lengths, pad_counts, out_grad, first_gain, first_shift, input_weight, query_bias,
    value_bias, output_weight, output_bias, second_gain, second_shift, up_weight, up_bias, down_weight,
    down_bias,
):
    vectors = jnp.stack(
        [first_gain, first_shift, query_bias, value_bias, output_bias, second_gain, second_shift, down_bias]
    )
    vectors = jnp.pad(vectors, ((0, 0), (0, SMALL - 24)))
    hidden = jnp.pad(up_bias[None], ((0, 15), (0, SMALL - 96)))
    packed = jnp.concatenate([vectors, hidden], axis=0)
    in_shard = jnp.concatenate(
        [input_weight[:, :1152], packed, input_weight[:, 1152:], jnp.zeros((24, SMALL), BF)], axis=1
    )
    vmem = pl.BlockSpec(memory_space=pltpu.VMEM)
    smem = pl.BlockSpec(memory_space=pltpu.SMEM)
    scratch = [
        pltpu.VMEM((2, 4, 2, 4, 24, 1280), BF),
        pltpu.VMEM((2, 4, 2, 4, 24, 384), BF),
        pltpu.VMEM((2, 4, 2, 4, 24, 1536), BF),
        pltpu.VMEM((2, 4, 2, 4, 96, 384), BF),
        pltpu.VMEM((2, 4, 2, 4, 16, SMALL), BF),
        pltpu.VMEM((D, 3 * D), BF),
        pltpu.VMEM((D, D), BF),
        pltpu.VMEM((D, FF), BF),
        pltpu.VMEM((FF, D), BF),
        pltpu.VMEM((ROWS, D), BF),
        pltpu.VMEM((ROWS, 3 * D), BF),
        pltpu.VMEM((HEADS, 1, ROWS), F32),
        pltpu.VMEM((ROWS, D), BF),
        pltpu.VMEM((ROWS, D), F32),
        pltpu.VMEM((ROWS, D), BF),
        pltpu.VMEM((D, ROWS), BF),
        pltpu.VMEM((ROWS, D), F32),
        pltpu.VMEM((16, D), F32),
        pltpu.VMEM((1, FF), F32),
        pltpu.VMEM((16, D), F32),
        pltpu.VMEM((1, FF), F32),
        pltpu.SemaphoreType.DMA((4, 16)),
        pltpu.SemaphoreType.DMA((4, 16)),
        pltpu.SemaphoreType.DMA((8, 19)),
        pltpu.SemaphoreType.DMA((8, 19)),
    ]
    for rows, half in ((24, 768), (24, 768), (96, 384), (24, 384), (24, 384), (24, 384), (24, 384), (16, SMALL)):
        scratch += reduce_scratch(rows, half)
    shape = jax.ShapeDtypeStruct
    layer_out, input_grad, d_in, d_out, d_up, d_down, d_small = pl.pallas_call(
        kernel,
        out_shape=[
            shape((ROWS, D), BF),
            shape((ROWS, D), F32),
            shape((24, 3 * D), F32),
            shape((24, D), F32),
            shape((24, FF), F32),
            shape((96, D), F32),
            shape((2, 16, SMALL), F32),
        ],
        in_specs=[vmem, smem, smem, vmem, vmem, vmem, vmem, vmem],
        out_specs=[vmem] * 7,
        scratch_shapes=scratch,
        compiler_params=pltpu.CompilerParams(
            collective_id=0, has_side_effects=True, vmem_limit_bytes=63 << 20
        ),
        cost_estimate=pl.CostEstimate(flops=25 * 10**9, bytes_accessed=6 * 10**6, transcendentals=8 * 10**6),
    )(
        tokens, image_lengths, pad_counts.reshape(1, 1), out_grad, in_shard, output_weight, up_weight, down_weight
    )
    v = [d_small[0, j, :24] for j in range(8)]
    return (
        layer_out, input_grad, v[0], v[1], d_in, v[2], v[3], d_out, v[4], v[5], v[6], d_up,
        d_small[1, 0, :96], d_down, v[7],
    )


def solution(mesh):
    tall, flat, part = P(("rep", "fsdp"), None), P("fsdp"), P("fsdp", None)
    return jax.shard_map(
        shards,
        mesh=mesh,
        in_specs=(
            tall, tall, P(("rep", "fsdp")), tall, flat, flat, part, flat, flat, part, flat, flat, flat,
            part, flat, part, flat,
        ),
        out_specs=(
            tall, tall, flat, flat, part, flat, flat, part, flat, flat, flat, part, flat, part, flat,
        ),
        check_vma=False,
    )
```

```python
import functools

import jax
import jax.numpy as jnp
from jax import lax
from jax.experimental import pallas as pl
from jax.experimental.pallas import tpu as pltpu
from jax.sharding import PartitionSpec as P

MESH = pl.DeviceIdType.MESH
BF = jnp.bfloat16
F32 = jnp.float32
EPSILON = 1e-06
ROWS, D, FF, HEADS, HEAD = 512, 768, 3072, 12, 64
TILE = 384
SMALL = 128
LOW = -1e30


def nn(left, right):
    return jnp.dot(left, right, preferred_element_type=F32)


def nt(left, right):
    return lax.dot_general(left, right, (((1,), (1,)), ((), ())), preferred_element_type=F32)


def tn(left, right):
    return lax.dot_general(left, right, (((0,), (0,)), ((), ())), preferred_element_type=F32)


class Where:
    def __init__(self):
        self.r = lax.axis_index("rep")
        self.f = lax.axis_index("fsdp")
        self.zl, self.core = self.r // 2, self.r % 2
        self.x, self.zh, self.y = self.f // 8, (self.f // 4) % 2, self.f % 4
        self.zo = 1 - self.zh
        c = self.core
        self.a = self.y + c * (self.x - self.y)
        self.b = self.x + c * (self.y - self.x)
        self.ap, self.a2, self.am = (self.a + 1) % 4, (self.a + 2) % 4, (self.a + 3) % 4
        self.bp, self.b2, self.bm = (self.b + 1) % 4, (self.b + 2) % 4, (self.b + 3) % 4
        self.a_up, self.a_down, self.a_far = self.at(1, 0), self.at(3, 0), self.at(2, 0)
        self.b_up, self.b_down, self.b_far = self.at(0, 1), self.at(0, 3), self.at(0, 2)
        self.z = self.zh * 2 + self.zl
        self.twin = {"rep": self.r + 1 - 2 * c, "fsdp": self.f}
        self.pair = {"rep": (1 - self.zl) * 2 + c, "fsdp": self.f}
        self.cross, self.cross_up, self.cross_down, self.cross_far = [self.over(i) for i in (0, 1, 3, 2)]
        self.third = {"rep": self.r, "fsdp": (self.x * 2 + self.zo) * 4 + self.y}

    def at(self, da, db):
        c = self.core
        y = (self.y + (1 - c) * da + c * db) % 4
        x = (self.x + c * da + (1 - c) * db) % 4
        return {"rep": self.r, "fsdp": (x * 2 + self.zh) * 4 + y}

    def over(self, da):
        c = self.core
        y = (self.y + (1 - c) * da) % 4
        x = (self.x + c * da) % 4
        return {"rep": (1 - self.zl) * 2 + c, "fsdp": (x * 2 + self.zo) * 4 + y}

    def friends(self):
        near = [self.a_up, self.a_down, self.a_far, self.b_up, self.b_down, self.b_far, self.twin]
        return near + [self.pair, self.third, self.cross, self.cross_up, self.cross_down, self.cross_far]

    def greet(self):
        sem = pltpu.get_barrier_semaphore()
        for device in self.friends():
            pl.semaphore_signal(sem, inc=1, device_id=device, device_id_type=MESH)

    def meet(self):
        pl.semaphore_wait(pltpu.get_barrier_semaphore(), len(self.friends()))


class Copies:
    def remote(self, k, src, dst, device):
        return pltpu.make_async_remote_copy(
            src_ref=src,
            dst_ref=dst,
            send_sem=self.ss.at[k],
            recv_sem=self.rs.at[k],
            device_id=device,
            device_id_type=MESH,
        )

    def send(self, *which):
        for k in which:
            self.remote(k, *self.route(k)).start()

    def take(self, *which):
        for k in which:
            here = self.lands(k)
            self.remote(k, here, here, self.w.twin).wait_recv()

    def end(self):
        for k in range(self.count):
            self.remote(k, *self.route(k)).wait_send()


class Gather(Copies):
    count = 16

    def __init__(self, w, src, raw, direct, local, ss, rs):
        self.w, self.src, self.raw, self.direct, self.ss, self.rs = w, src, raw, direct, ss, rs
        self.half = src.shape[1] // 2
        self.local = pltpu.make_async_copy(self.own(), self.slot(w.b, w.zh, w.a), local)

    def own(self):
        return self.src.at[:, pl.ds(pl.multiple_of(self.w.core * self.half, 128), self.half)]

    def slot(self, *i):
        return self.raw.at[(self.w.core, *i)]

    def route(self, k):
        w = self.w
        own = (w.b, w.zh, w.a)
        if k in (0, 1, 3) or (self.direct and k < 7):
            to = (w.a_up, w.a_down, w.a_far, w.cross, w.cross_up, w.cross_down, w.cross_far)[k]
            return self.own(), self.slot(*own), to
        place, device = {
            2: ((w.b, 0, w.am), w.a_up),
            4: ((w.b, w.zo, w.a), w.a_up),
            5: ((w.b, w.zo, w.a), w.a_down),
            6: ((w.b, 1, w.ap), w.a_down),
            7: ((w.b,), w.b_up),
            8: ((w.b,), w.b_down),
            9: ((w.bm, 0), w.b_up),
            10: ((w.bp, 1), w.b_down),
            11: ((w.b,), w.twin),
            12: ((w.bm,), w.twin),
            13: ((w.bp,), w.twin),
            14: ((w.b2, 0), w.twin),
            15: ((w.b2, 1), w.twin),
        }[k]
        here = self.slot(*place)
        return here, here, device

    def lands(self, k):
        w = self.w
        if not self.direct and k in (2, 6):
            return self.slot(w.b, k // 6, w.a2)
        if k < 7:
            return self.slot(w.b, w.zh if k < 3 else w.zo, (w.am, w.ap, w.a2, w.a, w.am, w.ap, w.a2)[k])
        if k >= 11:
            o = 1 - w.core
            return self.raw.at[
                {
                    11: (o, w.a),
                    12: (o, w.am),
                    13: (o, w.ap),
                    14: (o, w.a2, 0),
                    15: (o, w.a2, 1),
                }[k]
            ]
        return self.slot(*{7: (w.bm,), 8: (w.bp,), 9: (w.b2, 0), 10: (w.b2, 1)}[k])

    def g0(self):
        self.send(*((6, 4, 5, 2, 3, 0, 1) if self.direct else (3, 0, 1)))
        self.local.start()

    def g0a(self):
        self.take(3)
        self.send(4, 5)

    def g0b(self):
        self.take(0, 1, 4, 5)
        self.send(2, 6)

    def g1(self):
        self.local.wait()
        self.take(*((0, 1, 2, 3, 4, 5, 6) if self.direct else (2, 6)))
        self.send(7, 8, 11)

    def g2(self):
        self.take(7, 8)
        self.send(9, 10, 12, 13)

    def g3(self):
        self.take(9, 10)
        self.send(14, 15)

    def g4(self):
        self.take(11, 12, 13, 14, 15)


class Reduce(Copies):
    def __init__(self, w, part, columns, direct, bufs, ss, rs):
        self.w, self.part, self.direct, self.ss, self.rs = w, part, direct, ss, rs
        self.tw, self.fx, self.af, self.zb, self.done = bufs
        self.rows, self.columns = self.tw.shape[-2], pl.ds(columns, self.tw.shape[-1])
        self.used = [k for k in range(17) if k not in ((7, 8, 9) if direct else ())]

    def end(self):
        for k in self.used:
            self.remote(k, *self.route(k)).wait_send()

    def s(self, h, *i):
        left = (slice(None),) * (4 - 1 - len(i))
        return self.part.at[(h, *i, *left, slice(0, self.rows), self.columns)]

    def route(self, k):
        w, c = self.w, self.w.core
        every = slice(None)
        if k < 4:
            j = (w.a2, w.ap, w.am, w.a)[k]
            return self.s(1 - c, j), self.tw.at[j], w.twin
        if k == 16:
            return self.done.at[c], self.done.at[c], w.twin
        if k >= 13:
            place, device = {
                13: ((w.b, w.zo, w.a), w.third),
                14: ((w.b, w.zo, w.a), w.cross),
                15: ((w.b, w.zh, w.a), w.pair),
            }[k]
            return self.s(c, *place), self.zb.at[w.z], device
        if self.direct and k < 10:
            place, device = {4: ((w.b2,), w.b_far), 5: ((w.bp,), w.b_up), 6: ((w.bm,), w.b_down)}[k]
        else:
            place, device = {
                4: ((w.b2, 0), w.b_up),
                5: ((w.b2, 1), w.b_down),
                6: ((w.bp, 1), w.b_up),
                7: ((w.bm, 0), w.b_down),
                8: ((w.bp, 0), w.b_up),
                9: ((w.bm, 1), w.b_down),
                10: ((w.b, every, w.a2), w.a_far),
                11: ((w.b, every, w.ap), w.a_up),
                12: ((w.b, every, w.am), w.a_down),
            }[k]
        return self.s(c, *place), self.lands(k), device

    def lands(self, k):
        w = self.w
        if k < 4:
            return self.tw.at[(w.b2, w.bp, w.bm, w.b)[k]]
        if k == 16:
            return self.done.at[1 - w.core]
        if k >= 13:
            return self.zb.at[((w.z + 2) % 4, 3 - w.z, w.zh * 2 + 1 - w.zl)[k - 13]]
        if self.direct and k < 10:
            return self.fx.at[(2, 0, 1)[k - 4]]
        return {
            4: self.fx.at[2, 0],
            5: self.fx.at[2, 1],
            6: self.fx.at[0, 1],
            7: self.fx.at[1, 0],
            8: self.fx.at[0, 0],
            9: self.fx.at[1, 1],
            10: self.af.at[2],
            11: self.af.at[0],
            12: self.af.at[1],
        }[k]

    def add(self, place, *terms):
        here = self.s(self.w.core, *place)
        total = here[...].astype(F32)
        for term in terms:
            total = total + term[...].astype(F32)
        here[...] = total.astype(BF)

    def add8(self, b, *terms):
        def one(i, _):
            z, a = i // 4, i % 4
            self.add((b, z, a), *[t.at[z, a] for t in terms])
            return 0

        lax.fori_loop(0, 8, one, 0)

    def add4(self, b, z, term):
        def one(a, _):
            self.add((b, z, a), term.at[a])
            return 0

        lax.fori_loop(0, 4, one, 0)

    def r0(self):
        self.send(0, 1, 2, 3)

    def r1(self):
        w = self.w
        for k, b in enumerate((w.b2, w.bp, w.bm)):
            self.take(k)
            self.add8(b, self.tw.at[b])
            self.send(*((4 + k,) if self.direct else ((4, 5), (6,), (7,))[k]))

    def r2(self):
        w = self.w
        self.take(3)
        self.add8(w.b, self.tw.at[w.b])
        if not self.direct:
            self.take(4)
            self.add4(w.bp, 0, self.fx.at[2, 0])
            self.send(8)
            self.take(5)
            self.add4(w.bm, 1, self.fx.at[2, 1])
            self.send(9)

    def r3(self):
        if self.direct:
            self.take(4, 5, 6)
            self.add8(self.w.b, self.fx.at[0], self.fx.at[1], self.fx.at[2])
        else:
            self.take(6, 7, 8, 9)
            self.add8(self.w.b, self.fx.at[0], self.fx.at[1])
        self.send(10, 11, 12)

    def r4(self):
        w = self.w
        self.take(10, 11, 12)
        for z in range(2):
            self.add((w.b, z, w.a), self.af.at[0, z], self.af.at[1, z], self.af.at[2, z])
        self.send(13, 14, 15)
        self.zb[w.z] = self.s(w.core, w.b, w.zh, w.a)[...]

    def r5(self):
        self.take(13, 14, 15)
        self.done[self.w.core] = sum(self.zb[i].astype(F32) for i in range(4))
        self.send(16)

    def r6(self):
        self.take(16)


def reduce_scratch(rows, half):
    return [
        pltpu.VMEM((4, 2, 4, rows, half), BF),
        pltpu.VMEM((3, 2, 4, rows, half), BF),
        pltpu.VMEM((3, 2, rows, half), BF),
        pltpu.VMEM((4, rows, half), BF),
        pltpu.VMEM((2, rows, half), F32),
    ]


def assemble(raw, out, width):
    rows = raw.shape[4]

    def one(g, _):
        x, z = g // 2, g % 2
        place = pl.ds(pl.multiple_of(g * 4 * rows, 4 * rows), 4 * rows)
        for h in range(2):
            parts = [
                raw[0, x, z, y, :, :width] if h == 0 else raw[1, y, z, x, :, :width] for y in range(4)
            ]
            out[place, h * width : (h + 1) * width] = jnp.concatenate(parts, axis=0)
        return 0

    lax.fori_loop(0, 8, one, 0)


def scatter_rows(value, part, h, first):
    n = value.shape[1]
    for f in range(32):
        x, z, y = f // 8, (f // 4) % 2, f % 4
        part[h, x + h * (y - x), z, y + h * (x - y), :, pl.ds(first, n)] = value[
            24 * f : 24 * f + 24
        ].astype(BF)


def stats(x):
    centred = x - jnp.mean(x, axis=1, keepdims=True)
    inv = lax.rsqrt(jnp.mean(centred * centred, axis=1, keepdims=True) + EPSILON)
    return centred * inv, inv


def norm_backward(grad, normed, inv, gain):
    e = grad * gain
    return inv * (
        e - jnp.mean(e, axis=1, keepdims=True) - normed * jnp.mean(e * normed, axis=1, keepdims=True)
    )


def column_sum(v):
    return jnp.sum(v, axis=0, keepdims=True)


def iota(shape, d):
    return lax.broadcasted_iota(jnp.int32, shape, d)


def by24(n):
    return lax.shift_right_logical(n * 2731, 16)


def select24():
    n = iota((SMALL, D), 1)
    return (n - 24 * by24(n) == iota((SMALL, D), 0)).astype(F32).astype(BF)


def select96():
    n = iota((SMALL, FF), 1)
    return (n - 96 * lax.shift_right_logical(by24(n), 2) == iota((SMALL, FF), 0)).astype(F32).astype(BF)


def row_blocks(count, body):
    step = ROWS // count

    def one(i, c):
        return body(pl.ds(pl.multiple_of(i * step, step), step), c)

    return one


def kernel(
    tokens_in, lengths, pads, og_in, in_weight, out_weight, up_weight, down_weight,
    v0, v1, v2, v3, v4, v5, v6, v7, v8,
    layer_out, input_grad, d_in, d_out, d_up, d_down, d_small,
    tokens, og, in_pack, vpack, raw_in, raw_out, raw_up, raw_down, small, w_in, w_out, w_up, w_down,
    h1, joint, lse, attended, residual, h2, h2t, dh2, acc, slope, vec, ub, gvec, dub,
    ls, gs, gr, rs, rr, *bufs,
):
    w = Where()
    w.greet()
    loads = [
        pltpu.make_async_copy(src, dst, ls.at[i])
        for i, (src, dst) in enumerate(
            (
                (in_weight.at[:, 0:1152], in_pack.at[:, 0:1152]),
                (in_weight.at[:, 1152:2304], in_pack.at[:, 1280:2432]),
                (tokens_in, tokens),
                (og_in, og),
            )
        )
    ]
    for load in loads:
        load.start()
    gq, go, gu, gd = [
        Gather(w, s, r, i == 0, ls.at[4 + i], gs.at[i], gr.at[i])
        for i, (s, r) in enumerate(
            ((in_pack, raw_in), (out_weight, raw_out), (up_weight, raw_up), (down_weight, raw_down))
        )
    ]
    every = (gq, go, gu, gd)
    places = [(raw_up, 0, False), (raw_up, 768, False), (raw_down, 0, False), (raw_out, 0, False)]
    places += [(raw_in, 0, False), (raw_in, 384, False), (raw_in, 768, True), (small, 0, True)]
    ru0, ru1, rd, ro, rq0, rq1, rq2, rv = [
        Reduce(w, part, first, direct, bufs[5 * i : 5 * i + 5], rs.at[i], rr.at[i])
        for i, (part, first, direct) in enumerate(places)
    ]
    vpack[...] = jnp.zeros_like(vpack)
    for j, v in enumerate((v0, v1, v2, v3, v4, v5, v6, v7)):
        vpack[j : j + 1, 0:24] = v[...].astype(F32)
    vpack[8:9, 0:96] = v8[...].astype(F32)
    in_pack[:, 1152:1280] = vpack[...].astype(BF)
    in_pack[:, 2432:2560] = jnp.zeros((24, SMALL), BF)
    gvec[...] = jnp.zeros_like(gvec)

    def codes(dim):
        pos = iota((ROWS, 1) if dim == 0 else (1, ROWS), dim)
        seg = jnp.zeros_like(pos)
        start = jnp.int32(0)
        for j in range(lengths.shape[1]):
            seg = seg + (pos >= start).astype(jnp.int32)
            start = start + lengths[0, j]
        return jnp.where(pos < ROWS - pads[0, 0], seg, -1 - pos)

    loads[0].wait()
    loads[1].wait()
    w.meet()
    for g in every:
        g.g0()

    loads[2].wait()
    loads[3].wait()

    def norm_one(rows, c):
        residual[rows, :] = stats(tokens[rows, :].astype(F32))[0]
        return c

    lax.fori_loop(0, 4, row_blocks(4, norm_one), 0)
    for g in (go, gu, gd):
        g.g0a()
    gq.g1()
    for g in (go, gu, gd):
        g.g0b()
    go.g1()
    gq.g2()
    gu.g1()
    gd.g1()
    gq.g3()
    gq.g4()
    assemble(raw_in, w_in, 1152)

    packed = raw_in[0, :, :, :, 0:16, 1152:1280].reshape(32 * 16, SMALL)
    spread = nn(packed, select24())
    n, row = iota((ROWS, D), 1), iota((ROWS, D), 0)
    spread = jnp.where(by24(n) == lax.shift_right_logical(row, 4), spread, 0.0)
    vec[...] = jnp.sum(spread.reshape(32, 16, D), axis=0)
    packed = raw_in[0, :, :, :, 0:16, 1152:1280].reshape(32, 16, SMALL)[:, 8:9].reshape(32, SMALL)
    spread = nn(packed, select96())
    n, row = iota((32, FF), 1), iota((32, FF), 0)
    ub[...] = column_sum(jnp.where(lax.shift_right_logical(by24(n), 2) == row, spread, 0.0))

    h1[...] = (residual[...] * vec[0:1, :] + vec[1:2, :]).astype(BF)

    for t in range(3):
        bias = (vec[2:3, :], jnp.zeros((1, D), F32), vec[3:4, :])[t]
        for u in range(2):
            columns = slice(t * D + u * TILE, t * D + (u + 1) * TILE)
            joint[:, columns] = (nn(h1[...], w_in[:, columns]) + bias[:, u * TILE : (u + 1) * TILE]).astype(BF)

    same = codes(0)
    lane = iota((1, 128), 1)

    def scores(queries, keys, first):
        mine = (lane >= 64 * first) & (lane < 64 * first + 64)
        picked = jnp.where(mine, queries.astype(F32) * HEAD**-0.5, 0.0).astype(BF)
        return jnp.where(same == codes(1), nt(keys, picked), LOW)

    def pair_columns(p):
        return [pl.ds(pl.multiple_of(t * D + p * 128, 128), 128) for t in range(3)]

    def attend(p, c):
        cq, ck, cv = pair_columns(p)
        queries, keys, values = joint[:, cq], joint[:, ck], joint[:, cv]
        mixed = None
        for first in range(2):
            s = scores(queries, keys, first)
            top = jnp.max(s, axis=0, keepdims=True)
            e = jnp.exp(s - top)
            total = jnp.sum(e, axis=0, keepdims=True)
            weights = (e * (1.0 / total)).astype(BF)
            lse[2 * p + first] = top + jnp.log(total)
            o = tn(weights, values)
            mixed = o if first == 0 else jnp.where(lane < 64, mixed, o)
        attended[:, cq] = mixed.astype(BF)

        plan = ((go.g2,), (gu.g2,), (go.g3,), (gd.g2,), (gu.g3,), (gd.g3,))
        for i, stages in enumerate(plan):

            @pl.when(p == i)
            def _(stages=stages):
                for stage in stages:
                    stage()

        return c

    lax.fori_loop(0, 6, attend, 0)

    go.g4()
    assemble(raw_out, w_out, TILE)
    for u in range(2):
        columns = slice(u * TILE, (u + 1) * TILE)
        residual[:, columns] = (
            tokens[:, columns].astype(F32) + nn(attended[...], w_out[:, columns]) + vec[4:5, columns]
        )

    def norm_two(rows, c):
        normed, _ = stats(residual[rows, :])
        h2[rows, :] = (normed * vec[5:6, :] + vec[6:7, :]).astype(BF)
        return c

    lax.fori_loop(0, 4, row_blocks(4, norm_two), 0)
    h2t[...] = h2[...].T
    gu.g4()
    assemble(raw_up, w_up, 1536)
    gd.g4()
    assemble(raw_down, w_down, TILE)
    for g in every:
        g.end()

    acc[...] = residual[...] + vec[7:8, :]

    def forth(t, c):
        columns = pl.ds(pl.multiple_of(t * TILE, TILE), TILE)
        u = nn(h2[...], w_up[:, columns]) + ub[:, columns]
        k = 0.7978845608028654
        square = u * u
        th = jnp.tanh(u * (k + (k * 0.044715) * square))
        low = 0.5 * (1.0 + th)
        act = (u * low).astype(BF)
        slope[:, columns] = (
            low + u * (1.0 - th * th) * (0.5 * k + (1.5 * 0.044715 * k) * square)
        ).astype(BF)
        acc[...] += nn(act, w_down[columns, :])
        grad_down = tn(act, og[...]).astype(BF)
        x, z = t // 2, t % 2
        for y in range(4):
            raw_down[0, x, z, y] = grad_down[96 * y : 96 * y + 96, :TILE]
            raw_down[1, y, z, x] = grad_down[96 * y : 96 * y + 96, TILE:]
        return c

    lax.fori_loop(0, 8, forth, 0)
    rd.r0()
    h2[...] = acc[...].astype(BF)
    out_copy = pltpu.make_async_copy(h2, layer_out, ls.at[8])
    out_copy.start()

    dh2[...] = jnp.zeros_like(dh2)

    def back(i, c):
        t = i // 2 + 4 * (i % 2)
        columns = pl.ds(pl.multiple_of(t * TILE, TILE), TILE)
        grad_pre = (nt(og[...], w_down[columns, :]) * slope[:, columns].astype(F32)).astype(BF)
        dub[:, columns] = column_sum(grad_pre.astype(F32))
        scatter_rows(nn(h2t[...], grad_pre), raw_up, t // 4, pl.multiple_of((t % 4) * TILE, 128))
        dh2[...] += nt(grad_pre, w_up[:, columns])
        plan = {1: (rd.r1,), 3: (ru0.r0,), 4: (rd.r2,), 5: (ru0.r1,), 7: (rd.r3,)}
        for j, stages in plan.items():

            @pl.when(i == j)
            def _(stages=stages):
                for stage in stages:
                    stage()

        return c

    lax.fori_loop(0, 8, back, 0)
    ru1.r0()
    ru0.r2()

    def back_two(rows, c):
        normed, inv = stats(residual[rows, :])
        grad = dh2[rows, :]
        up = og[rows, :].astype(F32)
        total = up + norm_backward(grad, normed, inv, vec[5:6, :])
        residual[rows, :] = total
        rounded = total.astype(BF)
        w_up[rows, 0:D] = rounded
        return (
            c[0] + column_sum(rounded.astype(F32)),
            c[1] + column_sum(grad * normed),
            c[2] + column_sum(grad),
            c[3] + column_sum(up),
        )

    zero = jnp.zeros((1, D), F32)
    sums = lax.fori_loop(0, 4, row_blocks(4, back_two), (zero, zero, zero, zero))
    for j, v in zip((4, 5, 6, 7), sums):
        gvec[j : j + 1, :] = v
    ru1.r1()
    grad_branch = w_up.at[0:ROWS, 0:D]
    grad_attended = w_up.at[0:ROWS, D : 2 * D]
    for u in range(2):
        columns = slice(u * TILE, (u + 1) * TILE)
        scatter_rows(tn(attended[...], grad_branch[:, columns]), raw_out, u, 0)
        grad_attended[:, columns] = nt(grad_branch[...], w_out[columns, :]).astype(BF)
    ro.r0()
    rd.r4()
    ru0.r3()
    h1t = h2t
    h1t[...] = h1[...].T

    def attend_back(p, c):
        cq, ck, cv = pair_columns(p)
        queries, keys, values = joint[:, cq], joint[:, ck], joint[:, cv]
        gradient = grad_attended[:, cq]
        dq = dk = dv = None
        for first in range(2):
            mine = (lane >= 64 * first) & (lane < 64 * first + 64)
            weights = jnp.exp(scores(queries, keys, first) - lse[2 * p + first])
            picked = jnp.where(mine, gradient, jnp.zeros_like(gradient))
            grad_weights = nt(values, picked)
            along = jnp.sum(grad_weights * weights, axis=0, keepdims=True)
            grad_scores = (weights * (grad_weights - along)).astype(BF)
            v = nn(weights.astype(BF), gradient)
            k = nn(grad_scores, queries) * HEAD**-0.5
            q = tn(grad_scores, keys) * HEAD**-0.5
            if first == 0:
                dq, dk, dv = q, k, v
            else:
                dq, dk, dv = [jnp.where(lane < 64, l, r) for l, r in ((dq, q), (dk, k), (dv, v))]
        dq, dk, dv = dq.astype(BF), dk.astype(BF), dv.astype(BF)
        joint[:, cq], joint[:, ck], joint[:, cv] = dq, dk, dv
        gvec[2:3, cq] = column_sum(dq.astype(F32))
        gvec[3:4, cq] = column_sum(dv.astype(F32))
        both = jnp.concatenate([dq, dk, dv], axis=1)
        scatter_rows(nn(h1t[...], both), raw_in, p % 2, pl.multiple_of((p // 2) * TILE, 128))
        plan = (
            (ro.r1, ru1.r2),
            (rq0.r0, ru0.r4, rd.r5),
            (ro.r2, rq0.r1, ru1.r3, rd.r6),
            (rq1.r0, ro.r3, rq0.r2, ru0.r5),
            (rq1.r1, ru1.r4, ro.r4, ru0.r6),
            (rq2.r0, rq0.r3, rq1.r2),
        )
        for i, stages in enumerate(plan):

            @pl.when(p == i)
            def _(stages=stages):
                for stage in stages:
                    stage()

        return c

    lax.fori_loop(0, 6, attend_back, 0)

    rq2.r1()
    for u in range(2):
        columns = slice(u * TILE, (u + 1) * TILE)
        dh2[:, columns] = nt(joint[...], w_in[columns, :])
    rq2.r2()
    rq1.r3()
    ru1.r5()
    rq0.r4()
    ro.r5()

    def back_one(rows, c):
        normed, inv = stats(tokens[rows, :].astype(F32))
        grad = dh2[rows, :]
        acc[rows, :] = residual[rows, :] + norm_backward(grad, normed, inv, vec[0:1, :])
        return c[0] + column_sum(grad * normed), c[1] + column_sum(grad)

    sums = lax.fori_loop(0, 4, row_blocks(4, back_one), (zero, zero))
    grad_copy = pltpu.make_async_copy(acc, input_grad, ls.at[9])
    grad_copy.start()
    for j, v in zip((0, 1), sums):
        gvec[j : j + 1, :] = v
    rq2.r3()

    n, row = iota((32, 16, D), 2), iota((32, 16, D), 0)
    spread = jnp.where(by24(n) == row, jnp.broadcast_to(gvec[...][None], (32, 16, D)), 0.0)
    own = nt(spread.reshape(512, D).astype(BF), select24()).astype(BF).reshape(32, 16, SMALL)
    n, row = iota((32, FF), 1), iota((32, FF), 0)
    spread = jnp.where(lax.shift_right_logical(by24(n), 2) == row, jnp.broadcast_to(dub[...], (32, FF)), 0.0)
    hidden = nt(spread.astype(BF), select96())
    for f in range(32):
        x, z, y = f // 8, (f // 4) % 2, f % 4
        small[0, x, z, y] = own[f]
        small[1, y, z, x] = jnp.broadcast_to(hidden[f : f + 1], (16, SMALL)).astype(BF)
    rv.r0()
    rq1.r4()
    rv.r1()
    rq0.r5()
    rv.r2()
    rq2.r4()
    rv.r3()
    rq1.r5()
    ru1.r6()
    ro.r6()
    rq2.r5()
    rv.r4()
    rq0.r6()
    rq1.r6()
    rv.r5()
    rq2.r6()
    rv.r6()

    for h in range(2):
        d_up[:, h * 1536 : h * 1536 + 768] = ru0.done[h]
        d_up[:, h * 1536 + 768 : h * 1536 + 1536] = ru1.done[h]
        d_down[:, h * TILE : (h + 1) * TILE] = rd.done[h]
        d_out[:, h * TILE : (h + 1) * TILE] = ro.done[h]
        d_small[h] = rv.done[h]
        for k, r in enumerate((rq0, rq1, rq2)):
            for j in range(3):
                to = j * D + (2 * k + h) * 128
                d_in[:, to : to + 128] = r.done[h, :, 128 * j : 128 * j + 128]
    for r in (ru0, ru1, rd, ro, rq0, rq1, rq2, rv):
        r.end()
    out_copy.wait()
    grad_copy.wait()


def finish(*refs):
    packed, src, dst, vectors = refs[6], refs[:6], refs[7:13], refs[13:22]
    held, taken, given = refs[22:28], refs[28], refs[29]
    arrive = [pltpu.make_async_copy(s, h, taken.at[i]) for i, (s, h) in enumerate(zip(src, held))]
    leave = [pltpu.make_async_copy(h, d, given.at[i]) for i, (h, d) in enumerate(zip(held, dst))]
    for c in arrive:
        c.start()
    for j in range(8):
        vectors[j][...] = packed[0, j : j + 1, 0:24]
    vectors[8][...] = packed[1, 0:1, 0:96]
    for c, d in zip(arrive, leave):
        c.wait()
        d.start()
    for c in leave:
        c.wait()


def shards(
    tokens, image_lengths, pad_counts, out_grad, first_gain, first_shift, input_weight, query_bias,
    value_bias, output_weight, output_bias, second_gain, second_shift, up_weight, up_bias, down_weight,
    down_bias,
):
    vmem = pl.BlockSpec(memory_space=pltpu.VMEM)
    smem = pl.BlockSpec(memory_space=pltpu.SMEM)
    hbm = pl.BlockSpec(memory_space=pl.ANY)
    scratch = [
        pltpu.VMEM((ROWS, D), BF),
        pltpu.VMEM((ROWS, D), BF),
        pltpu.VMEM((24, 2560), BF),
        pltpu.VMEM((24, SMALL), F32),
        pltpu.VMEM((2, 4, 2, 4, 24, 1280), BF),
        pltpu.VMEM((2, 4, 2, 4, 24, 384), BF),
        pltpu.VMEM((2, 4, 2, 4, 24, 1536), BF),
        pltpu.VMEM((2, 4, 2, 4, 96, 384), BF),
        pltpu.VMEM((2, 4, 2, 4, 16, SMALL), BF),
        pltpu.VMEM((D, 3 * D), BF),
        pltpu.VMEM((D, D), BF),
        pltpu.VMEM((D, FF), BF),
        pltpu.VMEM((FF, D), BF),
        pltpu.VMEM((ROWS, D), BF),
        pltpu.VMEM((ROWS, 3 * D), BF),
        pltpu.VMEM((HEADS, 1, ROWS), F32),
        pltpu.VMEM((ROWS, D), BF),
        pltpu.VMEM((ROWS, D), F32),
        pltpu.VMEM((ROWS, D), BF),
        pltpu.VMEM((D, ROWS), BF),
        pltpu.VMEM((ROWS, D), F32),
        pltpu.VMEM((ROWS, D), F32),
        pltpu.VMEM((ROWS, FF), BF),
        pltpu.VMEM((16, D), F32),
        pltpu.VMEM((1, FF), F32),
        pltpu.VMEM((16, D), F32),
        pltpu.VMEM((1, FF), F32),
        pltpu.SemaphoreType.DMA((10,)),
        pltpu.SemaphoreType.DMA((4, 16)),
        pltpu.SemaphoreType.DMA((4, 16)),
        pltpu.SemaphoreType.DMA((8, 17)),
        pltpu.SemaphoreType.DMA((8, 17)),
    ]
    for rows, half in ((24, 768), (24, 768), (96, 384), (24, 384), (24, 384), (24, 384), (24, 384), (16, SMALL)):
        scratch += reduce_scratch(rows, half)
    shape = jax.ShapeDtypeStruct
    large = [
        shape((ROWS, D), BF),
        shape((ROWS, D), F32),
        shape((24, 3 * D), F32),
        shape((24, D), F32),
        shape((24, FF), F32),
        shape((96, D), F32),
    ]
    vectors = (
        first_gain, first_shift, query_bias, value_bias, output_bias, second_gain, second_shift, down_bias,
        up_bias,
    )
    results = pl.pallas_call(
        kernel,
        out_shape=[*large, shape((2, 16, SMALL), F32)],
        in_specs=[hbm, smem, smem, hbm, hbm, hbm, hbm, hbm, *[vmem] * 9],
        out_specs=[hbm, hbm, *[vmem] * 5],
        scratch_shapes=scratch,
        compiler_params=pltpu.CompilerParams(
            collective_id=0, has_side_effects=True, vmem_limit_bytes=63 << 20
        ),
        cost_estimate=pl.CostEstimate(flops=25 * 10**9, bytes_accessed=6 * 10**6, transcendentals=8 * 10**6),
    )(
        tokens, image_lengths, pad_counts.reshape(1, 1), out_grad, input_weight, output_weight, up_weight,
        down_weight, *[v.reshape(1, -1) for v in vectors],
    )
    done = pl.pallas_call(
        finish,
        out_shape=[*large, *[shape((1, v.shape[0]), F32) for v in vectors]],
        in_specs=[*[hbm] * 6, vmem],
        out_specs=[*[hbm] * 6, *[vmem] * 9],
        scratch_shapes=[
            *[pltpu.VMEM(x.shape, x.dtype) for x in large],
            pltpu.SemaphoreType.DMA((6,)),
            pltpu.SemaphoreType.DMA((6,)),
        ],
    )(*results)
    layer_out, input_grad, d_in, d_out, d_up, d_down = done[:6]
    v = [x.reshape(-1) for x in done[6:]]
    return (
        layer_out, input_grad, v[0], v[1], d_in, v[2], v[3], d_out, v[4], v[5], v[6], d_up, v[8], d_down,
        v[7],
    )


def solution(mesh):
    tall, flat, part = P(("rep", "fsdp"), None), P("fsdp"), P("fsdp", None)
    return jax.shard_map(
        shards,
        mesh=mesh,
        in_specs=(
            tall, tall, P(("rep", "fsdp")), tall, flat, flat, part, flat, flat, part, flat, flat, flat,
            part, flat, part, flat,
        ),
        out_specs=(
            tall, tall, flat, flat, part, flat, flat, part, flat, flat, flat, part, flat, part, flat,
        ),
        check_vma=False,
    )
```

```python
import functools

import jax
import jax.numpy as jnp
from jax import lax
from jax.experimental import pallas as pl
from jax.experimental.pallas import tpu as pltpu
from jax.sharding import PartitionSpec as P

MESH = pl.DeviceIdType.MESH
BF = jnp.bfloat16
F32 = jnp.float32
EPSILON = 1e-06
ROWS, D, FF, HEADS, HEAD = 512, 768, 3072, 12, 64
TILE = 384
SMALL = 128
LOW = -1e30
SLOPE = 0.7978845608028654


def nn(left, right):
    return jnp.dot(left, right, preferred_element_type=F32)


def nt(left, right):
    return lax.dot_general(left, right, (((1,), (1,)), ((), ())), preferred_element_type=F32)


def tn(left, right):
    return lax.dot_general(left, right, (((0,), (0,)), ((), ())), preferred_element_type=F32)


class Where:
    def __init__(self):
        self.r = lax.axis_index("rep")
        self.f = lax.axis_index("fsdp")
        self.zl, self.core = self.r // 2, self.r % 2
        self.x, self.zh, self.y = self.f // 8, (self.f // 4) % 2, self.f % 4
        self.zo = 1 - self.zh
        c = self.core
        self.a = self.y + c * (self.x - self.y)
        self.b = self.x + c * (self.y - self.x)
        self.ap, self.a2, self.am = (self.a + 1) % 4, (self.a + 2) % 4, (self.a + 3) % 4
        self.bp, self.b2, self.bm = (self.b + 1) % 4, (self.b + 2) % 4, (self.b + 3) % 4
        self.a_up, self.a_down, self.a_far = self.at(1, 0), self.at(3, 0), self.at(2, 0)
        self.b_up, self.b_down, self.b_far = self.at(0, 1), self.at(0, 3), self.at(0, 2)
        self.z = self.zh * 2 + self.zl
        self.twin = {"rep": self.r + 1 - 2 * c, "fsdp": self.f}
        self.pair = {"rep": (1 - self.zl) * 2 + c, "fsdp": self.f}
        self.diagonal = {"rep": (1 - self.zl) * 2 + 1 - c, "fsdp": self.f}
        self.cross, self.cross_up, self.cross_down, self.cross_far = [self.over(i) for i in (0, 1, 3, 2)]
        self.third = {"rep": self.r, "fsdp": (self.x * 2 + self.zo) * 4 + self.y}

    def at(self, da, db):
        c = self.core
        y = (self.y + (1 - c) * da + c * db) % 4
        x = (self.x + c * da + (1 - c) * db) % 4
        return {"rep": self.r, "fsdp": (x * 2 + self.zh) * 4 + y}

    def over(self, da):
        c = self.core
        y = (self.y + (1 - c) * da) % 4
        x = (self.x + c * da) % 4
        return {"rep": (1 - self.zl) * 2 + c, "fsdp": (x * 2 + self.zo) * 4 + y}

    def friends(self):
        near = [self.a_up, self.a_down, self.a_far, self.b_up, self.b_down, self.b_far, self.twin]
        return near + [self.pair, self.diagonal, self.third, self.cross, self.cross_up, self.cross_down, self.cross_far]

    def greet(self):
        sem = pltpu.get_barrier_semaphore()
        for device in self.friends():
            pl.semaphore_signal(sem, inc=1, device_id=device, device_id_type=MESH)

    def meet(self):
        pl.semaphore_wait(pltpu.get_barrier_semaphore(), len(self.friends()))


class Copies:
    def remote(self, k, src, dst, device):
        return pltpu.make_async_remote_copy(
            src_ref=src,
            dst_ref=dst,
            send_sem=self.ss.at[k],
            recv_sem=self.rs.at[k],
            device_id=device,
            device_id_type=MESH,
        )

    def send(self, *which):
        for k in which:
            self.remote(k, *self.route(k)).start()

    def take(self, *which):
        for k in which:
            here = self.lands(k)
            self.remote(k, here, here, self.w.twin).wait_recv()

    def end(self):
        for k in range(self.count):
            self.remote(k, *self.route(k)).wait_send()


class Gather(Copies):
    count = 16

    def __init__(self, w, src, raw, direct, local, ss, rs):
        self.w, self.src, self.raw, self.direct, self.ss, self.rs = w, src, raw, direct, ss, rs
        self.half = src.shape[1] // 2
        self.local = pltpu.make_async_copy(self.own(), self.slot(w.b, w.zh, w.a), local)

    def own(self):
        return self.src.at[:, pl.ds(pl.multiple_of(self.w.core * self.half, 128), self.half)]

    def slot(self, *i):
        return self.raw.at[(self.w.core, *i)]

    def route(self, k):
        w = self.w
        own = (w.b, w.zh, w.a)
        if k in (0, 1, 3) or (self.direct and k < 7):
            to = (w.a_up, w.a_down, w.a_far, w.cross, w.cross_up, w.cross_down, w.cross_far)[k]
            return self.own(), self.slot(*own), to
        place, device = {
            2: ((w.b, 0, w.am), w.a_up),
            4: ((w.b, w.zo, w.a), w.a_up),
            5: ((w.b, w.zo, w.a), w.a_down),
            6: ((w.b, 1, w.ap), w.a_down),
            7: ((w.b,), w.b_up),
            8: ((w.b,), w.b_down),
            9: ((w.bm, 0), w.b_up),
            10: ((w.bp, 1), w.b_down),
            11: ((w.b,), w.twin),
            12: ((w.bm,), w.twin),
            13: ((w.bp,), w.twin),
            14: ((w.b2, 0), w.twin),
            15: ((w.b2, 1), w.twin),
        }[k]
        here = self.slot(*place)
        return here, here, device

    def lands(self, k):
        w = self.w
        if not self.direct and k in (2, 6):
            return self.slot(w.b, k // 6, w.a2)
        if k < 7:
            return self.slot(w.b, w.zh if k < 3 else w.zo, (w.am, w.ap, w.a2, w.a, w.am, w.ap, w.a2)[k])
        if k >= 11:
            o = 1 - w.core
            return self.raw.at[
                {
                    11: (o, w.a),
                    12: (o, w.am),
                    13: (o, w.ap),
                    14: (o, w.a2, 0),
                    15: (o, w.a2, 1),
                }[k]
            ]
        return self.slot(*{7: (w.bm,), 8: (w.bp,), 9: (w.b2, 0), 10: (w.b2, 1)}[k])

    def g0(self):
        self.send(*((6, 4, 5, 2, 3, 0, 1) if self.direct else (3, 0, 1)))
        self.local.start()

    def g0a(self):
        self.take(3)
        self.send(4, 5)

    def g0b(self):
        self.take(0, 1, 4, 5)
        self.send(2, 6)

    def g1(self):
        self.local.wait()
        self.take(*((0, 1, 2, 3, 4, 5, 6) if self.direct else (2, 6)))
        self.send(7, 8, 11)

    def g2(self):
        self.take(7, 8)
        self.send(9, 10, 12, 13)

    def g3(self):
        self.take(9, 10)
        self.send(14, 15)

    def g4(self):
        self.take(11, 12, 13, 14, 15)


class GatherZ(Copies):
    count = 23

    def __init__(self, w, src, raw, local, ss, rs):
        self.w, self.src, self.raw, self.ss, self.rs = w, src, raw, ss, rs
        self.half, self.part = src.shape[1] // 2, src.shape[0] // 2
        self.rows = (w.b, w.bm, w.bp, w.b2)
        self.local = pltpu.make_async_copy(self.own(), self.slot(w.core, w.b, w.zh, w.a, w.zl), local)

    def quarter(self, q):
        return pl.ds(pl.multiple_of(q * self.part, 16), self.part)

    def own(self):
        w = self.w
        return self.src.at[self.quarter(w.zl), pl.ds(pl.multiple_of(w.core * self.half, 128), self.half)]

    def slot(self, h, b, z, a, q):
        return self.raw.at[h, b, z, a, self.quarter(q), :]

    def route(self, k):
        w, c, every = self.w, self.w.core, slice(None)
        if k < 3:
            return self.own(), self.slot(c, w.b, w.zh, w.a, w.zl), (w.a_up, w.a_down, w.a_far)[k]
        if 7 <= k < 19:
            here = self.slot(c, self.rows[(k - 7) // 3], w.zh, every, w.zl)
            return here, here, (w.pair, w.cross, w.third)[(k - 7) % 3]
        place, device = {
            3: ((w.b, w.zh, every, w.zl), w.b_up),
            4: ((w.b, w.zh, every, w.zl), w.b_down),
            5: ((w.bm, w.zh, slice(0, 2), w.zl), w.b_up),
            6: ((w.bp, w.zh, slice(2, 4), w.zl), w.b_down),
            19: ((every, w.zh, every, w.zl), w.twin),
            20: ((every, w.zh, every, 1 - w.zl), w.twin),
            21: ((every, w.zo, every, 1 - w.zl), w.twin),
            22: ((every, w.zo, every, w.zl), w.twin),
        }[k]
        here = self.slot(c, *place)
        return here, here, device

    def lands(self, k):
        w, c, every = self.w, self.w.core, slice(None)
        if k < 3:
            return self.slot(c, w.b, w.zh, (w.am, w.ap, w.a2)[k], w.zl)
        if 7 <= k < 19:
            z, q = ((w.zh, 1 - w.zl), (w.zo, 1 - w.zl), (w.zo, w.zl))[(k - 7) % 3]
            return self.slot(c, self.rows[(k - 7) // 3], z, every, q)
        return self.slot(
            *{
                3: (c, w.bm, w.zh, every, w.zl),
                4: (c, w.bp, w.zh, every, w.zl),
                5: (c, w.b2, w.zh, slice(0, 2), w.zl),
                6: (c, w.b2, w.zh, slice(2, 4), w.zl),
                19: (1 - c, every, w.zh, every, w.zl),
                20: (1 - c, every, w.zh, every, 1 - w.zl),
                21: (1 - c, every, w.zo, every, 1 - w.zl),
                22: (1 - c, every, w.zo, every, w.zl),
            }[k]
        )

    def g0(self):
        self.send(2, 0, 1)
        self.local.start()

    def g1(self):
        self.local.wait()
        self.take(0, 1, 2)
        self.send(3, 4, 9, 7, 8)

    def g2(self):
        self.take(3, 4)
        self.send(5, 6, 12, 10, 11, 15, 13, 14)

    def g3(self):
        self.take(5, 6)
        self.send(18, 16, 17, 19)

    def g3z(self):
        for d in range(3):
            self.take(7 + d, 10 + d, 13 + d, 16 + d)
            self.send(20 + d)

    def g4(self):
        self.take(19, 20, 21, 22)


class Reduce(Copies):
    def __init__(self, w, part, columns, direct, bufs, ss, rs):
        self.w, self.part, self.direct, self.ss, self.rs = w, part, direct, ss, rs
        self.tw, self.fx, self.af, self.zb, self.done = bufs
        self.rows, self.columns = self.tw.shape[-2], pl.ds(columns, self.tw.shape[-1])
        self.used = [k for k in range(17) if k not in ((7, 8, 9) if direct else ())]

    def end(self):
        for k in self.used:
            self.remote(k, *self.route(k)).wait_send()

    def s(self, h, *i):
        left = (slice(None),) * (4 - 1 - len(i))
        return self.part.at[(h, *i, *left, slice(0, self.rows), self.columns)]

    def route(self, k):
        w, c = self.w, self.w.core
        every = slice(None)
        if k < 4:
            j = (w.a2, w.ap, w.am, w.a)[k]
            return self.s(1 - c, j), self.tw.at[j], w.twin
        if k == 16:
            return self.done.at[c], self.done.at[c], w.twin
        if k >= 13:
            place, device = {
                13: ((w.b, w.zo, w.a), w.third),
                14: ((w.b, w.zo, w.a), w.cross),
                15: ((w.b, w.zh, w.a), w.pair),
            }[k]
            return self.s(c, *place), self.zb.at[w.z], device
        if self.direct and k < 10:
            place, device = {4: ((w.b2,), w.b_far), 5: ((w.bp,), w.b_up), 6: ((w.bm,), w.b_down)}[k]
        else:
            place, device = {
                4: ((w.b2, 0), w.b_up),
                5: ((w.b2, 1), w.b_down),
                6: ((w.bp, 1), w.b_up),
                7: ((w.bm, 0), w.b_down),
                8: ((w.bp, 0), w.b_up),
                9: ((w.bm, 1), w.b_down),
                10: ((w.b, every, w.a2), w.a_far),
                11: ((w.b, every, w.ap), w.a_up),
                12: ((w.b, every, w.am), w.a_down),
            }[k]
        return self.s(c, *place), self.lands(k), device

    def lands(self, k):
        w = self.w
        if k < 4:
            return self.tw.at[(w.b2, w.bp, w.bm, w.b)[k]]
        if k == 16:
            return self.done.at[1 - w.core]
        if k >= 13:
            return self.zb.at[((w.z + 2) % 4, 3 - w.z, w.zh * 2 + 1 - w.zl)[k - 13]]
        if self.direct and k < 10:
            return self.fx.at[(2, 0, 1)[k - 4]]
        return {
            4: self.fx.at[2, 0],
            5: self.fx.at[2, 1],
            6: self.fx.at[0, 1],
            7: self.fx.at[1, 0],
            8: self.fx.at[0, 0],
            9: self.fx.at[1, 1],
            10: self.af.at[2],
            11: self.af.at[0],
            12: self.af.at[1],
        }[k]

    def add(self, place, *terms):
        here = self.s(self.w.core, *place)
        total = here[...].astype(F32)
        for term in terms:
            total = total + term[...].astype(F32)
        here[...] = total.astype(BF)

    def add8(self, b, *terms):
        def one(i, _):
            z, a = i // 4, i % 4
            self.add((b, z, a), *[t.at[z, a] for t in terms])
            return 0

        lax.fori_loop(0, 8, one, 0)

    def add4(self, b, z, term):
        def one(a, _):
            self.add((b, z, a), term.at[a])
            return 0

        lax.fori_loop(0, 4, one, 0)

    def r0(self):
        self.send(0, 1, 2, 3)

    def r1(self):
        w = self.w
        for k, b in enumerate((w.b2, w.bp, w.bm)):
            self.take(k)
            self.add8(b, self.tw.at[b])
            self.send(*((4 + k,) if self.direct else ((4, 5), (6,), (7,))[k]))

    def r2(self):
        w = self.w
        self.take(3)
        self.add8(w.b, self.tw.at[w.b])
        if not self.direct:
            self.take(4)
            self.add4(w.bp, 0, self.fx.at[2, 0])
            self.send(8)
            self.take(5)
            self.add4(w.bm, 1, self.fx.at[2, 1])
            self.send(9)

    def r3(self):
        if self.direct:
            self.take(4, 5, 6)
            self.add8(self.w.b, self.fx.at[0], self.fx.at[1], self.fx.at[2])
        else:
            self.take(6, 7, 8, 9)
            self.add8(self.w.b, self.fx.at[0], self.fx.at[1])
        self.send(10, 11, 12)

    def r4(self):
        w = self.w
        self.take(10, 11, 12)
        for z in range(2):
            self.add((w.b, z, w.a), self.af.at[0, z], self.af.at[1, z], self.af.at[2, z])
        self.send(13, 14, 15)
        self.zb[w.z] = self.s(w.core, w.b, w.zh, w.a)[...]

    def r5(self):
        self.take(13, 14, 15)
        self.done[self.w.core] = sum(self.zb[i].astype(F32) for i in range(4))
        self.send(16)

    def r6(self):
        self.take(16)


class ReduceZ(Copies):
    def __init__(self, w, part, bufs, ss, rs):
        self.w, self.part, self.ss, self.rs = w, part, ss, rs
        self.tw, self.zr, self.fx, self.af, self.done = bufs
        self.half = self.af.shape[-2]
        self.rows = (w.b2, w.bp, w.bm, w.b)
        self.count = 25

    def s(self, b, z, a, q):
        return self.part.at[
            self.w.core, b, z, a, pl.ds(pl.multiple_of(q * self.half, 16), self.half), :
        ]

    def route(self, k):
        w, c, every = self.w, self.w.core, slice(None)
        if k < 4:
            j = (w.a2, w.ap, w.am, w.a)[k]
            return self.part.at[1 - c, j], self.tw.at[j], w.twin
        if k < 16:
            b, d = self.rows[(k - 4) // 3], (k - 4) % 3
            z, q, device = (
                (w.zh, 1 - w.zl, w.pair),
                (w.zo, 1 - w.zl, w.cross),
                (w.zo, w.zl, w.third),
            )[d]
            return self.s(b, z, every, q), self.zr.at[d, b], device
        if k >= 22:
            here = self.done.at[c, w.zl]
            return here, here, (w.twin, w.pair, w.diagonal)[k - 22]
        b, a, device = {
            16: (w.b2, every, w.b_far),
            17: (w.bp, every, w.b_up),
            18: (w.bm, every, w.b_down),
            19: (w.b, w.a2, w.a_far),
            20: (w.b, w.ap, w.a_up),
            21: (w.b, w.am, w.a_down),
        }[k]
        return self.s(b, w.zh, a, w.zl), self.lands(k), device

    def lands(self, k):
        w, c = self.w, self.w.core
        if k < 4:
            return self.tw.at[self.rows[k]]
        if k < 16:
            return self.zr.at[(k - 4) % 3, self.rows[(k - 4) // 3]]
        if k < 22:
            return (self.fx if k < 19 else self.af).at[(2, 0, 1)[(k - 16) % 3]]
        return self.done.at[((1 - c, w.zl), (c, 1 - w.zl), (1 - c, 1 - w.zl))[k - 22]]

    def r0(self):
        self.send(0, 1, 2, 3)

    def r1(self, which=(0, 1, 2, 3)):
        for i in which:
            b = self.rows[i]
            self.take(i)

            def one(j, _, b=b):
                z, a = j // 4, j % 4
                here = self.part.at[self.w.core, b, z, a]
                here[...] = (here[...].astype(F32) + self.tw[b, z, a].astype(F32)).astype(BF)
                return 0

            lax.fori_loop(0, 8, one, 0)
            self.send(6 + 3 * i, 4 + 3 * i, 5 + 3 * i)

    def r2(self, which=(0, 1, 2, 3)):
        w = self.w
        for i in which:
            b = self.rows[i]
            self.take(4 + 3 * i, 5 + 3 * i, 6 + 3 * i)

            def one(a, _, b=b):
                self.sum_up(self.s(b, w.zh, a, w.zl), *[self.zr.at[d, b, a] for d in range(3)])
                return 0

            lax.fori_loop(0, 4, one, 0)
            if i < 3:
                self.send(16 + i)

    def sum_up(self, here, *terms):
        total = here[...].astype(F32)
        for term in terms:
            total = total + term[...].astype(F32)
        here[...] = total.astype(BF)

    def r3(self):
        w = self.w
        self.take(16, 17, 18)

        def one(a, _):
            self.sum_up(self.s(w.b, w.zh, a, w.zl), *[self.fx.at[d, a] for d in range(3)])
            return 0

        lax.fori_loop(0, 4, one, 0)
        self.send(19, 20, 21)

    def r4(self):
        w = self.w
        self.take(19, 20, 21)
        total = self.s(w.b, w.zh, w.a, w.zl)[...].astype(F32)
        for d in range(3):
            total = total + self.af[d].astype(F32)
        self.done[w.core, w.zl] = total
        self.send(22, 23, 24)

    def r5(self):
        self.take(22, 23, 24)


def reduce_z_scratch(rows, half):
    part = rows // 2
    return [
        pltpu.VMEM((4, 2, 4, rows, half), BF),
        pltpu.VMEM((3, 4, 4, part, half), BF),
        pltpu.VMEM((3, 4, part, half), BF),
        pltpu.VMEM((3, part, half), BF),
        pltpu.VMEM((2, 2, part, half), F32),
    ]


def reduce_scratch(rows, half):
    return [
        pltpu.VMEM((4, 2, 4, rows, half), BF),
        pltpu.VMEM((3, 2, 4, rows, half), BF),
        pltpu.VMEM((3, 2, rows, half), BF),
        pltpu.VMEM((4, rows, half), BF),
        pltpu.VMEM((2, rows, half), F32),
    ]


def assemble(raw, out, width):
    rows = raw.shape[4]

    def one(g, _):
        x, z = g // 2, g % 2
        place = pl.ds(pl.multiple_of(g * 4 * rows, 4 * rows), 4 * rows)
        for h in range(2):
            parts = [
                raw[0, x, z, y, :, :width] if h == 0 else raw[1, y, z, x, :, :width] for y in range(4)
            ]
            out[place, h * width : (h + 1) * width] = jnp.concatenate(parts, axis=0)
        return 0

    lax.fori_loop(0, 8, one, 0)


def scatter_rows(value, part, h, first):
    n = value.shape[1]
    for f in range(32):
        x, z, y = f // 8, (f // 4) % 2, f % 4
        part[h, x + h * (y - x), z, y + h * (x - y), :, pl.ds(first, n)] = value[
            24 * f : 24 * f + 24
        ].astype(BF)


def stats(x):
    centred = x - jnp.mean(x, axis=1, keepdims=True)
    inv = lax.rsqrt(jnp.mean(centred * centred, axis=1, keepdims=True) + EPSILON)
    return centred * inv, inv


def norm_backward(grad, normed, inv, gain):
    e = grad * gain
    return inv * (
        e - jnp.mean(e, axis=1, keepdims=True) - normed * jnp.mean(e * normed, axis=1, keepdims=True)
    )


def column_sum(v):
    return jnp.sum(v, axis=0, keepdims=True)


def iota(shape, d):
    return lax.broadcasted_iota(jnp.int32, shape, d)


def by24(n):
    return lax.shift_right_logical(n * 2731, 16)


def select24():
    n = iota((SMALL, D), 1)
    return (n - 24 * by24(n) == iota((SMALL, D), 0)).astype(F32).astype(BF)


def select96():
    n = iota((SMALL, FF), 1)
    return (n - 96 * lax.shift_right_logical(by24(n), 2) == iota((SMALL, FF), 0)).astype(F32).astype(BF)


def gate(u):
    square = u * u
    th = jnp.tanh(u * (SLOPE + (SLOPE * 0.044715) * square))
    return 0.5 + 0.5 * th, th, square


def follow(plan, step):
    for at, stages in plan.items():

        @pl.when(step == at)
        def _(stages=stages):
            for stage in stages:
                stage()


def only(stage, i):
    return lambda: stage((i,))


def row_blocks(count, body):
    step = ROWS // count

    def one(i, c):
        return body(pl.ds(pl.multiple_of(i * step, step), step), c)

    return one


def kernel(
    tokens_in, lengths, pads, og_in, in_weight, out_weight, up_weight, down_weight,
    v0, v1, v2, v3, v4, v5, v6, v7, v8,
    layer_out, input_grad, d_in, d_out, d_up, d_down, d_small,
    tokens, og, in_pack, vpack, raw_in, raw_out, raw_up, raw_down, small, w_in, w_out, w_up, w_down,
    h1, joint, lse, attended, residual, h2, h2t, dh2, acc, pre, vec, ub, gvec, dub,
    ls, gs, gr, rs, rr, *bufs,
):
    w = Where()
    w.greet()
    loads = [
        pltpu.make_async_copy(src, dst, ls.at[i])
        for i, (src, dst) in enumerate(
            (
                (in_weight.at[:, 0:1152], in_pack.at[:, 0:1152]),
                (in_weight.at[:, 1152:2304], in_pack.at[:, 1280:2432]),
                (tokens_in, tokens),
                (og_in, og),
            )
        )
    ]
    for load in loads:
        load.start()
    gq, go, gu = [
        Gather(w, s, r, i == 0, ls.at[4 + i], gs.at[i], gr.at[i])
        for i, (s, r) in enumerate(((in_pack, raw_in), (out_weight, raw_out), (up_weight, raw_up)))
    ]
    gd = GatherZ(w, down_weight, raw_down, ls.at[7], gs.at[3], gr.at[3])
    every = (gq, go, gu, gd)
    places = [(raw_up, 0, False), (raw_up, 768, False), (raw_out, 0, False)]
    places += [(raw_in, 0, False), (raw_in, 384, False), (raw_in, 768, True), (small, 0, True)]
    ru0, ru1, ro, rq0, rq1, rq2, rv = [
        Reduce(w, part, first, direct, bufs[5 * i : 5 * i + 5], rs.at[i], rr.at[i])
        for i, (part, first, direct) in enumerate(places)
    ]
    rd = ReduceZ(w, raw_down, bufs[35:40], rs.at[7], rr.at[7])
    vpack[...] = jnp.zeros_like(vpack)
    for j, v in enumerate((v0, v1, v2, v3, v4, v5, v6, v7)):
        vpack[j : j + 1, 0:24] = v[...].astype(F32)
    vpack[8:9, 0:96] = v8[...].astype(F32)
    in_pack[:, 1152:1280] = vpack[...].astype(BF)
    in_pack[:, 2432:2560] = jnp.zeros((24, SMALL), BF)
    gvec[...] = jnp.zeros_like(gvec)

    def codes(dim):
        pos = iota((ROWS, 1) if dim == 0 else (1, ROWS), dim)
        seg = jnp.zeros_like(pos)
        start = jnp.int32(0)
        for j in range(lengths.shape[1]):
            seg = seg + (pos >= start).astype(jnp.int32)
            start = start + lengths[0, j]
        return jnp.where(pos < ROWS - pads[0, 0], seg, -1 - pos)

    loads[0].wait()
    loads[1].wait()
    w.meet()
    for g in every:
        g.g0()

    loads[2].wait()
    loads[3].wait()

    def norm_one(rows, c):
        residual[rows, :] = stats(tokens[rows, :].astype(F32))[0]
        return c

    lax.fori_loop(0, 4, row_blocks(4, norm_one), 0)
    go.g0a()
    gu.g0a()
    gq.g1()
    go.g0b()
    gu.g0b()
    gd.g1()
    go.g1()
    gq.g2()
    gu.g1()
    gd.g2()
    gq.g3()
    gq.g4()
    assemble(raw_in, w_in, 1152)

    packed = raw_in[0, :, :, :, 0:16, 1152:1280].reshape(32 * 16, SMALL)
    spread = nn(packed, select24())
    n, row = iota((ROWS, D), 1), iota((ROWS, D), 0)
    spread = jnp.where(by24(n) == lax.shift_right_logical(row, 4), spread, 0.0)
    vec[...] = jnp.sum(spread.reshape(32, 16, D), axis=0)
    packed = raw_in[0, :, :, :, 0:16, 1152:1280].reshape(32, 16, SMALL)[:, 8:9].reshape(32, SMALL)
    spread = nn(packed, select96())
    n, row = iota((32, FF), 1), iota((32, FF), 0)
    ub[...] = column_sum(jnp.where(lax.shift_right_logical(by24(n), 2) == row, spread, 0.0))

    h1[...] = (residual[...] * vec[0:1, :] + vec[1:2, :]).astype(BF)

    for t in range(3):
        bias = (vec[2:3, :], jnp.zeros((1, D), F32), vec[3:4, :])[t]
        for u in range(2):
            columns = slice(t * D + u * TILE, t * D + (u + 1) * TILE)
            joint[:, columns] = (nn(h1[...], w_in[:, columns]) + bias[:, u * TILE : (u + 1) * TILE]).astype(BF)

    same = codes(0)
    lane = iota((1, 128), 1)

    def scores(queries, keys, first):
        mine = (lane >= 64 * first) & (lane < 64 * first + 64)
        picked = jnp.where(mine, queries.astype(F32) * HEAD**-0.5, 0.0).astype(BF)
        return jnp.where(same == codes(1), nt(keys, picked), LOW)

    def pair_columns(p):
        return [pl.ds(pl.multiple_of(t * D + p * 128, 128), 128) for t in range(3)]

    def attend(p, c):
        cq, ck, cv = pair_columns(p)
        queries, keys, values = joint[:, cq], joint[:, ck], joint[:, cv]
        mixed = None
        for first in range(2):
            s = scores(queries, keys, first)
            top = jnp.max(s, axis=0, keepdims=True)
            e = jnp.exp(s - top)
            total = jnp.sum(e, axis=0, keepdims=True)
            weights = (e * (1.0 / total)).astype(BF)
            lse[2 * p + first] = top + jnp.log(total)
            o = tn(weights, values)
            mixed = o if first == 0 else jnp.where(lane < 64, mixed, o)
        attended[:, cq] = mixed.astype(BF)

        plan = ((gd.g3,), (go.g2,), (gu.g2,), (go.g3,), (), (gu.g3,))
        follow(dict(enumerate(plan)), p)
        return c

    lax.fori_loop(0, 6, attend, 0)

    go.g4()
    assemble(raw_out, w_out, TILE)
    for u in range(2):
        columns = slice(u * TILE, (u + 1) * TILE)
        residual[:, columns] = (
            tokens[:, columns].astype(F32) + nn(attended[...], w_out[:, columns]) + vec[4:5, columns]
        )

    def norm_two(rows, c):
        normed, _ = stats(residual[rows, :])
        h2[rows, :] = (normed * vec[5:6, :] + vec[6:7, :]).astype(BF)
        return c

    lax.fori_loop(0, 4, row_blocks(4, norm_two), 0)
    h2t[...] = h2[...].T
    gu.g4()
    assemble(raw_up, w_up, 1536)
    gd.g3z()
    gd.g4()
    assemble(raw_down, w_down, TILE)
    for g in every:
        g.end()


    def forth(t, c):
        columns = pl.ds(pl.multiple_of(t * TILE, TILE), TILE)
        u = nn(h2[...], w_up[:, columns]) + ub[:, columns]
        pre[:, columns] = u.astype(BF)
        act = (u * gate(u)[0]).astype(BF)
        grad_down = tn(act, og[...]).astype(BF)
        x, z = t // 2, t % 2
        for y in range(4):
            raw_down[0, x, z, y] = grad_down[96 * y : 96 * y + 96, :TILE]
            raw_down[1, y, z, x] = grad_down[96 * y : 96 * y + 96, TILE:]
        return c

    lax.fori_loop(0, 8, forth, 0)
    rd.r0()
    dh2[...] = jnp.zeros_like(dh2)

    def back(i, c):
        t = i // 2 + 4 * (i % 2)
        columns = pl.ds(pl.multiple_of(t * TILE, TILE), TILE)
        u = pre[:, columns].astype(F32)
        low, th, square = gate(u)
        slope = low + u * (1.0 - th * th) * (0.5 * SLOPE + (1.5 * 0.044715 * SLOPE) * square)
        grad_pre = (nt(og[...], w_down[columns, :]) * slope).astype(BF)
        dub[:, columns] = column_sum(grad_pre.astype(F32))
        scatter_rows(nn(h2t[...], grad_pre), raw_up, t // 4, pl.multiple_of((t % 4) * TILE, 128))
        dh2[...] += nt(grad_pre, w_up[:, columns])
        plan = {
            1: (only(rd.r1, 0),),
            2: (only(rd.r1, 1),),
            3: (ru0.r0, only(rd.r1, 2)),
            4: (only(rd.r1, 3),),
            6: (ru0.r1,),
        }
        follow(plan, i)
        return c

    lax.fori_loop(0, 8, back, 0)
    ru1.r0()
    rd.r2((0,))
    ru0.r2()

    def back_two(rows, c):
        normed, inv = stats(residual[rows, :])
        grad = dh2[rows, :]
        up = og[rows, :].astype(F32)
        total = up + norm_backward(grad, normed, inv, vec[5:6, :])
        acc[rows, :] = total
        rounded = total.astype(BF)
        w_up[rows, 0:D] = rounded
        return (
            c[0] + column_sum(rounded.astype(F32)),
            c[1] + column_sum(grad * normed),
            c[2] + column_sum(grad),
            c[3] + column_sum(up),
        )

    zero = jnp.zeros((1, D), F32)
    sums = lax.fori_loop(0, 4, row_blocks(4, back_two), (zero, zero, zero, zero))
    for j, v in zip((4, 5, 6, 7), sums):
        gvec[j : j + 1, :] = v
    ru1.r1()
    grad_branch = w_up.at[0:ROWS, 0:D]
    grad_attended = w_up.at[0:ROWS, D : 2 * D]
    for u in range(2):
        columns = slice(u * TILE, (u + 1) * TILE)
        scatter_rows(tn(attended[...], grad_branch[:, columns]), raw_out, u, 0)
        grad_attended[:, columns] = nt(grad_branch[...], w_out[columns, :]).astype(BF)
    ro.r0()
    rd.r2((1,))
    ru0.r3()
    h1t = h2t
    h1t[...] = h1[...].T

    def attend_back(p, c):
        cq, ck, cv = pair_columns(p)
        queries, keys, values = joint[:, cq], joint[:, ck], joint[:, cv]
        gradient = grad_attended[:, cq]
        dq = dk = dv = None
        for first in range(2):
            mine = (lane >= 64 * first) & (lane < 64 * first + 64)
            weights = jnp.exp(scores(queries, keys, first) - lse[2 * p + first])
            picked = jnp.where(mine, gradient, jnp.zeros_like(gradient))
            grad_weights = nt(values, picked)
            along = jnp.sum(grad_weights * weights, axis=0, keepdims=True)
            grad_scores = (weights * (grad_weights - along)).astype(BF)
            v = nn(weights.astype(BF), gradient)
            k = nn(grad_scores, queries) * HEAD**-0.5
            q = tn(grad_scores, keys) * HEAD**-0.5
            if first == 0:
                dq, dk, dv = q, k, v
            else:
                dq, dk, dv = [jnp.where(lane < 64, l, r) for l, r in ((dq, q), (dk, k), (dv, v))]
        dq, dk, dv = dq.astype(BF), dk.astype(BF), dv.astype(BF)
        joint[:, cq], joint[:, ck], joint[:, cv] = dq, dk, dv
        gvec[2:3, cq] = column_sum(dq.astype(F32))
        gvec[3:4, cq] = column_sum(dv.astype(F32))
        both = jnp.concatenate([dq, dk, dv], axis=1)
        scatter_rows(nn(h1t[...], both), raw_in, p % 2, pl.multiple_of((p // 2) * TILE, 128))
        plan = (
            (ro.r1, ru1.r2),
            (rq0.r0, ru0.r4, only(rd.r2, 2)),
            (rq0.r1, ro.r2, ru1.r3, ru0.r5),
            (rq1.r0, rq0.r2, ro.r3, ru1.r4, only(rd.r2, 3)),
            (rq1.r1, rq0.r3, ro.r4, ru0.r6),
            (rq2.r0, rd.r3, rq1.r2, ru1.r5, rq0.r4),
        )
        follow(dict(enumerate(plan)), p)
        return c

    lax.fori_loop(0, 6, attend_back, 0)

    rq2.r1()
    for u in range(2):
        columns = slice(u * TILE, (u + 1) * TILE)
        dh2[:, columns] = nt(joint[...], w_in[columns, :])

    def sums_one(rows, c):
        normed, _ = stats(tokens[rows, :].astype(F32))
        grad = dh2[rows, :]
        return c[0] + column_sum(grad * normed), c[1] + column_sum(grad)

    sums = lax.fori_loop(0, 4, row_blocks(4, sums_one), (zero, zero))
    for j, v in zip((0, 1), sums):
        gvec[j : j + 1, :] = v

    n, row = iota((32, 16, D), 2), iota((32, 16, D), 0)
    spread = jnp.where(by24(n) == row, jnp.broadcast_to(gvec[...][None], (32, 16, D)), 0.0)
    own = nt(spread.reshape(512, D).astype(BF), select24()).astype(BF).reshape(32, 16, SMALL)
    n, row = iota((32, FF), 1), iota((32, FF), 0)
    spread = jnp.where(lax.shift_right_logical(by24(n), 2) == row, jnp.broadcast_to(dub[...], (32, FF)), 0.0)
    hidden = nt(spread.astype(BF), select96())
    for f in range(32):
        x, z, y = f // 8, (f // 4) % 2, f % 4
        small[0, x, z, y] = own[f]
        small[1, y, z, x] = jnp.broadcast_to(hidden[f : f + 1], (16, SMALL)).astype(BF)
    rv.r0()
    rq2.r2()
    rd.r4()
    rq1.r3()
    ro.r5()
    rv.r1()
    rv.r2()

    def back_one(rows, c):
        normed, inv = stats(tokens[rows, :].astype(F32))
        acc[rows, :] = acc[rows, :] + norm_backward(dh2[rows, :], normed, inv, vec[0:1, :])
        return c

    lax.fori_loop(0, 4, row_blocks(4, back_one), 0)
    grad_copy = pltpu.make_async_copy(acc, input_grad, ls.at[9])
    grad_copy.start()
    rq2.r3()
    rq1.r4()
    rq0.r5()
    rv.r3()

    def result(t, c):
        columns = pl.ds(pl.multiple_of(t * TILE, TILE), TILE)
        u = pre[:, columns].astype(F32)
        residual[...] += nn((u * gate(u)[0]).astype(BF), w_down[columns, :])
        plan = {1: (rq2.r4, rv.r4), 3: (rq1.r5, ru1.r6), 5: (ro.r6, rd.r5)}
        follow(plan, t)
        return c

    lax.fori_loop(0, 8, result, 0)
    h2[...] = (residual[...] + vec[7:8, :]).astype(BF)
    out_copy = pltpu.make_async_copy(h2, layer_out, ls.at[8])
    out_copy.start()
    rq2.r5()
    rv.r5()
    rq0.r6()
    rq1.r6()
    rq2.r6()
    rv.r6()

    for h in range(2):
        d_up[:, h * 1536 : h * 1536 + 768] = ru0.done[h]
        d_up[:, h * 1536 + 768 : h * 1536 + 1536] = ru1.done[h]
        for q in range(2):
            d_down[48 * q : 48 * q + 48, h * TILE : (h + 1) * TILE] = rd.done[h, q]
        d_out[:, h * TILE : (h + 1) * TILE] = ro.done[h]
        d_small[h] = rv.done[h]
        for k, r in enumerate((rq0, rq1, rq2)):
            for j in range(3):
                to = j * D + (2 * k + h) * 128
                d_in[:, to : to + 128] = r.done[h, :, 128 * j : 128 * j + 128]
    for r in (ru0, ru1, rd, ro, rq0, rq1, rq2, rv):
        r.end()
    out_copy.wait()
    grad_copy.wait()


def finish(*refs):
    packed, src, dst, vectors = refs[6], refs[:6], refs[7:13], refs[13:22]
    held, taken, given = refs[22:28], refs[28], refs[29]
    arrive = [pltpu.make_async_copy(s, h, taken.at[i]) for i, (s, h) in enumerate(zip(src, held))]
    leave = [pltpu.make_async_copy(h, d, given.at[i]) for i, (h, d) in enumerate(zip(held, dst))]
    for c in arrive:
        c.start()
    for j in range(8):
        vectors[j][...] = packed[0, j : j + 1, 0:24]
    vectors[8][...] = packed[1, 0:1, 0:96]
    for c, d in zip(arrive, leave):
        c.wait()
        d.start()
    for c in leave:
        c.wait()


def shards(
    tokens, image_lengths, pad_counts, out_grad, first_gain, first_shift, input_weight, query_bias,
    value_bias, output_weight, output_bias, second_gain, second_shift, up_weight, up_bias, down_weight,
    down_bias,
):
    vmem = pl.BlockSpec(memory_space=pltpu.VMEM)
    smem = pl.BlockSpec(memory_space=pltpu.SMEM)
    hbm = pl.BlockSpec(memory_space=pl.ANY)
    scratch = [
        pltpu.VMEM((ROWS, D), BF),
        pltpu.VMEM((ROWS, D), BF),
        pltpu.VMEM((24, 2560), BF),
        pltpu.VMEM((24, SMALL), F32),
        pltpu.VMEM((2, 4, 2, 4, 24, 1280), BF),
        pltpu.VMEM((2, 4, 2, 4, 24, 384), BF),
        pltpu.VMEM((2, 4, 2, 4, 24, 1536), BF),
        pltpu.VMEM((2, 4, 2, 4, 96, 384), BF),
        pltpu.VMEM((2, 4, 2, 4, 16, SMALL), BF),
        pltpu.VMEM((D, 3 * D), BF),
        pltpu.VMEM((D, D), BF),
        pltpu.VMEM((D, FF), BF),
        pltpu.VMEM((FF, D), BF),
        pltpu.VMEM((ROWS, D), BF),
        pltpu.VMEM((ROWS, 3 * D), BF),
        pltpu.VMEM((HEADS, 1, ROWS), F32),
        pltpu.VMEM((ROWS, D), BF),
        pltpu.VMEM((ROWS, D), F32),
        pltpu.VMEM((ROWS, D), BF),
        pltpu.VMEM((D, ROWS), BF),
        pltpu.VMEM((ROWS, D), F32),
        pltpu.VMEM((ROWS, D), F32),
        pltpu.VMEM((ROWS, FF), BF),
        pltpu.VMEM((16, D), F32),
        pltpu.VMEM((1, FF), F32),
        pltpu.VMEM((16, D), F32),
        pltpu.VMEM((1, FF), F32),
        pltpu.SemaphoreType.DMA((10,)),
        pltpu.SemaphoreType.DMA((4, 23)),
        pltpu.SemaphoreType.DMA((4, 23)),
        pltpu.SemaphoreType.DMA((8, 25)),
        pltpu.SemaphoreType.DMA((8, 25)),
    ]
    for rows, half in ((24, 768), (24, 768), (24, 384), (24, 384), (24, 384), (24, 384), (16, SMALL)):
        scratch += reduce_scratch(rows, half)
    scratch += reduce_z_scratch(96, 384)
    shape = jax.ShapeDtypeStruct
    large = [
        shape((ROWS, D), BF),
        shape((ROWS, D), F32),
        shape((24, 3 * D), F32),
        shape((24, D), F32),
        shape((24, FF), F32),
        shape((96, D), F32),
    ]
    vectors = (
        first_gain, first_shift, query_bias, value_bias, output_bias, second_gain, second_shift, down_bias,
        up_bias,
    )
    results = pl.pallas_call(
        kernel,
        out_shape=[*large, shape((2, 16, SMALL), F32)],
        in_specs=[hbm, smem, smem, hbm, hbm, hbm, hbm, hbm, *[vmem] * 9],
        out_specs=[hbm, hbm, *[vmem] * 5],
        scratch_shapes=scratch,
        compiler_params=pltpu.CompilerParams(
            collective_id=0, has_side_effects=True, vmem_limit_bytes=65400 << 10
        ),
        cost_estimate=pl.CostEstimate(flops=25 * 10**9, bytes_accessed=6 * 10**6, transcendentals=8 * 10**6),
    )(
        tokens, image_lengths, pad_counts.reshape(1, 1), out_grad, input_weight, output_weight, up_weight,
        down_weight, *[v.reshape(1, -1) for v in vectors],
    )
    done = pl.pallas_call(
        finish,
        out_shape=[*large, *[shape((1, v.shape[0]), F32) for v in vectors]],
        in_specs=[*[hbm] * 6, vmem],
        out_specs=[*[hbm] * 6, *[vmem] * 9],
        scratch_shapes=[
            *[pltpu.VMEM(x.shape, x.dtype) for x in large],
            pltpu.SemaphoreType.DMA((6,)),
            pltpu.SemaphoreType.DMA((6,)),
        ],
    )(*results)
    layer_out, input_grad, d_in, d_out, d_up, d_down = done[:6]
    v = [x.reshape(-1) for x in done[6:]]
    return (
        layer_out, input_grad, v[0], v[1], d_in, v[2], v[3], d_out, v[4], v[5], v[6], d_up, v[8], d_down,
        v[7],
    )


def solution(mesh):
    tall, flat, part = P(("rep", "fsdp"), None), P("fsdp"), P("fsdp", None)
    return jax.shard_map(
        shards,
        mesh=mesh,
        in_specs=(
            tall, tall, P(("rep", "fsdp")), tall, flat, flat, part, flat, flat, part, flat, flat, flat,
            part, flat, part, flat,
        ),
        out_specs=(
            tall, tall, flat, flat, part, flat, flat, part, flat, flat, flat, part, flat, part, flat,
        ),
        check_vma=False,
    )
```

```python
import functools

import jax
import jax.numpy as jnp
from jax import lax
from jax.experimental import pallas as pl
from jax.experimental.pallas import tpu as pltpu
from jax.sharding import PartitionSpec as P

MESH = pl.DeviceIdType.MESH
BF = jnp.bfloat16
F32 = jnp.float32
EPSILON = 1e-06
ROWS, D, FF, HEADS, HEAD = 512, 768, 3072, 12, 64
TILE = 384
SMALL = 128
LOW = -1e30
SLOPE = 0.7978845608028654


def nn(left, right):
    return jnp.dot(left, right, preferred_element_type=F32)


def nt(left, right):
    return lax.dot_general(left, right, (((1,), (1,)), ((), ())), preferred_element_type=F32)


def tn(left, right):
    return lax.dot_general(left, right, (((0,), (0,)), ((), ())), preferred_element_type=F32)


class Where:
    def __init__(self):
        self.r = lax.axis_index("rep")
        self.f = lax.axis_index("fsdp")
        self.zl, self.core = self.r // 2, self.r % 2
        self.x, self.zh, self.y = self.f // 8, (self.f // 4) % 2, self.f % 4
        self.zo = 1 - self.zh
        c = self.core
        self.a = self.y + c * (self.x - self.y)
        self.b = self.x + c * (self.y - self.x)
        self.ap, self.a2, self.am = (self.a + 1) % 4, (self.a + 2) % 4, (self.a + 3) % 4
        self.bp, self.b2, self.bm = (self.b + 1) % 4, (self.b + 2) % 4, (self.b + 3) % 4
        self.a_up, self.a_down, self.a_far = self.at(1, 0), self.at(3, 0), self.at(2, 0)
        self.b_up, self.b_down, self.b_far = self.at(0, 1), self.at(0, 3), self.at(0, 2)
        self.z = self.zh * 2 + self.zl
        self.twin = {"rep": self.r + 1 - 2 * c, "fsdp": self.f}
        self.pair = {"rep": (1 - self.zl) * 2 + c, "fsdp": self.f}
        self.diagonal = {"rep": (1 - self.zl) * 2 + 1 - c, "fsdp": self.f}
        self.cross, self.cross_up, self.cross_down, self.cross_far = [self.over(i) for i in (0, 1, 3, 2)]
        self.third = {"rep": self.r, "fsdp": (self.x * 2 + self.zo) * 4 + self.y}

    def at(self, da, db):
        c = self.core
        y = (self.y + (1 - c) * da + c * db) % 4
        x = (self.x + c * da + (1 - c) * db) % 4
        return {"rep": self.r, "fsdp": (x * 2 + self.zh) * 4 + y}

    def over(self, da):
        c = self.core
        y = (self.y + (1 - c) * da) % 4
        x = (self.x + c * da) % 4
        return {"rep": (1 - self.zl) * 2 + c, "fsdp": (x * 2 + self.zo) * 4 + y}

    def friends(self):
        near = [self.a_up, self.a_down, self.a_far, self.b_up, self.b_down, self.b_far, self.twin]
        return near + [self.pair, self.diagonal, self.third, self.cross, self.cross_up, self.cross_down, self.cross_far]

    def greet(self):
        sem = pltpu.get_barrier_semaphore()
        for device in self.friends():
            pl.semaphore_signal(sem, inc=1, device_id=device, device_id_type=MESH)

    def meet(self):
        pl.semaphore_wait(pltpu.get_barrier_semaphore(), len(self.friends()))


class Copies:
    def remote(self, k, src, dst, device):
        return pltpu.make_async_remote_copy(
            src_ref=src,
            dst_ref=dst,
            send_sem=self.ss.at[k],
            recv_sem=self.rs.at[k],
            device_id=device,
            device_id_type=MESH,
        )

    def send(self, *which):
        for k in which:
            self.remote(k, *self.route(k)).start()

    def take(self, *which):
        for k in which:
            here = self.lands(k)
            self.remote(k, here, here, self.w.twin).wait_recv()

    def end(self):
        for k in range(self.count):
            self.remote(k, *self.route(k)).wait_send()


class Gather(Copies):
    count = 16

    def __init__(self, w, src, raw, direct, local, ss, rs):
        self.w, self.src, self.raw, self.direct, self.ss, self.rs = w, src, raw, direct, ss, rs
        self.half = src.shape[1] // 2
        self.local = pltpu.make_async_copy(self.own(), self.slot(w.b, w.zh, w.a), local)

    def own(self):
        return self.src.at[:, pl.ds(pl.multiple_of(self.w.core * self.half, 128), self.half)]

    def slot(self, *i):
        return self.raw.at[(self.w.core, *i)]

    def route(self, k):
        w = self.w
        own = (w.b, w.zh, w.a)
        if k in (0, 1, 3) or (self.direct and k < 7):
            to = (w.a_up, w.a_down, w.a_far, w.cross, w.cross_up, w.cross_down, w.cross_far)[k]
            return self.own(), self.slot(*own), to
        place, device = {
            2: ((w.b, 0, w.am), w.a_up),
            4: ((w.b, w.zo, w.a), w.a_up),
            5: ((w.b, w.zo, w.a), w.a_down),
            6: ((w.b, 1, w.ap), w.a_down),
            7: ((w.b,), w.b_up),
            8: ((w.b,), w.b_down),
            9: ((w.bm, 0), w.b_up),
            10: ((w.bp, 1), w.b_down),
            11: ((w.b,), w.twin),
            12: ((w.bm,), w.twin),
            13: ((w.bp,), w.twin),
            14: ((w.b2, 0), w.twin),
            15: ((w.b2, 1), w.twin),
        }[k]
        here = self.slot(*place)
        return here, here, device

    def lands(self, k):
        w = self.w
        if not self.direct and k in (2, 6):
            return self.slot(w.b, k // 6, w.a2)
        if k < 7:
            return self.slot(w.b, w.zh if k < 3 else w.zo, (w.am, w.ap, w.a2, w.a, w.am, w.ap, w.a2)[k])
        if k >= 11:
            o = 1 - w.core
            return self.raw.at[
                {
                    11: (o, w.a),
                    12: (o, w.am),
                    13: (o, w.ap),
                    14: (o, w.a2, 0),
                    15: (o, w.a2, 1),
                }[k]
            ]
        return self.slot(*{7: (w.bm,), 8: (w.bp,), 9: (w.b2, 0), 10: (w.b2, 1)}[k])

    def g0(self):
        self.send(*((6, 4, 5, 2, 3, 0, 1) if self.direct else (3, 0, 1)))
        self.local.start()

    def g0a(self):
        self.take(3)
        self.send(4, 5)

    def g0b(self):
        self.take(0, 1, 4, 5)
        self.send(2, 6)

    def g1(self):
        self.local.wait()
        self.take(*((0, 1, 2, 3, 4, 5, 6) if self.direct else (2, 6)))
        self.send(7, 8, 11)

    def g2(self):
        self.take(7, 8)
        self.send(9, 10, 12, 13)

    def g3(self):
        self.take(9, 10)
        self.send(14, 15)

    def g4(self):
        self.take(11, 12, 13, 14, 15)


class GatherZ(Copies):
    count = 23

    def __init__(self, w, src, raw, local, ss, rs):
        self.w, self.src, self.raw, self.ss, self.rs = w, src, raw, ss, rs
        self.half, self.part = src.shape[1] // 2, src.shape[0] // 2
        self.rows = (w.b, w.bm, w.bp, w.b2)
        self.local = pltpu.make_async_copy(self.own(), self.slot(w.core, w.b, w.zh, w.a, w.zl), local)

    def quarter(self, q):
        return pl.ds(pl.multiple_of(q * self.part, 16), self.part)

    def own(self):
        w = self.w
        return self.src.at[self.quarter(w.zl), pl.ds(pl.multiple_of(w.core * self.half, 128), self.half)]

    def slot(self, h, b, z, a, q):
        return self.raw.at[h, b, z, a, self.quarter(q), :]

    def route(self, k):
        w, c, every = self.w, self.w.core, slice(None)
        if k < 3:
            return self.own(), self.slot(c, w.b, w.zh, w.a, w.zl), (w.a_up, w.a_down, w.a_far)[k]
        if 7 <= k < 19:
            here = self.slot(c, self.rows[(k - 7) // 3], w.zh, every, w.zl)
            return here, here, (w.pair, w.cross, w.third)[(k - 7) % 3]
        place, device = {
            3: ((w.b, w.zh, every, w.zl), w.b_up),
            4: ((w.b, w.zh, every, w.zl), w.b_down),
            5: ((w.bm, w.zh, slice(0, 2), w.zl), w.b_up),
            6: ((w.bp, w.zh, slice(2, 4), w.zl), w.b_down),
            19: ((every, w.zh, every, w.zl), w.twin),
            20: ((every, w.zh, every, 1 - w.zl), w.twin),
            21: ((every, w.zo, every, 1 - w.zl), w.twin),
            22: ((every, w.zo, every, w.zl), w.twin),
        }[k]
        here = self.slot(c, *place)
        return here, here, device

    def lands(self, k):
        w, c, every = self.w, self.w.core, slice(None)
        if k < 3:
            return self.slot(c, w.b, w.zh, (w.am, w.ap, w.a2)[k], w.zl)
        if 7 <= k < 19:
            z, q = ((w.zh, 1 - w.zl), (w.zo, 1 - w.zl), (w.zo, w.zl))[(k - 7) % 3]
            return self.slot(c, self.rows[(k - 7) // 3], z, every, q)
        return self.slot(
            *{
                3: (c, w.bm, w.zh, every, w.zl),
                4: (c, w.bp, w.zh, every, w.zl),
                5: (c, w.b2, w.zh, slice(0, 2), w.zl),
                6: (c, w.b2, w.zh, slice(2, 4), w.zl),
                19: (1 - c, every, w.zh, every, w.zl),
                20: (1 - c, every, w.zh, every, 1 - w.zl),
                21: (1 - c, every, w.zo, every, 1 - w.zl),
                22: (1 - c, every, w.zo, every, w.zl),
            }[k]
        )

    def g0(self):
        self.send(2, 0, 1)
        self.local.start()

    def g1(self):
        self.local.wait()
        self.take(0, 1, 2)
        self.send(3, 4, 9, 7, 8)

    def g2(self):
        self.take(3, 4)
        self.send(5, 6, 12, 10, 11, 15, 13, 14)

    def g3(self):
        self.take(5, 6)
        self.send(18, 16, 17, 19)

    def g3z(self):
        for d in range(3):
            self.take(7 + d, 10 + d, 13 + d, 16 + d)
            self.send(20 + d)

    def g4(self):
        self.take(19, 20, 21, 22)


class Reduce(Copies):
    def __init__(self, w, part, columns, direct, bufs, ss, rs):
        self.w, self.part, self.direct, self.ss, self.rs = w, part, direct, ss, rs
        self.tw, self.fx, self.af, self.zb, self.done = bufs
        self.rows, self.columns = self.tw.shape[-2], pl.ds(columns, self.tw.shape[-1])
        self.used = [k for k in range(17) if k not in ((7, 8, 9) if direct else ())]

    def end(self):
        for k in self.used:
            self.remote(k, *self.route(k)).wait_send()

    def s(self, h, *i):
        left = (slice(None),) * (4 - 1 - len(i))
        return self.part.at[(h, *i, *left, slice(0, self.rows), self.columns)]

    def route(self, k):
        w, c = self.w, self.w.core
        every = slice(None)
        if k < 4:
            j = (w.a2, w.ap, w.am, w.a)[k]
            return self.s(1 - c, j), self.tw.at[j], w.twin
        if k == 16:
            return self.done.at[c], self.done.at[c], w.twin
        if k >= 13:
            place, device = {
                13: ((w.b, w.zo, w.a), w.third),
                14: ((w.b, w.zo, w.a), w.cross),
                15: ((w.b, w.zh, w.a), w.pair),
            }[k]
            return self.s(c, *place), self.zb.at[w.z], device
        if self.direct and k < 10:
            place, device = {4: ((w.b2,), w.b_far), 5: ((w.bp,), w.b_up), 6: ((w.bm,), w.b_down)}[k]
        else:
            place, device = {
                4: ((w.b2, 0), w.b_up),
                5: ((w.b2, 1), w.b_down),
                6: ((w.bp, 1), w.b_up),
                7: ((w.bm, 0), w.b_down),
                8: ((w.bp, 0), w.b_up),
                9: ((w.bm, 1), w.b_down),
                10: ((w.b, every, w.a2), w.a_far),
                11: ((w.b, every, w.ap), w.a_up),
                12: ((w.b, every, w.am), w.a_down),
            }[k]
        return self.s(c, *place), self.lands(k), device

    def lands(self, k):
        w = self.w
        if k < 4:
            return self.tw.at[(w.b2, w.bp, w.bm, w.b)[k]]
        if k == 16:
            return self.done.at[1 - w.core]
        if k >= 13:
            return self.zb.at[((w.z + 2) % 4, 3 - w.z, w.zh * 2 + 1 - w.zl)[k - 13]]
        if self.direct and k < 10:
            return self.fx.at[(2, 0, 1)[k - 4]]
        return {
            4: self.fx.at[2, 0],
            5: self.fx.at[2, 1],
            6: self.fx.at[0, 1],
            7: self.fx.at[1, 0],
            8: self.fx.at[0, 0],
            9: self.fx.at[1, 1],
            10: self.af.at[2],
            11: self.af.at[0],
            12: self.af.at[1],
        }[k]

    def add(self, place, *terms):
        here = self.s(self.w.core, *place)
        if len(terms) == 1:
            here[...] = here[...] + terms[0][...]
            return
        total = here[...].astype(F32)
        for term in terms:
            total = total + term[...].astype(F32)
        here[...] = total.astype(BF)

    def add8(self, b, *terms):
        def one(i, _):
            z, a = i // 4, i % 4
            self.add((b, z, a), *[t.at[z, a] for t in terms])
            return 0

        lax.fori_loop(0, 8, one, 0)

    def add4(self, b, z, term):
        def one(a, _):
            self.add((b, z, a), term.at[a])
            return 0

        lax.fori_loop(0, 4, one, 0)

    def r0(self):
        self.send(0, 1, 2, 3)

    def r1(self):
        w = self.w
        for k, b in enumerate((w.b2, w.bp, w.bm)):
            self.take(k)
            self.add8(b, self.tw.at[b])
            self.send(*((4 + k,) if self.direct else ((4, 5), (6,), (7,))[k]))

    def r2(self):
        w = self.w
        self.take(3)
        self.add8(w.b, self.tw.at[w.b])
        if not self.direct:
            self.take(4)
            self.add4(w.bp, 0, self.fx.at[2, 0])
            self.send(8)
            self.take(5)
            self.add4(w.bm, 1, self.fx.at[2, 1])
            self.send(9)

    def r3(self):
        if self.direct:
            self.take(4, 5, 6)
            self.add8(self.w.b, self.fx.at[0], self.fx.at[1], self.fx.at[2])
        else:
            self.take(6, 7, 8, 9)
            self.add8(self.w.b, self.fx.at[0], self.fx.at[1])
        self.send(10, 11, 12)

    def r4(self):
        w = self.w
        self.take(10, 11, 12)
        for z in range(2):
            self.add((w.b, z, w.a), self.af.at[0, z], self.af.at[1, z], self.af.at[2, z])
        self.send(13, 14, 15)
        self.zb[w.z] = self.s(w.core, w.b, w.zh, w.a)[...]

    def r5(self):
        self.take(13, 14, 15)
        self.done[self.w.core] = sum(self.zb[i].astype(F32) for i in range(4))
        self.send(16)

    def r6(self):
        self.take(16)


class ReduceZ(Copies):
    def __init__(self, w, part, bufs, ss, rs):
        self.w, self.part, self.ss, self.rs = w, part, ss, rs
        self.tw, self.zr, self.fx, self.af, self.done = bufs
        self.half = self.af.shape[-2]
        self.rows = (w.b2, w.bp, w.bm, w.b)
        self.count = 25

    def s(self, b, z, a, q):
        return self.part.at[
            self.w.core, b, z, a, pl.ds(pl.multiple_of(q * self.half, 16), self.half), :
        ]

    def route(self, k):
        w, c, every = self.w, self.w.core, slice(None)
        if k < 4:
            j = (w.a2, w.ap, w.am, w.a)[k]
            return self.part.at[1 - c, j], self.tw.at[j], w.twin
        if k < 16:
            b, d = self.rows[(k - 4) // 3], (k - 4) % 3
            z, q, device = (
                (w.zh, 1 - w.zl, w.pair),
                (w.zo, 1 - w.zl, w.cross),
                (w.zo, w.zl, w.third),
            )[d]
            return self.s(b, z, every, q), self.zr.at[d, b], device
        if k >= 22:
            here = self.done.at[c, w.zl]
            return here, here, (w.twin, w.pair, w.diagonal)[k - 22]
        b, a, device = {
            16: (w.b2, every, w.b_far),
            17: (w.bp, every, w.b_up),
            18: (w.bm, every, w.b_down),
            19: (w.b, w.a2, w.a_far),
            20: (w.b, w.ap, w.a_up),
            21: (w.b, w.am, w.a_down),
        }[k]
        return self.s(b, w.zh, a, w.zl), self.lands(k), device

    def lands(self, k):
        w, c = self.w, self.w.core
        if k < 4:
            return self.tw.at[self.rows[k]]
        if k < 16:
            return self.zr.at[(k - 4) % 3, self.rows[(k - 4) // 3]]
        if k < 22:
            return (self.fx if k < 19 else self.af).at[(2, 0, 1)[(k - 16) % 3]]
        return self.done.at[((1 - c, w.zl), (c, 1 - w.zl), (1 - c, 1 - w.zl))[k - 22]]

    def r0(self):
        self.send(0, 1, 2, 3)

    def r1(self, which=(0, 1, 2, 3)):
        for i in which:
            b = self.rows[i]
            self.take(i)

            def one(j, _, b=b):
                z, a = j // 4, j % 4
                here = self.part.at[self.w.core, b, z, a]
                here[...] = here[...] + self.tw[b, z, a]
                return 0

            lax.fori_loop(0, 8, one, 0)
            self.send(6 + 3 * i, 4 + 3 * i, 5 + 3 * i)

    def r2(self, which=(0, 1, 2, 3)):
        w = self.w
        for i in which:
            b = self.rows[i]
            self.take(4 + 3 * i, 5 + 3 * i, 6 + 3 * i)

            def one(a, _, b=b):
                self.sum_up(self.s(b, w.zh, a, w.zl), *[self.zr.at[d, b, a] for d in range(3)])
                return 0

            lax.fori_loop(0, 4, one, 0)
            if i < 3:
                self.send(16 + i)

    def sum_up(self, here, *terms):
        total = here[...].astype(F32)
        for term in terms:
            total = total + term[...].astype(F32)
        here[...] = total.astype(BF)

    def r3(self):
        w = self.w
        self.take(16, 17, 18)

        def one(a, _):
            self.sum_up(self.s(w.b, w.zh, a, w.zl), *[self.fx.at[d, a] for d in range(3)])
            return 0

        lax.fori_loop(0, 4, one, 0)
        self.send(19, 20, 21)

    def r4(self):
        w = self.w
        self.take(19, 20, 21)
        total = self.s(w.b, w.zh, w.a, w.zl)[...].astype(F32)
        for d in range(3):
            total = total + self.af[d].astype(F32)
        self.done[w.core, w.zl] = total
        self.send(22, 23, 24)

    def r5(self):
        self.take(22, 23, 24)


def reduce_z_scratch(rows, half):
    part = rows // 2
    return [
        pltpu.VMEM((4, 2, 4, rows, half), BF),
        pltpu.VMEM((3, 4, 4, part, half), BF),
        pltpu.VMEM((3, 4, part, half), BF),
        pltpu.VMEM((3, part, half), BF),
        pltpu.VMEM((2, 2, part, half), F32),
    ]


def reduce_scratch(rows, half):
    return [
        pltpu.VMEM((4, 2, 4, rows, half), BF),
        pltpu.VMEM((3, 2, 4, rows, half), BF),
        pltpu.VMEM((3, 2, rows, half), BF),
        pltpu.VMEM((4, rows, half), BF),
        pltpu.VMEM((2, rows, half), F32),
    ]


def assemble(raw, out, width):
    rows = raw.shape[4]

    def one(g, _):
        x, z = g // 2, g % 2
        place = pl.ds(pl.multiple_of(g * 4 * rows, 4 * rows), 4 * rows)
        for h in range(2):
            parts = [
                raw[0, x, z, y, :, :width] if h == 0 else raw[1, y, z, x, :, :width] for y in range(4)
            ]
            out[place, h * width : (h + 1) * width] = jnp.concatenate(parts, axis=0)
        return 0

    lax.fori_loop(0, 8, one, 0)


def scatter_rows(left, right, part, h, first):
    n = right.shape[1]
    for k in range(2):
        value = nn(left[k * TILE : (k + 1) * TILE, :], right[...])
        for i in range(16):
            f = 16 * k + i
            x, z, y = f // 8, (f // 4) % 2, f % 4
            part[h, x + h * (y - x), z, y + h * (x - y), :, pl.ds(first, n)] = value[
                24 * i : 24 * i + 24
            ].astype(BF)


def stats(x):
    centred = x - jnp.mean(x, axis=1, keepdims=True)
    inv = lax.rsqrt(jnp.mean(centred * centred, axis=1, keepdims=True) + EPSILON)
    return centred * inv, inv


def norm_backward(grad, normed, inv, gain):
    e = grad * gain
    return inv * (
        e - jnp.mean(e, axis=1, keepdims=True) - normed * jnp.mean(e * normed, axis=1, keepdims=True)
    )


def column_sum(v):
    return jnp.sum(v, axis=0, keepdims=True)


def iota(shape, d):
    return lax.broadcasted_iota(jnp.int32, shape, d)


def by24(n):
    return lax.shift_right_logical(n * 2731, 16)


def select24():
    n = iota((SMALL, D), 1)
    return (n - 24 * by24(n) == iota((SMALL, D), 0)).astype(F32).astype(BF)


def select96():
    n = iota((SMALL, FF), 1)
    return (n - 96 * lax.shift_right_logical(by24(n), 2) == iota((SMALL, FF), 0)).astype(F32).astype(BF)


def gate(u):
    inner = u * (SLOPE + (SLOPE * 0.044715) * (u * u))
    return 0.5 + 0.5 * jnp.tanh(inner), inner


def gelu(u):
    return u * gate(u)[0]


def gelu_slope(u):
    low, inner = gate(u)
    return low + low * (1.0 - low) * (6.0 * inner - (4.0 * SLOPE) * u)


def follow(plan, step):
    for at, stages in plan.items():

        @pl.when(step == at)
        def _(stages=stages):
            for stage in stages:
                stage()


def only(stage, i):
    return lambda: stage((i,))


def row_blocks(count, body):
    step = ROWS // count

    def one(i, c):
        return body(pl.ds(pl.multiple_of(i * step, step), step), c)

    return one


def kernel(
    tokens_in, lengths, pads, og_in, in_weight, out_weight, up_weight, down_weight,
    v0, v1, v2, v3, v4, v5, v6, v7, v8,
    layer_out, input_grad, s_up0, s_up1, s_out, s_in0, s_in1, s_in2, s_small, s_down,
    tokens, og, in_pack, vpack, raw_in, raw_out, raw_up, raw_down, small, w_in, w_out, w_up, w_down,
    h1, joint, lse, attended, residual, h2, h2t, dh2, part, other, pre, vec, ub, gvec, dub,
    ls, gs, gr, rs, rr, *bufs,
):
    w = Where()
    w.greet()
    loads = [
        pltpu.make_async_copy(src, dst, ls.at[i])
        for i, (src, dst) in enumerate(
            (
                (in_weight.at[:, 0:1152], in_pack.at[:, 0:1152]),
                (in_weight.at[:, 1152:2304], in_pack.at[:, 1280:2432]),
                (tokens_in, tokens),
                (og_in, og),
            )
        )
    ]
    for load in loads:
        load.start()
    gq, go, gu = [
        Gather(w, s, r, i == 0, ls.at[4 + i], gs.at[i], gr.at[i])
        for i, (s, r) in enumerate(((in_pack, raw_in), (out_weight, raw_out), (up_weight, raw_up)))
    ]
    gd = GatherZ(w, down_weight, raw_down, ls.at[7], gs.at[3], gr.at[3])
    every = (gq, go, gu, gd)
    places = [(raw_up, 0, False), (raw_up, 768, False), (raw_out, 0, False)]
    places += [(raw_in, 0, False), (raw_in, 384, False), (raw_in, 768, True), (small, 0, True)]
    ru0, ru1, ro, rq0, rq1, rq2, rv = [
        Reduce(w, part, first, direct, bufs[5 * i : 5 * i + 5], rs.at[i], rr.at[i])
        for i, (part, first, direct) in enumerate(places)
    ]
    rd = ReduceZ(w, raw_down, bufs[35:40], rs.at[7], rr.at[7])
    vpack[...] = jnp.zeros_like(vpack)
    for j, v in enumerate((v0, v1, v2, v3, v4, v5, v6, v7)):
        vpack[j : j + 1, 0:24] = v[...].astype(F32)
    vpack[8:9, 0:96] = v8[...].astype(F32)
    in_pack[:, 1152:1280] = vpack[...].astype(BF)
    in_pack[:, 2432:2560] = jnp.zeros((24, SMALL), BF)
    gvec[...] = jnp.zeros_like(gvec)

    def codes(dim):
        pos = iota((ROWS, 1) if dim == 0 else (1, ROWS), dim)
        seg = jnp.zeros_like(pos)
        start = jnp.int32(0)
        for j in range(lengths.shape[1]):
            seg = seg + (pos >= start).astype(jnp.int32)
            start = start + lengths[0, j]
        return jnp.where(pos < ROWS - pads[0, 0], seg, -1 - pos)

    loads[0].wait()
    loads[1].wait()
    w.meet()
    for g in every:
        g.g0()

    loads[2].wait()
    loads[3].wait()

    def norm_one(rows, c):
        residual[rows, :] = stats(tokens[rows, :].astype(F32))[0]
        return c

    lax.fori_loop(0, 4, row_blocks(4, norm_one), 0)
    go.g0a()
    gu.g0a()
    gq.g1()
    go.g0b()
    gu.g0b()
    gd.g1()
    go.g1()
    gq.g2()
    gu.g1()
    gd.g2()
    gq.g3()
    gq.g4()
    assemble(raw_in, w_in, 1152)

    packed = raw_in[0, :, :, :, 0:16, 1152:1280].reshape(32 * 16, SMALL)
    spread = nn(packed, select24())
    n, row = iota((ROWS, D), 1), iota((ROWS, D), 0)
    spread = jnp.where(by24(n) == lax.shift_right_logical(row, 4), spread, 0.0)
    vec[...] = jnp.sum(spread.reshape(32, 16, D), axis=0)
    packed = raw_in[0, :, :, :, 0:16, 1152:1280].reshape(32, 16, SMALL)[:, 8:9].reshape(32, SMALL)
    spread = nn(packed, select96())
    n, row = iota((32, FF), 1), iota((32, FF), 0)
    ub[...] = column_sum(jnp.where(lax.shift_right_logical(by24(n), 2) == row, spread, 0.0))

    h1[...] = (residual[...] * vec[0:1, :] + vec[1:2, :]).astype(BF)

    for t, bias in enumerate((vec[2:3, :], 0.0, vec[3:4, :])):
        columns = slice(t * D, (t + 1) * D)
        joint[:, columns] = (nn(h1[...], w_in[:, columns]) + bias).astype(BF)

    same = codes(0)
    lane = iota((1, 128), 1)

    def scores(queries, keys, first):
        mine = (lane >= 64 * first) & (lane < 64 * first + 64)
        picked = jnp.where(mine, queries.astype(F32) * HEAD**-0.5, 0.0).astype(BF)
        return jnp.where(same == codes(1), nt(keys, picked), LOW)

    def pair_columns(p):
        return [pl.ds(pl.multiple_of(t * D + p * 128, 128), 128) for t in range(3)]

    def attend(p, c):
        cq, ck, cv = pair_columns(p)
        queries, keys, values = joint[:, cq], joint[:, ck], joint[:, cv]
        mixed = None
        for first in range(2):
            s = scores(queries, keys, first)
            top = jnp.max(s, axis=0, keepdims=True)
            e = jnp.exp(s - top)
            total = jnp.sum(e, axis=0, keepdims=True)
            weights = (e * (1.0 / total)).astype(BF)
            lse[2 * p + first] = top + jnp.log(total)
            o = tn(weights, values)
            mixed = o if first == 0 else jnp.where(lane < 64, mixed, o)
        attended[:, cq] = mixed.astype(BF)

        plan = ((gd.g3,), (go.g2,), (gu.g2,), (go.g3,), (), (gu.g3,))
        follow(dict(enumerate(plan)), p)
        return c

    lax.fori_loop(0, 6, attend, 0)

    go.g4()
    assemble(raw_out, w_out, TILE)
    residual[...] = tokens[...].astype(F32) + nn(attended[...], w_out[...]) + vec[4:5, :]

    def norm_two(rows, c):
        normed, _ = stats(residual[rows, :])
        h2[rows, :] = (normed * vec[5:6, :] + vec[6:7, :]).astype(BF)
        return c

    lax.fori_loop(0, 4, row_blocks(4, norm_two), 0)
    h2t[...] = h2[...].T
    gu.g4()
    assemble(raw_up, w_up, 1536)
    def wide(t):
        return pl.ds(pl.multiple_of(t * D, D), D)

    def ahead(t, c):
        columns = wide(t)
        pre[:, columns] = (nn(h2[...], w_up[:, columns]) + ub[:, columns]).astype(BF)
        return c

    lax.fori_loop(0, 4, ahead, 0)
    gd.g3z()
    gd.g4()
    assemble(raw_down, w_down, TILE)
    for g in every:
        g.end()


    def activate(to, t):
        to[...] = gelu(pre[:, wide(t)].astype(F32)).astype(BF)

    def forth(i, c):
        for now, later, t in ((part, other, 2 * i), (other, part, 2 * i + 1)):
            activate(later, (t + 1) % 4)
            grad = tn(now[...], og[...])
            for f in range(8):
                z, y, rows = f // 4, f % 4, slice(96 * f, 96 * f + 96)
                raw_down[0, t, z, y] = grad[rows, :TILE].astype(BF)
                raw_down[1, y, z, t] = grad[rows, TILE:].astype(BF)
        return c

    activate(part, 0)
    lax.fori_loop(0, 2, forth, 0)
    rd.r0()

    dh2[...] = jnp.zeros_like(dh2)

    def tile_at(i):
        return i // 2 + 2 * (i % 2)

    def front(to, t):
        columns = wide(t)
        total = jnp.zeros((1, D), F32)
        for r in range(0, ROWS, 256):
            slope = gelu_slope(pre[r : r + 256, columns].astype(F32))
            grad_pre = (nt(og[r : r + 256, :], w_down[columns, :]) * slope).astype(BF)
            to[r : r + 256, :] = grad_pre
            total = total + column_sum(grad_pre.astype(F32))
        dub[:, columns] = total

    def back(j, c):
        for now, later, i in ((part, other, 2 * j), (other, part, 2 * j + 1)):
            t = tile_at(i)
            front(later, tile_at((i + 1) % 4))
            scatter_rows(h2t, now, raw_up, t // 2, pl.multiple_of((t % 2) * D, 128))
            dh2[...] += nt(now[...], w_up[:, wide(t)])
            plan = {
                0: (only(rd.r1, 0),),
                1: (ru0.r0, only(rd.r1, 1), only(rd.r1, 2)),
                2: (only(rd.r1, 3),),
                3: (ru0.r1,),
            }
            follow(plan, i)
        return c

    front(part, 0)
    lax.fori_loop(0, 2, back, 0)
    ru1.r0()

    def back_two(rows, c):
        normed, inv = stats(residual[rows, :])
        grad = dh2[rows, :]
        up = og[rows, :].astype(F32)
        total = up + norm_backward(grad, normed, inv, vec[5:6, :])
        rounded = total.astype(BF)
        w_up[rows, 0:D] = rounded
        return (
            c[0] + column_sum(rounded.astype(F32)),
            c[1] + column_sum(grad * normed),
            c[2] + column_sum(grad),
            c[3] + column_sum(up),
        )

    zero = jnp.zeros((1, D), F32)
    sums = lax.fori_loop(0, 4, row_blocks(4, back_two), (zero, zero, zero, zero))
    for j, v in zip((4, 5, 6, 7), sums):
        gvec[j : j + 1, :] = v
    grad_branch = w_up.at[0:ROWS, 0:D]
    grad_attended = w_up.at[0:ROWS, D : 2 * D]
    attended_t = h2t
    attended_t[...] = attended[...].T
    for u in range(2):
        columns = slice(u * TILE, (u + 1) * TILE)
        scatter_rows(attended_t, grad_branch.at[:, columns], raw_out, u, 0)
    grad_attended[...] = nt(grad_branch[...], w_out[...]).astype(BF)
    ro.r0()
    ru0.r2()
    ru1.r1()
    h1t = h2t
    h1t[...] = h1[...].T

    def attend_back(p, c):
        cq, ck, cv = pair_columns(p)
        queries, keys, values = joint[:, cq], joint[:, ck], joint[:, cv]
        gradient = grad_attended[:, cq]
        dq = dk = dv = None
        for first in range(2):
            mine = (lane >= 64 * first) & (lane < 64 * first + 64)
            weights = jnp.exp(scores(queries, keys, first) - lse[2 * p + first])
            picked = jnp.where(mine, gradient, jnp.zeros_like(gradient))
            grad_weights = nt(values, picked)
            along = jnp.sum(grad_weights * weights, axis=0, keepdims=True)
            grad_scores = (weights * (grad_weights - along)).astype(BF)
            v = nn(weights.astype(BF), gradient)
            k = nn(grad_scores, queries) * HEAD**-0.5
            q = tn(grad_scores, keys) * HEAD**-0.5
            if first == 0:
                dq, dk, dv = q, k, v
            else:
                dq, dk, dv = [jnp.where(lane < 64, l, r) for l, r in ((dq, q), (dk, k), (dv, v))]
        dq, dk, dv = dq.astype(BF), dk.astype(BF), dv.astype(BF)
        joint[:, cq], joint[:, ck], joint[:, cv] = dq, dk, dv
        gvec[2:3, cq] = column_sum(dq.astype(F32))
        gvec[3:4, cq] = column_sum(dv.astype(F32))
        both = part.at[:, 0:TILE]
        both[:, 0:128], both[:, 128:256], both[:, 256:384] = dq, dk, dv
        scatter_rows(h1t, both, raw_in, p % 2, pl.multiple_of((p // 2) * TILE, 128))
        plan = (
            (ro.r1,),
            (rq0.r0, ru0.r3, ru1.r2),
            (rq0.r1, ro.r2, ru0.r4),
            (rq1.r0, rq0.r2, ru1.r3, ro.r3),
            (rq1.r1, ru0.r5, rd.r2, ru1.r4),
            (rq2.r0, rq0.r3, rq1.r2, ro.r4, rd.r3),
        )
        follow(dict(enumerate(plan)), p)
        return c

    lax.fori_loop(0, 6, attend_back, 0)

    rq2.r1()
    dh2[...] = nt(joint[...], w_in[...])

    def sums_one(rows, c):
        normed, _ = stats(tokens[rows, :].astype(F32))
        grad = dh2[rows, :]
        return c[0] + column_sum(grad * normed), c[1] + column_sum(grad)

    sums = lax.fori_loop(0, 4, row_blocks(4, sums_one), (zero, zero))
    for j, v in zip((0, 1), sums):
        gvec[j : j + 1, :] = v

    n, row = iota((32, 16, D), 2), iota((32, 16, D), 0)
    spread = jnp.where(by24(n) == row, jnp.broadcast_to(gvec[...][None], (32, 16, D)), 0.0)
    own = nt(spread.reshape(512, D).astype(BF), select24()).astype(BF).reshape(32, 16, SMALL)
    n, row = iota((32, FF), 1), iota((32, FF), 0)
    spread = jnp.where(lax.shift_right_logical(by24(n), 2) == row, jnp.broadcast_to(dub[...], (32, FF)), 0.0)
    hidden = nt(spread.astype(BF), select96())
    for f in range(32):
        x, z, y = f // 8, (f // 4) % 2, f % 4
        small[0, x, z, y] = own[f]
        small[1, y, z, x] = jnp.broadcast_to(hidden[f : f + 1], (16, SMALL)).astype(BF)
    rv.r0()
    rq2.r2()
    rd.r4()
    rq0.r4()
    rq1.r3()
    ru1.r5()
    ro.r5()
    rv.r1()
    rv.r2()

    def back_one(rows, c):
        normed, inv = stats(tokens[rows, :].astype(F32))
        dh2[rows, :] = grad_branch[rows, :].astype(F32) + norm_backward(dh2[rows, :], normed, inv, vec[0:1, :])
        return c

    lax.fori_loop(0, 4, row_blocks(4, back_one), 0)
    grad_copy = pltpu.make_async_copy(dh2, input_grad, ls.at[9])
    grad_copy.start()
    rq2.r3()
    rq1.r4()
    rq0.r5()
    rv.r3()
    for t in range(4):
        activate(pre.at[:, t * D : (t + 1) * D], t)
    rq2.r4()
    rv.r4()

    def result(t, c):
        columns = pl.ds(pl.multiple_of(t * 256, 256), 256)
        h2[:, columns] = (residual[:, columns] + vec[7:8, columns] + nn(pre[...], w_down[:, columns])).astype(BF)
        follow({1: (rq2.r5, rq1.r5, rv.r5)}, t)
        return c

    lax.fori_loop(0, 3, result, 0)
    out_copy = pltpu.make_async_copy(h2, layer_out, ls.at[8])
    out_copy.start()
    sums = (ru0, ru1, ro, rq0, rq1, rq2, rv, rd)
    hand = [
        pltpu.make_async_copy(r.done, to, ls.at[10 + i])
        for i, (r, to) in enumerate(
            zip(sums, (s_up0, s_up1, s_out, s_in0, s_in1, s_in2, s_small, s_down))
        )
    ]
    for r, c in zip(sums, hand):
        (r.r5 if r is rd else r.r6)()
        c.start()

    for r in sums:
        r.end()
    out_copy.wait()
    grad_copy.wait()
    for c in hand:
        c.wait()


def finish(
    layer_in, grad_in, up0, up1, out, in0, in1, in2, small, down,
    layer_out, grad_out, d_in, d_out, d_up, d_down, v0, v1, v2, v3, v4, v5, v6, v7, v8,
    held_layer, held_grad, taken, given,
):
    pairs = ((layer_in, held_layer, layer_out), (grad_in, held_grad, grad_out))
    arrive = [pltpu.make_async_copy(s, h, taken.at[i]) for i, (s, h, d) in enumerate(pairs)]
    leave = [pltpu.make_async_copy(h, d, given.at[i]) for i, (s, h, d) in enumerate(pairs)]
    for c in arrive:
        c.start()
    for h in range(2):
        d_up[:, h * 1536 : h * 1536 + 768] = up0[h]
        d_up[:, h * 1536 + 768 : h * 1536 + 1536] = up1[h]
        for q in range(2):
            d_down[48 * q : 48 * q + 48, h * TILE : (h + 1) * TILE] = down[h, q]
        d_out[:, h * TILE : (h + 1) * TILE] = out[h]
        for k, part in enumerate((in0, in1, in2)):
            for j in range(3):
                to = j * D + (2 * k + h) * 128
                d_in[:, to : to + 128] = part[h, :, 128 * j : 128 * j + 128]
    for j, v in enumerate((v0, v1, v2, v3, v4, v5, v6, v7)):
        v[...] = small[0, j : j + 1, 0:24]
    v8[...] = small[1, 0:1, 0:96]
    for c, d in zip(arrive, leave):
        c.wait()
        d.start()
    for c in leave:
        c.wait()


def shards(
    tokens, image_lengths, pad_counts, out_grad, first_gain, first_shift, input_weight, query_bias,
    value_bias, output_weight, output_bias, second_gain, second_shift, up_weight, up_bias, down_weight,
    down_bias,
):
    vmem = pl.BlockSpec(memory_space=pltpu.VMEM)
    smem = pl.BlockSpec(memory_space=pltpu.SMEM)
    hbm = pl.BlockSpec(memory_space=pl.ANY)
    scratch = [
        pltpu.VMEM((ROWS, D), BF),
        pltpu.VMEM((ROWS, D), BF),
        pltpu.VMEM((24, 2560), BF),
        pltpu.VMEM((24, SMALL), F32),
        pltpu.VMEM((2, 4, 2, 4, 24, 1280), BF),
        pltpu.VMEM((2, 4, 2, 4, 24, 384), BF),
        pltpu.VMEM((2, 4, 2, 4, 24, 1536), BF),
        pltpu.VMEM((2, 4, 2, 4, 96, 384), BF),
        pltpu.VMEM((2, 4, 2, 4, 16, SMALL), BF),
        pltpu.VMEM((D, 3 * D), BF),
        pltpu.VMEM((D, D), BF),
        pltpu.VMEM((D, FF), BF),
        pltpu.VMEM((FF, D), BF),
        pltpu.VMEM((ROWS, D), BF),
        pltpu.VMEM((ROWS, 3 * D), BF),
        pltpu.VMEM((HEADS, 1, ROWS), F32),
        pltpu.VMEM((ROWS, D), BF),
        pltpu.VMEM((ROWS, D), F32),
        pltpu.VMEM((ROWS, D), BF),
        pltpu.VMEM((D, ROWS), BF),
        pltpu.VMEM((ROWS, D), F32),
        pltpu.VMEM((ROWS, D), BF),
        pltpu.VMEM((ROWS, D), BF),
        pltpu.VMEM((ROWS, FF), BF),
        pltpu.VMEM((16, D), F32),
        pltpu.VMEM((1, FF), F32),
        pltpu.VMEM((16, D), F32),
        pltpu.VMEM((1, FF), F32),
        pltpu.SemaphoreType.DMA((18,)),
        pltpu.SemaphoreType.DMA((4, 23)),
        pltpu.SemaphoreType.DMA((4, 23)),
        pltpu.SemaphoreType.DMA((8, 25)),
        pltpu.SemaphoreType.DMA((8, 25)),
    ]
    for rows, half in ((24, 768), (24, 768), (24, 384), (24, 384), (24, 384), (24, 384), (16, SMALL)):
        scratch += reduce_scratch(rows, half)
    scratch += reduce_z_scratch(96, 384)
    shape = jax.ShapeDtypeStruct
    large = [
        shape((ROWS, D), BF),
        shape((ROWS, D), F32),
        shape((24, 3 * D), F32),
        shape((24, D), F32),
        shape((24, FF), F32),
        shape((96, D), F32),
    ]
    vectors = (
        first_gain, first_shift, query_bias, value_bias, output_bias, second_gain, second_shift, down_bias,
        up_bias,
    )
    halves = [shape((2, 24, 768), F32)] * 2 + [shape((2, 24, 384), F32)] * 4
    halves += [shape((2, 16, SMALL), F32), shape((2, 2, 48, 384), F32)]
    results = pl.pallas_call(
        kernel,
        out_shape=[*large[:2], *halves],
        in_specs=[hbm, smem, smem, hbm, hbm, hbm, hbm, hbm, *[vmem] * 9],
        out_specs=[hbm] * 10,
        scratch_shapes=scratch,
        compiler_params=pltpu.CompilerParams(
            collective_id=0, has_side_effects=True, vmem_limit_bytes=65400 << 10
        ),
        cost_estimate=pl.CostEstimate(flops=25 * 10**9, bytes_accessed=6 * 10**6, transcendentals=8 * 10**6),
    )(
        tokens, image_lengths, pad_counts.reshape(1, 1), out_grad, input_weight, output_weight, up_weight,
        down_weight, *[v.reshape(1, -1) for v in vectors],
    )
    done = pl.pallas_call(
        finish,
        out_shape=[*large, *[shape((1, v.shape[0]), F32) for v in vectors]],
        in_specs=[hbm, hbm, *[vmem] * 8],
        out_specs=[hbm, hbm, *[vmem] * 13],
        scratch_shapes=[
            *[pltpu.VMEM(x.shape, x.dtype) for x in large[:2]],
            pltpu.SemaphoreType.DMA((2,)),
            pltpu.SemaphoreType.DMA((2,)),
        ],
    )(*results)
    layer_out, input_grad, d_in, d_out, d_up, d_down = done[:6]
    v = [x.reshape(-1) for x in done[6:]]
    return (
        layer_out, input_grad, v[0], v[1], d_in, v[2], v[3], d_out, v[4], v[5], v[6], d_up, v[8], d_down,
        v[7],
    )


def solution(mesh):
    tall, flat, part = P(("rep", "fsdp"), None), P("fsdp"), P("fsdp", None)
    return jax.shard_map(
        shards,
        mesh=mesh,
        in_specs=(
            tall, tall, P(("rep", "fsdp")), tall, flat, flat, part, flat, flat, part, flat, flat, flat,
            part, flat, part, flat,
        ),
        out_specs=(
            tall, tall, flat, flat, part, flat, flat, part, flat, flat, flat, part, flat, part, flat,
        ),
        check_vma=False,
    )
```

```python
import functools

import jax
import jax.numpy as jnp
from jax import lax
from jax.experimental import pallas as pl
from jax.experimental.pallas import tpu as pltpu
from jax.sharding import PartitionSpec as P

MESH = pl.DeviceIdType.MESH
BF = jnp.bfloat16
F32 = jnp.float32
EPSILON = 1e-06
ROWS, D, FF, HEADS, HEAD = 512, 768, 3072, 12, 64
TILE = 384
SMALL = 128
LOW = -1e30
SLOPE = 0.7978845608028654


def nn(left, right):
    return jnp.dot(left, right, preferred_element_type=F32)


def nt(left, right):
    return lax.dot_general(left, right, (((1,), (1,)), ((), ())), preferred_element_type=F32)


def tn(left, right):
    return lax.dot_general(left, right, (((0,), (0,)), ((), ())), preferred_element_type=F32)


class Where:
    def __init__(self):
        self.r = lax.axis_index("rep")
        self.f = lax.axis_index("fsdp")
        self.zl, self.core = self.r // 2, self.r % 2
        self.x, self.zh, self.y = self.f // 8, (self.f // 4) % 2, self.f % 4
        self.zo = 1 - self.zh
        c = self.core
        self.a = self.y + c * (self.x - self.y)
        self.b = self.x + c * (self.y - self.x)
        self.ap, self.a2, self.am = (self.a + 1) % 4, (self.a + 2) % 4, (self.a + 3) % 4
        self.bp, self.b2, self.bm = (self.b + 1) % 4, (self.b + 2) % 4, (self.b + 3) % 4
        self.a_up, self.a_down, self.a_far = self.at(1, 0), self.at(3, 0), self.at(2, 0)
        self.b_up, self.b_down, self.b_far = self.at(0, 1), self.at(0, 3), self.at(0, 2)
        self.z = self.zh * 2 + self.zl
        self.twin = {"rep": self.r + 1 - 2 * c, "fsdp": self.f}
        self.pair = {"rep": (1 - self.zl) * 2 + c, "fsdp": self.f}
        self.cross, self.cross_up, self.cross_down, self.cross_far = [self.over(i) for i in (0, 1, 3, 2)]
        self.third = {"rep": self.r, "fsdp": (self.x * 2 + self.zo) * 4 + self.y}

    def at(self, da, db):
        c = self.core
        y = (self.y + (1 - c) * da + c * db) % 4
        x = (self.x + c * da + (1 - c) * db) % 4
        return {"rep": self.r, "fsdp": (x * 2 + self.zh) * 4 + y}

    def over(self, da):
        c = self.core
        y = (self.y + (1 - c) * da) % 4
        x = (self.x + c * da) % 4
        return {"rep": (1 - self.zl) * 2 + c, "fsdp": (x * 2 + self.zo) * 4 + y}

    def friends(self):
        near = [self.a_up, self.a_down, self.a_far, self.b_up, self.b_down, self.b_far, self.twin]
        return near + [self.pair, self.third, self.cross, self.cross_up, self.cross_down, self.cross_far]

    def greet(self):
        sem = pltpu.get_barrier_semaphore()
        for device in self.friends():
            pl.semaphore_signal(sem, inc=1, device_id=device, device_id_type=MESH)

    def meet(self):
        pl.semaphore_wait(pltpu.get_barrier_semaphore(), len(self.friends()))


class Copies:
    def remote(self, k, src, dst, device):
        return pltpu.make_async_remote_copy(
            src_ref=src,
            dst_ref=dst,
            send_sem=self.ss.at[k],
            recv_sem=self.rs.at[k],
            device_id=device,
            device_id_type=MESH,
        )

    def send(self, *which):
        for k in which:
            self.remote(k, *self.route(k)).start()

    def take(self, *which):
        for k in which:
            here = self.lands(k)
            self.remote(k, here, here, self.w.twin).wait_recv()

    def end(self):
        for k in range(self.count):
            self.remote(k, *self.route(k)).wait_send()


class Gather(Copies):
    count = 16

    def __init__(self, w, src, raw, direct, window, local, ss, rs):
        self.w, self.src, self.raw, self.direct, self.ss, self.rs = w, src, raw, direct, ss, rs
        self.half = src.shape[1] // 2
        self.first, self.width = window or (0, self.half)
        self.local = pltpu.make_async_copy(self.own(), self.slot(w.b, w.zh, w.a), local)

    def own(self):
        start = self.w.core * self.half + self.first
        return self.src.at[:, pl.ds(pl.multiple_of(start, 128), self.width)]

    def slot(self, *i):
        return self.place(self.w.core, *i)

    def place(self, *i):
        left = (slice(None),) * (5 - len(i))
        return self.raw.at[(*i, *left, pl.ds(self.first, self.width))]

    def route(self, k):
        w = self.w
        own = (w.b, w.zh, w.a)
        if k in (0, 1, 3) or (self.direct and k < 7):
            to = (w.a_up, w.a_down, w.a_far, w.cross, w.cross_up, w.cross_down, w.cross_far)[k]
            return self.own(), self.slot(*own), to
        place, device = {
            2: ((w.b, 0, w.am), w.a_up),
            4: ((w.b, w.zo, w.a), w.a_up),
            5: ((w.b, w.zo, w.a), w.a_down),
            6: ((w.b, 1, w.ap), w.a_down),
            7: ((w.b,), w.b_up),
            8: ((w.b,), w.b_down),
            9: ((w.bm, 0), w.b_up),
            10: ((w.bp, 1), w.b_down),
            11: ((w.b,), w.twin),
            12: ((w.bm,), w.twin),
            13: ((w.bp,), w.twin),
            14: ((w.b2, 0), w.twin),
            15: ((w.b2, 1), w.twin),
        }[k]
        here = self.slot(*place)
        return here, here, device

    def lands(self, k):
        w = self.w
        if not self.direct and k in (2, 6):
            return self.slot(w.b, k // 6, w.a2)
        if k < 7:
            return self.slot(w.b, w.zh if k < 3 else w.zo, (w.am, w.ap, w.a2, w.a, w.am, w.ap, w.a2)[k])
        if k >= 11:
            o = 1 - w.core
            return self.place(
                *{
                    11: (o, w.a),
                    12: (o, w.am),
                    13: (o, w.ap),
                    14: (o, w.a2, 0),
                    15: (o, w.a2, 1),
                }[k]
            )
        return self.slot(*{7: (w.bm,), 8: (w.bp,), 9: (w.b2, 0), 10: (w.b2, 1)}[k])

    def g0(self):
        self.send(*((6, 4, 5, 2, 3, 0, 1) if self.direct else (3, 0, 1)))
        self.local.start()

    def g0a(self):
        self.take(3)
        self.send(4, 5)

    def g0b(self):
        self.take(0, 1, 4, 5)
        self.send(2, 6)

    def g1(self):
        self.local.wait()
        self.take(*((0, 1, 2, 3, 4, 5, 6) if self.direct else (2, 6)))
        self.send(7, 8, 11)

    def g2(self):
        self.take(7, 8)
        self.send(9, 10, 12, 13)

    def g3(self):
        self.take(9, 10)
        self.send(14, 15)

    def g4(self):
        self.take(11, 12, 13, 14, 15)


class GatherZ(Copies):
    count = 23

    def __init__(self, w, src, raw, local, ss, rs):
        self.w, self.src, self.raw, self.ss, self.rs = w, src, raw, ss, rs
        self.half, self.part = src.shape[1] // 2, src.shape[0] // 2
        self.rows = (w.b, w.bm, w.bp, w.b2)
        self.local = pltpu.make_async_copy(self.own(), self.slot(w.core, w.b, w.zh, w.a, w.zl), local)

    def quarter(self, q):
        return pl.ds(pl.multiple_of(q * self.part, 16), self.part)

    def own(self):
        w = self.w
        return self.src.at[self.quarter(w.zl), pl.ds(pl.multiple_of(w.core * self.half, 128), self.half)]

    def slot(self, h, b, z, a, q):
        return self.raw.at[h, b, z, a, self.quarter(q), :]

    def route(self, k):
        w, c, every = self.w, self.w.core, slice(None)
        if k < 3:
            return self.own(), self.slot(c, w.b, w.zh, w.a, w.zl), (w.a_up, w.a_down, w.a_far)[k]
        if 7 <= k < 19:
            here = self.slot(c, self.rows[(k - 7) // 3], w.zh, every, w.zl)
            return here, here, (w.pair, w.cross, w.third)[(k - 7) % 3]
        place, device = {
            3: ((w.b, w.zh, every, w.zl), w.b_up),
            4: ((w.b, w.zh, every, w.zl), w.b_down),
            5: ((w.bm, w.zh, slice(0, 2), w.zl), w.b_up),
            6: ((w.bp, w.zh, slice(2, 4), w.zl), w.b_down),
            19: ((every, w.zh, every, w.zl), w.twin),
            20: ((every, w.zh, every, 1 - w.zl), w.twin),
            21: ((every, w.zo, every, 1 - w.zl), w.twin),
            22: ((every, w.zo, every, w.zl), w.twin),
        }[k]
        here = self.slot(c, *place)
        return here, here, device

    def lands(self, k):
        w, c, every = self.w, self.w.core, slice(None)
        if k < 3:
            return self.slot(c, w.b, w.zh, (w.am, w.ap, w.a2)[k], w.zl)
        if 7 <= k < 19:
            z, q = ((w.zh, 1 - w.zl), (w.zo, 1 - w.zl), (w.zo, w.zl))[(k - 7) % 3]
            return self.slot(c, self.rows[(k - 7) // 3], z, every, q)
        return self.slot(
            *{
                3: (c, w.bm, w.zh, every, w.zl),
                4: (c, w.bp, w.zh, every, w.zl),
                5: (c, w.b2, w.zh, slice(0, 2), w.zl),
                6: (c, w.b2, w.zh, slice(2, 4), w.zl),
                19: (1 - c, every, w.zh, every, w.zl),
                20: (1 - c, every, w.zh, every, 1 - w.zl),
                21: (1 - c, every, w.zo, every, 1 - w.zl),
                22: (1 - c, every, w.zo, every, w.zl),
            }[k]
        )

    def g0(self):
        self.send(2, 0, 1)
        self.local.start()

    def g1(self):
        self.local.wait()
        self.take(0, 1, 2)
        self.send(3, 4, 9, 7, 8)

    def g2(self):
        self.take(3, 4)
        self.send(5, 6, 12, 10, 11, 15, 13, 14)

    def g3(self):
        self.take(5, 6)
        self.send(18, 16, 17, 19)

    def g3z(self):
        for d in range(3):
            self.take(7 + d, 10 + d, 13 + d, 16 + d)
            self.send(20 + d)

    def g4(self):
        self.take(19, 20, 21, 22)


class Reduce(Copies):
    def __init__(self, w, part, columns, direct, bufs, ss, rs):
        self.w, self.part, self.direct, self.ss, self.rs = w, part, direct, ss, rs
        self.tw, self.fx, self.af, self.zb, self.done = bufs
        self.rows, self.columns = self.tw.shape[-2], pl.ds(columns, self.tw.shape[-1])
        self.used = [k for k in range(17) if k not in ((7, 8, 9) if direct else ())]

    def end(self):
        for k in self.used:
            self.remote(k, *self.route(k)).wait_send()

    def s(self, h, *i):
        left = (slice(None),) * (4 - 1 - len(i))
        return self.part.at[(h, *i, *left, slice(0, self.rows), self.columns)]

    def route(self, k):
        w, c = self.w, self.w.core
        every = slice(None)
        if k < 4:
            j = (w.a2, w.ap, w.am, w.a)[k]
            return self.s(1 - c, j), self.tw.at[j], w.twin
        if k == 16:
            return self.done.at[c], self.done.at[c], w.twin
        if k >= 13:
            place, device = {
                13: ((w.b, w.zo, w.a), w.third),
                14: ((w.b, w.zo, w.a), w.cross),
                15: ((w.b, w.zh, w.a), w.pair),
            }[k]
            return self.s(c, *place), self.zb.at[w.z], device
        if self.direct and k < 10:
            place, device = {4: ((w.b2,), w.b_far), 5: ((w.bp,), w.b_up), 6: ((w.bm,), w.b_down)}[k]
        else:
            place, device = {
                4: ((w.b2, 0), w.b_up),
                5: ((w.b2, 1), w.b_down),
                6: ((w.bp, 1), w.b_up),
                7: ((w.bm, 0), w.b_down),
                8: ((w.bp, 0), w.b_up),
                9: ((w.bm, 1), w.b_down),
                10: ((w.b, every, w.a2), w.a_far),
                11: ((w.b, every, w.ap), w.a_up),
                12: ((w.b, every, w.am), w.a_down),
            }[k]
        return self.s(c, *place), self.lands(k), device

    def lands(self, k):
        w = self.w
        if k < 4:
            return self.tw.at[(w.b2, w.bp, w.bm, w.b)[k]]
        if k == 16:
            return self.done.at[1 - w.core]
        if k >= 13:
            return self.zb.at[((w.z + 2) % 4, 3 - w.z, w.zh * 2 + 1 - w.zl)[k - 13]]
        if self.direct and k < 10:
            return self.fx.at[(2, 0, 1)[k - 4]]
        return {
            4: self.fx.at[2, 0],
            5: self.fx.at[2, 1],
            6: self.fx.at[0, 1],
            7: self.fx.at[1, 0],
            8: self.fx.at[0, 0],
            9: self.fx.at[1, 1],
            10: self.af.at[2],
            11: self.af.at[0],
            12: self.af.at[1],
        }[k]

    def add(self, place, *terms):
        here = self.s(self.w.core, *place)
        if len(terms) == 1:
            here[...] = here[...] + terms[0][...]
            return
        total = here[...].astype(F32)
        for term in terms:
            total = total + term[...].astype(F32)
        here[...] = total.astype(BF)

    def add8(self, b, *terms):
        def one(i, _):
            z, a = i // 4, i % 4
            self.add((b, z, a), *[t.at[z, a] for t in terms])
            return 0

        lax.fori_loop(0, 8, one, 0)

    def add4(self, b, z, term):
        def one(a, _):
            self.add((b, z, a), term.at[a])
            return 0

        lax.fori_loop(0, 4, one, 0)

    def r0(self):
        self.send(0, 1, 2, 3)

    def r1(self):
        w = self.w
        for k, b in enumerate((w.b2, w.bp, w.bm)):
            self.take(k)
            self.add8(b, self.tw.at[b])
            self.send(*((4 + k,) if self.direct else ((4, 5), (6,), (7,))[k]))

    def r2(self):
        w = self.w
        self.take(3)
        self.add8(w.b, self.tw.at[w.b])
        if not self.direct:
            self.take(4)
            self.add4(w.bp, 0, self.fx.at[2, 0])
            self.send(8)
            self.take(5)
            self.add4(w.bm, 1, self.fx.at[2, 1])
            self.send(9)

    def r3(self):
        if self.direct:
            self.take(4, 5, 6)
            self.add8(self.w.b, self.fx.at[0], self.fx.at[1], self.fx.at[2])
        else:
            self.take(6, 7, 8, 9)
            self.add8(self.w.b, self.fx.at[0], self.fx.at[1])
        self.send(10, 11, 12)

    def r4(self):
        w = self.w
        self.take(10, 11, 12)
        for z in range(2):
            self.add((w.b, z, w.a), self.af.at[0, z], self.af.at[1, z], self.af.at[2, z])
        self.send(13, 14, 15)
        self.zb[w.z] = self.s(w.core, w.b, w.zh, w.a)[...]

    def r5(self):
        self.take(13, 14, 15)
        self.done[self.w.core] = sum(self.zb[i].astype(F32) for i in range(4))
        self.send(16)

    def r6(self):
        self.take(16)


def reduce_scratch(rows, half):
    return [
        pltpu.VMEM((4, 2, 4, rows, half), BF),
        pltpu.VMEM((3, 2, 4, rows, half), BF),
        pltpu.VMEM((3, 2, rows, half), BF),
        pltpu.VMEM((4, rows, half), BF),
        pltpu.VMEM((2, rows, half), F32),
    ]


def assemble(raw, out, width, source=0, target=0):
    rows = raw.shape[4]

    def one(g, _):
        x, z = g // 2, g % 2
        place = pl.ds(pl.multiple_of(g * 4 * rows, 4 * rows), 4 * rows)
        for h in range(2):
            parts = [
                raw[0, x, z, y, :, source : source + width]
                if h == 0
                else raw[1, y, z, x, :, source : source + width]
                for y in range(4)
            ]
            to = target + h * width
            out[place, to : to + width] = jnp.concatenate(parts, axis=0)
        return 0

    lax.fori_loop(0, 8, one, 0)


def scatter_rows(left, right, part, h, first):
    n = right.shape[1]
    for k in range(2):
        value = nn(left[k * TILE : (k + 1) * TILE, :], right[...])
        for i in range(16):
            f = 16 * k + i
            x, z, y = f // 8, (f // 4) % 2, f % 4
            part[h, x + h * (y - x), z, y + h * (x - y), :, pl.ds(first, n)] = value[
                24 * i : 24 * i + 24
            ].astype(BF)


def stats(x):
    centred = x - jnp.mean(x, axis=1, keepdims=True)
    inv = lax.rsqrt(jnp.mean(centred * centred, axis=1, keepdims=True) + EPSILON)
    return centred * inv, inv


def norm_backward(grad, normed, inv, gain):
    e = grad * gain
    return inv * (
        e - jnp.mean(e, axis=1, keepdims=True) - normed * jnp.mean(e * normed, axis=1, keepdims=True)
    )


def column_sum(v):
    return jnp.sum(v, axis=0, keepdims=True)


def iota(shape, d):
    return lax.broadcasted_iota(jnp.int32, shape, d)


def by24(n):
    return lax.shift_right_logical(n * 2731, 16)


def select24():
    n = iota((SMALL, D), 1)
    return (n - 24 * by24(n) == iota((SMALL, D), 0)).astype(F32).astype(BF)


def select96():
    n = iota((SMALL, FF), 1)
    return (n - 96 * lax.shift_right_logical(by24(n), 2) == iota((SMALL, FF), 0)).astype(F32).astype(BF)


def gate(u):
    inner = u * (SLOPE + (SLOPE * 0.044715) * (u * u))
    return 0.5 + 0.5 * jnp.tanh(inner), inner


def gelu(u):
    return u * gate(u)[0]


def gelu_slope(u):
    low, inner = gate(u)
    return low + low * (1.0 - low) * (6.0 * inner - (4.0 * SLOPE) * u)


def follow(plan, step):
    for at, stages in plan.items():

        @pl.when(step == at)
        def _(stages=stages):
            for stage in stages:
                stage()


def row_blocks(count, body):
    step = ROWS // count

    def one(i, c):
        return body(pl.ds(pl.multiple_of(i * step, step), step), c)

    return one


def kernel(
    tokens_in, lengths, pads, og_in, in_weight, out_weight, up_weight, down_weight,
    v0, v1, v2, v3, v4, v5, v6, v7, v8,
    layer_out, input_grad, s_up0, s_up1, s_out, s_in0, s_in1, s_in2, s_small, s_down,
    tokens, og, in_pack, vpack, raw_in, raw_out, raw_up, raw_down, small, w_in, w_out, w_up, w_down,
    h1, joint, lse, attended, residual, h2, h2t, dh2, part, other, pre, vec, ub, gvec, dub,
    ls, gs, gr, rs, rr, *bufs,
):
    w = Where()
    w.greet()
    pack = ((0, 0, 256), (768, 256, 128), (256, 512, 512), (1024, 1024, 256))
    pack += ((896, 1280, 128), (1536, 1408, 256), (1280, 1792, 256), (1792, 2048, 512))
    moves = [(in_weight.at[:, a : a + n], in_pack.at[:, b : b + n]) for a, b, n in pack]
    moves += [(tokens_in, tokens), (og_in, og)]
    loads = [pltpu.make_async_copy(src, dst, ls.at[18 + i]) for i, (src, dst) in enumerate(moves)]
    for load in loads:
        load.start()
    ga, gb, go, gu = [
        Gather(w, s, r, i < 2, window, ls.at[(4, 28, 5, 6)[i]], gs.at[i], gr.at[i])
        for i, (s, r, window) in enumerate(
            (
                (in_pack, raw_in, (0, 512)),
                (in_pack, raw_in, (512, 768)),
                (out_weight, raw_out, None),
                (up_weight, raw_up, None),
            )
        )
    ]
    gd = GatherZ(w, down_weight, raw_down, ls.at[7], gs.at[4], gr.at[4])
    every = (ga, gb, go, gu, gd)
    places = [(raw_up, 0, False), (raw_up, 768, False), (raw_out, 0, False)]
    places += [(raw_in, 0, False), (raw_in, 384, False), (raw_in, 768, True), (small, 0, True), (raw_down, 0, False)]
    ru0, ru1, ro, rq0, rq1, rq2, rv, rd = [
        Reduce(w, part, first, direct, bufs[5 * i : 5 * i + 5], rs.at[i], rr.at[i])
        for i, (part, first, direct) in enumerate(places)
    ]
    vpack[...] = jnp.zeros_like(vpack)
    for j, v in enumerate((v0, v1, v2, v3, v4, v5, v6, v7)):
        vpack[j : j + 1, 0:24] = v[...].astype(F32)
    vpack[8:9, 0:96] = v8[...].astype(F32)
    in_pack[:, 384:512] = vpack[...].astype(BF)
    in_pack[:, 1664:1792] = jnp.zeros((24, SMALL), BF)
    gvec[...] = jnp.zeros_like(gvec)

    def codes(dim):
        pos = iota((ROWS, 1) if dim == 0 else (1, ROWS), dim)
        seg = jnp.zeros_like(pos)
        start = jnp.int32(0)
        for j in range(lengths.shape[1]):
            seg = seg + (pos >= start).astype(jnp.int32)
            start = start + lengths[0, j]
        return jnp.where(pos < ROWS - pads[0, 0], seg, -1 - pos)

    for load in loads[:8]:
        load.wait()
    w.meet()
    for g in every:
        g.g0()

    loads[8].wait()
    loads[9].wait()

    def norm_one(rows, c):
        residual[rows, :] = stats(tokens[rows, :].astype(F32))[0]
        return c

    lax.fori_loop(0, 4, row_blocks(4, norm_one), 0)
    ga.g1()
    go.g0a()
    gu.g0a()
    gb.g1()
    ga.g2()
    go.g0b()
    gu.g0b()
    gd.g1()
    ga.g3()
    gb.g2()
    go.g1()
    gu.g1()
    gd.g2()
    ga.g4()
    assemble(raw_in, w_in, TILE, 0, 0)

    packed = raw_in[0, :, :, :, 0:16, 384:512].reshape(32 * 16, SMALL)
    spread = nn(packed, select24())
    n, row = iota((ROWS, D), 1), iota((ROWS, D), 0)
    spread = jnp.where(by24(n) == lax.shift_right_logical(row, 4), spread, 0.0)
    vec[...] = jnp.sum(spread.reshape(32, 16, D), axis=0)
    packed = raw_in[0, :, :, :, 0:16, 384:512].reshape(32, 16, SMALL)[:, 8:9].reshape(32, SMALL)
    spread = nn(packed, select96())
    n, row = iota((32, FF), 1), iota((32, FF), 0)
    ub[...] = column_sum(jnp.where(lax.shift_right_logical(by24(n), 2) == row, spread, 0.0))

    h1[...] = (residual[...] * vec[0:1, :] + vec[1:2, :]).astype(BF)

    def project(first, heads, at):
        n = heads * HEAD
        for t, bias in enumerate((vec[2:3, at : at + n], 0.0, vec[3:4, at : at + n])):
            columns = slice(first + t * n, first + (t + 1) * n)
            joint[:, columns] = (nn(h1[...], w_in[:, columns]) + bias).astype(BF)

    project(0, 4, 0)

    same = codes(0)
    lane = iota((1, 128), 1)

    def scores(queries, keys, first):
        mine = (lane >= 64 * first) & (lane < 64 * first + 64)
        picked = jnp.where(mine, queries.astype(F32) * HEAD**-0.5, 0.0).astype(BF)
        return jnp.where(same == codes(1), nt(keys, picked), LOW)

    def pair_columns(p):
        late = (p + 4) // 6
        start = p * 128 + late * 512
        return [pl.ds(pl.multiple_of(start + t * (256 + 256 * late), 128), 128) for t in range(3)]

    def pair_lanes(p):
        return pl.ds(pl.multiple_of(p * 128, 128), 128)

    def attend(p, c):
        cq, ck, cv = pair_columns(p)
        queries, keys, values = joint[:, cq], joint[:, ck], joint[:, cv]
        mixed = None
        for first in range(2):
            s = scores(queries, keys, first)
            top = jnp.max(s, axis=0, keepdims=True)
            e = jnp.exp(s - top)
            total = jnp.sum(e, axis=0, keepdims=True)
            weights = (e * (1.0 / total)).astype(BF)
            lse[2 * p + first] = top + jnp.log(total)
            o = tn(weights, values)
            mixed = o if first == 0 else jnp.where(lane < 64, mixed, o)
        attended[:, pair_lanes(p)] = mixed.astype(BF)

        plan = ((gb.g3, go.g2), (gu.g2,), (gd.g3,), (go.g3, gu.g3), (), (gd.g3z,))
        follow(dict(enumerate(plan)), p)
        return c

    lax.fori_loop(0, 2, attend, 0)
    gb.g4()
    assemble(raw_in, w_in, D, 512, D)
    project(D, 8, 256)
    lax.fori_loop(2, 6, attend, 0)

    go.g4()
    assemble(raw_out, w_out, TILE)
    residual[...] = tokens[...].astype(F32) + nn(attended[...], w_out[...]) + vec[4:5, :]

    def norm_two(rows, c):
        normed, _ = stats(residual[rows, :])
        h2[rows, :] = (normed * vec[5:6, :] + vec[6:7, :]).astype(BF)
        return c

    lax.fori_loop(0, 4, row_blocks(4, norm_two), 0)
    h2t[...] = h2[...].T
    gu.g4()
    assemble(raw_up, w_up, 1536)
    def wide(t):
        return pl.ds(pl.multiple_of(t * D, D), D)

    def ahead(t, c):
        columns = wide(t)
        pre[:, columns] = (nn(h2[...], w_up[:, columns]) + ub[:, columns]).astype(BF)
        return c

    lax.fori_loop(0, 4, ahead, 0)
    gd.g4()
    assemble(raw_down, w_down, TILE)
    for g in every:
        g.end()


    def activate(to, t):
        to[...] = gelu(pre[:, wide(t)].astype(F32)).astype(BF)

    def forth(i, c):
        for now, later, t in ((part, other, 2 * i), (other, part, 2 * i + 1)):
            activate(later, (t + 1) % 4)
            grad = tn(now[...], og[...])
            for f in range(8):
                z, y, rows = f // 4, f % 4, slice(96 * f, 96 * f + 96)
                raw_down[0, t, z, y] = grad[rows, :TILE].astype(BF)
                raw_down[1, y, z, t] = grad[rows, TILE:].astype(BF)
        return c

    activate(part, 0)
    lax.fori_loop(0, 2, forth, 0)
    rd.r0()

    dh2[...] = jnp.zeros_like(dh2)

    def tile_at(i):
        return i // 2 + 2 * (i % 2)

    def front(to, t):
        columns = wide(t)
        total = jnp.zeros((1, D), F32)
        for r in range(0, ROWS, 256):
            slope = gelu_slope(pre[r : r + 256, columns].astype(F32))
            grad_pre = (nt(og[r : r + 256, :], w_down[columns, :]) * slope).astype(BF)
            to[r : r + 256, :] = grad_pre
            total = total + column_sum(grad_pre.astype(F32))
        dub[:, columns] = total

    def back(j, c):
        for now, later, i in ((part, other, 2 * j), (other, part, 2 * j + 1)):
            t = tile_at(i)
            front(later, tile_at((i + 1) % 4))
            scatter_rows(h2t, now, raw_up, t // 2, pl.multiple_of((t % 2) * D, 128))
            dh2[...] += nt(now[...], w_up[:, wide(t)])
            plan = {
                1: (ru0.r0, rd.r1),
                3: (ru0.r1, rd.r2),
            }
            follow(plan, i)
        return c

    front(part, 0)
    lax.fori_loop(0, 2, back, 0)
    ru1.r0()

    def back_two(rows, c):
        normed, inv = stats(residual[rows, :])
        grad = dh2[rows, :]
        up = og[rows, :].astype(F32)
        total = up + norm_backward(grad, normed, inv, vec[5:6, :])
        rounded = total.astype(BF)
        w_up[rows, 0:D] = rounded
        return (
            c[0] + column_sum(rounded.astype(F32)),
            c[1] + column_sum(grad * normed),
            c[2] + column_sum(grad),
            c[3] + column_sum(up),
        )

    zero = jnp.zeros((1, D), F32)
    sums = lax.fori_loop(0, 4, row_blocks(4, back_two), (zero, zero, zero, zero))
    for j, v in zip((4, 5, 6, 7), sums):
        gvec[j : j + 1, :] = v
    grad_branch = w_up.at[0:ROWS, 0:D]
    grad_attended = w_up.at[0:ROWS, D : 2 * D]
    attended_t = h2t
    attended_t[...] = attended[...].T
    for u in range(2):
        columns = slice(u * TILE, (u + 1) * TILE)
        scatter_rows(attended_t, grad_branch.at[:, columns], raw_out, u, 0)
    grad_attended[...] = nt(grad_branch[...], w_out[...]).astype(BF)
    ro.r0()
    ru1.r1()
    h1t = h2t
    h1t[...] = h1[...].T

    def weight_gradient(p, both):
        scatter_rows(h1t, both.at[:, 0:TILE], raw_in, p % 2, pl.multiple_of((p // 2) * TILE, 128))

    def pair_back(p, both):
        cq, ck, cv = pair_columns(p)
        queries, keys, values = joint[:, cq], joint[:, ck], joint[:, cv]
        lanes = pair_lanes(p)
        gradient = grad_attended[:, lanes]
        dq = dk = dv = None
        for first in range(2):
            mine = (lane >= 64 * first) & (lane < 64 * first + 64)
            weights = jnp.exp(scores(queries, keys, first) - lse[2 * p + first])
            picked = jnp.where(mine, gradient, jnp.zeros_like(gradient))
            grad_weights = nt(values, picked)
            along = jnp.sum(grad_weights * weights, axis=0, keepdims=True)
            grad_scores = (weights * (grad_weights - along)).astype(BF)
            v = nn(weights.astype(BF), gradient)
            k = nn(grad_scores, queries) * HEAD**-0.5
            q = tn(grad_scores, keys) * HEAD**-0.5
            if first == 0:
                dq, dk, dv = q, k, v
            else:
                dq, dk, dv = [jnp.where(lane < 64, l, r) for l, r in ((dq, q), (dk, k), (dv, v))]
        dq, dk, dv = dq.astype(BF), dk.astype(BF), dv.astype(BF)
        joint[:, cq], joint[:, ck], joint[:, cv] = dq, dk, dv
        gvec[2:3, lanes] = column_sum(dq.astype(F32))
        gvec[3:4, lanes] = column_sum(dv.astype(F32))
        both[:, 0:128], both[:, 128:256], both[:, 256:384] = dq, dk, dv

    def attend_back(j, c):
        for now, before, p in ((part, other, 2 * j), (other, part, 2 * j + 1)):
            pair_back(p, now)
            weight_gradient((p + 5) % 6, before)
            plan = (
                (rd.r3, ru0.r2, ro.r1),
                (),
                (rq0.r0, rd.r4, ru1.r2),
                (rq0.r1, ru0.r3, ro.r2, rd.r5),
                (rq1.r0, ru0.r4, ru1.r3),
                (rq1.r1, rq0.r2, ro.r3, ru0.r5),
            )
            follow(dict(enumerate(plan)), p)
        return c

    lax.fori_loop(0, 3, attend_back, 0)
    weight_gradient(5, other)
    rq2.r0()
    ru1.r4()

    rq2.r1()
    dh2[...] = nt(joint[...], w_in[...])

    def sums_one(rows, c):
        normed, _ = stats(tokens[rows, :].astype(F32))
        grad = dh2[rows, :]
        return c[0] + column_sum(grad * normed), c[1] + column_sum(grad)

    sums = lax.fori_loop(0, 4, row_blocks(4, sums_one), (zero, zero))
    for j, v in zip((0, 1), sums):
        gvec[j : j + 1, :] = v

    n, row = iota((32, 16, D), 2), iota((32, 16, D), 0)
    spread = jnp.where(by24(n) == row, jnp.broadcast_to(gvec[...][None], (32, 16, D)), 0.0)
    own = nt(spread.reshape(512, D).astype(BF), select24()).astype(BF).reshape(32, 16, SMALL)
    n, row = iota((32, FF), 1), iota((32, FF), 0)
    spread = jnp.where(lax.shift_right_logical(by24(n), 2) == row, jnp.broadcast_to(dub[...], (32, FF)), 0.0)
    hidden = nt(spread.astype(BF), select96())
    for f in range(32):
        x, z, y = f // 8, (f // 4) % 2, f % 4
        small[0, x, z, y] = own[f]
        small[1, y, z, x] = jnp.broadcast_to(hidden[f : f + 1], (16, SMALL)).astype(BF)
    rv.r0()
    rq2.r2()
    rq1.r2()
    rq0.r3()
    rv.r1()
    rv.r2()

    def back_one(rows, c):
        normed, inv = stats(tokens[rows, :].astype(F32))
        dh2[rows, :] = grad_branch[rows, :].astype(F32) + norm_backward(dh2[rows, :], normed, inv, vec[0:1, :])
        return c

    lax.fori_loop(0, 4, row_blocks(4, back_one), 0)
    grad_copy = pltpu.make_async_copy(dh2, input_grad, ls.at[9])
    grad_copy.start()
    ro.r4()
    rq2.r3()
    rq1.r3()
    rv.r3()
    ru1.r5()
    rq0.r4()
    for t in range(4):
        activate(pre.at[:, t * D : (t + 1) * D], t)
    rq2.r4()
    rv.r4()
    rq1.r4()
    rq0.r5()
    ro.r5()

    def result(t, c):
        columns = pl.ds(pl.multiple_of(t * 256, 256), 256)
        h2[:, columns] = (residual[:, columns] + vec[7:8, columns] + nn(pre[...], w_down[:, columns])).astype(BF)
        follow({1: (rq2.r5, rq1.r5, rv.r5)}, t)
        return c

    lax.fori_loop(0, 3, result, 0)
    out_copy = pltpu.make_async_copy(h2, layer_out, ls.at[8])
    out_copy.start()
    sums = (ru0, ru1, ro, rq0, rq1, rq2, rv, rd)
    hand = [
        pltpu.make_async_copy(r.done, to, ls.at[10 + i])
        for i, (r, to) in enumerate(
            zip(sums, (s_up0, s_up1, s_out, s_in0, s_in1, s_in2, s_small, s_down))
        )
    ]
    for r, c in zip(sums, hand):
        r.r6()
        c.start()

    for r in sums:
        r.end()
    out_copy.wait()
    grad_copy.wait()
    for c in hand:
        c.wait()


def finish(
    layer_in, grad_in, up0, up1, out, in0, in1, in2, small, down,
    layer_out, grad_out, d_in, d_out, d_up, d_down, v0, v1, v2, v3, v4, v5, v6, v7, v8,
    held_layer, held_grad, taken, given,
):
    pairs = ((layer_in, held_layer, layer_out), (grad_in, held_grad, grad_out))
    arrive = [pltpu.make_async_copy(s, h, taken.at[i]) for i, (s, h, d) in enumerate(pairs)]
    leave = [pltpu.make_async_copy(h, d, given.at[i]) for i, (s, h, d) in enumerate(pairs)]
    for c in arrive:
        c.start()
    for h in range(2):
        d_up[:, h * 1536 : h * 1536 + 768] = up0[h]
        d_up[:, h * 1536 + 768 : h * 1536 + 1536] = up1[h]
        d_down[:, h * TILE : (h + 1) * TILE] = down[h]
        d_out[:, h * TILE : (h + 1) * TILE] = out[h]
        for k, part in enumerate((in0, in1, in2)):
            for j in range(3):
                to = j * D + (2 * k + h) * 128
                d_in[:, to : to + 128] = part[h, :, 128 * j : 128 * j + 128]
    for j, v in enumerate((v0, v1, v2, v3, v4, v5, v6, v7)):
        v[...] = small[0, j : j + 1, 0:24]
    v8[...] = small[1, 0:1, 0:96]
    for c, d in zip(arrive, leave):
        c.wait()
        d.start()
    for c in leave:
        c.wait()


def shards(
    tokens, image_lengths, pad_counts, out_grad, first_gain, first_shift, input_weight, query_bias,
    value_bias, output_weight, output_bias, second_gain, second_shift, up_weight, up_bias, down_weight,
    down_bias,
):
    vmem = pl.BlockSpec(memory_space=pltpu.VMEM)
    smem = pl.BlockSpec(memory_space=pltpu.SMEM)
    hbm = pl.BlockSpec(memory_space=pl.ANY)
    scratch = [
        pltpu.VMEM((ROWS, D), BF),
        pltpu.VMEM((ROWS, D), BF),
        pltpu.VMEM((24, 2560), BF),
        pltpu.VMEM((24, SMALL), F32),
        pltpu.VMEM((2, 4, 2, 4, 24, 1280), BF),
        pltpu.VMEM((2, 4, 2, 4, 24, 384), BF),
        pltpu.VMEM((2, 4, 2, 4, 24, 1536), BF),
        pltpu.VMEM((2, 4, 2, 4, 96, 384), BF),
        pltpu.VMEM((2, 4, 2, 4, 16, SMALL), BF),
        pltpu.VMEM((D, 3 * D), BF),
        pltpu.VMEM((D, D), BF),
        pltpu.VMEM((D, FF), BF),
        pltpu.VMEM((FF, D), BF),
        pltpu.VMEM((ROWS, D), BF),
        pltpu.VMEM((ROWS, 3 * D), BF),
        pltpu.VMEM((HEADS, 1, ROWS), F32),
        pltpu.VMEM((ROWS, D), BF),
        pltpu.VMEM((ROWS, D), F32),
        pltpu.VMEM((ROWS, D), BF),
        pltpu.VMEM((D, ROWS), BF),
        pltpu.VMEM((ROWS, D), F32),
        pltpu.VMEM((ROWS, D), BF),
        pltpu.VMEM((ROWS, D), BF),
        pltpu.VMEM((ROWS, FF), BF),
        pltpu.VMEM((16, D), F32),
        pltpu.VMEM((1, FF), F32),
        pltpu.VMEM((16, D), F32),
        pltpu.VMEM((1, FF), F32),
        pltpu.SemaphoreType.DMA((29,)),
        pltpu.SemaphoreType.DMA((5, 23)),
        pltpu.SemaphoreType.DMA((5, 23)),
        pltpu.SemaphoreType.DMA((8, 17)),
        pltpu.SemaphoreType.DMA((8, 17)),
    ]
    for rows, half in ((24, 768), (24, 768), (24, 384), (24, 384), (24, 384), (24, 384), (16, SMALL), (96, 384)):
        scratch += reduce_scratch(rows, half)
    shape = jax.ShapeDtypeStruct
    large = [
        shape((ROWS, D), BF),
        shape((ROWS, D), F32),
        shape((24, 3 * D), F32),
        shape((24, D), F32),
        shape((24, FF), F32),
        shape((96, D), F32),
    ]
    vectors = (
        first_gain, first_shift, query_bias, value_bias, output_bias, second_gain, second_shift, down_bias,
        up_bias,
    )
    halves = [shape((2, 24, 768), F32)] * 2 + [shape((2, 24, 384), F32)] * 4
    halves += [shape((2, 16, SMALL), F32), shape((2, 96, 384), F32)]
    results = pl.pallas_call(
        kernel,
        out_shape=[*large[:2], *halves],
        in_specs=[hbm, smem, smem, hbm, hbm, hbm, hbm, hbm, *[vmem] * 9],
        out_specs=[hbm] * 10,
        scratch_shapes=scratch,
        compiler_params=pltpu.CompilerParams(
            collective_id=0, has_side_effects=True, vmem_limit_bytes=65400 << 10
        ),
        cost_estimate=pl.CostEstimate(flops=25 * 10**9, bytes_accessed=6 * 10**6, transcendentals=8 * 10**6),
    )(
        tokens, image_lengths, pad_counts.reshape(1, 1), out_grad, input_weight, output_weight, up_weight,
        down_weight, *[v.reshape(1, -1) for v in vectors],
    )
    done = pl.pallas_call(
        finish,
        out_shape=[*large, *[shape((1, v.shape[0]), F32) for v in vectors]],
        in_specs=[hbm, hbm, *[vmem] * 8],
        out_specs=[hbm, hbm, *[vmem] * 13],
        scratch_shapes=[
            *[pltpu.VMEM(x.shape, x.dtype) for x in large[:2]],
            pltpu.SemaphoreType.DMA((2,)),
            pltpu.SemaphoreType.DMA((2,)),
        ],
    )(*results)
    layer_out, input_grad, d_in, d_out, d_up, d_down = done[:6]
    v = [x.reshape(-1) for x in done[6:]]
    return (
        layer_out, input_grad, v[0], v[1], d_in, v[2], v[3], d_out, v[4], v[5], v[6], d_up, v[8], d_down,
        v[7],
    )


def solution(mesh):
    tall, flat, part = P(("rep", "fsdp"), None), P("fsdp"), P("fsdp", None)
    return jax.shard_map(
        shards,
        mesh=mesh,
        in_specs=(
            tall, tall, P(("rep", "fsdp")), tall, flat, flat, part, flat, flat, part, flat, flat, flat,
            part, flat, part, flat,
        ),
        out_specs=(
            tall, tall, flat, flat, part, flat, flat, part, flat, flat, flat, part, flat, part, flat,
        ),
        check_vma=False,
    )
```
